32 devices in a mesh: gx: 8 (over z, x), gz: 4 (over y, core).
Axes of the slice: x: 2, y: 2, z: 4, core: 2. Of those that a mesh axis runs over, the one named last changes fastest.
Arguments:
- state: float32 [5, 32, 32, 2048], P(None, 'gx', None, 'gz'), as said below
- mask_x: int32 [32, 32, 2048], P('gx', None, 'gz'), may hold values from 0 to 1, as said below
- mask_y: int32 [32, 32, 2048], P('gx', None, 'gz'), may hold values from 0 to 1, as said below
- span_filter: float32 [1024], replicated, may hold values from 0.25 to 1
Outputs:
- updated: float32 [5, 32, 32, 2048], P(None, 'gx', None, 'gz')
The draws below stay inside these ranges and needn't reach their ends.
Inputs may be any that keep to these rules, and one draw needn't show every extreme that they name: `state`: density and pressure of every cell lie between 0.5 and 2; the streamwise velocity lies between 0.8 and 3.2, the others between -1.2 and 1.2. `mask_x`: 1 selects the upwind value at that face, 0 the central one. `mask_y`: 1 selects the upwind value at that face, 0 the central one.
All inputs are finite; a program needn't handle non-finite values.
Results may differ from the reference program's by a relative error of at most 0.0003.
Values sent between devices are 32-bit elements; how exact they have to be, the bound alone decides.
No kernel may reach another device: no remote copies, remote signals or barrier semaphores. Data moves between devices by JAX's collectives and lax.ppermute only.
A program may use at most 64 MiB of HBM per device.

```python
import math
from functools import reduce
import jax
import jax.numpy as jnp
from jax import lax

NY = 32
NZ = 2048
NX = 32


def shock_centre(key):
    return jax.random.randint(jax.random.fold_in(key, 5), (), 0, NX)


def switch_draw(key, centre):
    rolls = jax.random.randint(key, (NX, NY, NZ), 0, 20)
    place = jnp.arange(NX, dtype=jnp.int32)
    near = jnp.abs(place - centre) < max(NX // 8, 4)
    limit = jnp.where(near, 12, 0)
    return (rolls < limit[:, None, None]).astype(jnp.int32)


def draw_state(key, part):
    key = jax.random.fold_in(key, 11)
    keys = jax.random.split(key, 5)
    shape = (NX, NY, NZ)
    density = jnp.exp(jax.random.uniform(keys[0], shape, jnp.float32, jnp.log(0.5), jnp.log(2.0)))
    along = 2.0 + 0.4 * jax.random.truncated_normal(keys[1], -3.0, 3.0, shape, jnp.float32)
    normal_speed = 0.3 * jax.random.truncated_normal(keys[2], -3.0, 3.0, shape, jnp.float32)
    span_speed = 0.4 * jax.random.truncated_normal(keys[3], -3.0, 3.0, shape, jnp.float32)
    pressure = jnp.exp(jax.random.uniform(keys[4], shape, jnp.float32, jnp.log(0.5), jnp.log(2.0)))
    energy = pressure / 0.4 + 0.5 * density * (along * along + normal_speed * normal_speed + span_speed * span_speed)
    return jnp.stack([density, density * along, density * normal_speed, density * span_speed, energy])


def draw_mask_x(key, part):
    centre = shock_centre(key)
    key = jax.random.fold_in(key, 21)
    return switch_draw(key, centre)


def draw_mask_y(key, part):
    centre = shock_centre(key)
    key = jax.random.fold_in(key, 22)
    return switch_draw(key, centre)


def setup_inputs(seed: int = 0) -> dict:
    key_of = jax.random.split(jax.random.key(seed), 5)
    state = draw_state(jax.random.fold_in(key_of[4], 71), 0)
    mask_x = draw_mask_x(jax.random.fold_in(key_of[4], 71), 0)
    mask_y = draw_mask_y(jax.random.fold_in(key_of[4], 71), 0)
    span_filter = jnp.clip(jnp.exp(jax.random.uniform(key_of[3], (NZ // 2,), jnp.float32, math.log(0.25), math.log(1.0))), 0.25, 1.0)
    return dict(state=state, mask_x=mask_x, mask_y=mask_y, span_filter=span_filter)


GAMMA_GAS = 1.4
SMALL_EPS = 1e-06
TIME_STEP = 0.1

def directional(state, normal):
    density = state[0]
    velocity = [state[1] / density, state[2] / density, state[3] / density]
    pressure = (GAMMA_GAS - 1.0) * (state[4] - 0.5 * (state[1] * velocity[0] + state[2] * velocity[1] + state[3] * velocity[2]))
    along = velocity[normal]
    momentum_flux = [state[1] * along, state[2] * along, state[3] * along]
    momentum_flux[normal] = momentum_flux[normal] + pressure
    flux = jnp.stack([state[normal + 1]] + momentum_flux + [(state[4] + pressure) * along])
    speed = jnp.abs(along) + jnp.sqrt(GAMMA_GAS * pressure / density)
    return (flux, speed)

def upwind_edge(far_left, left, centre, right, far_right):
    guess_zero = (2.0 * far_left - 7.0 * left + 11.0 * centre) / 6.0
    guess_one = (-left + 5.0 * centre + 2.0 * right) / 6.0
    guess_two = (2.0 * centre + 5.0 * right - far_right) / 6.0
    rough_zero = 13.0 / 12.0 * (far_left - 2.0 * left + centre) ** 2 + 0.25 * (far_left - 4.0 * left + 3.0 * centre) ** 2
    rough_one = 13.0 / 12.0 * (left - 2.0 * centre + right) ** 2 + 0.25 * (left - right) ** 2
    rough_two = 13.0 / 12.0 * (centre - 2.0 * right + far_right) ** 2 + 0.25 * (3.0 * centre - 4.0 * right + far_right) ** 2
    weight_zero = 0.1 / (SMALL_EPS + rough_zero) ** 2
    weight_one = 0.6 / (SMALL_EPS + rough_one) ** 2
    weight_two = 0.3 / (SMALL_EPS + rough_two) ** 2
    return (weight_zero * guess_zero + weight_one * guess_one + weight_two * guess_two) / (weight_zero + weight_one + weight_two)

def face_flux(cells, normal, axis, count, switch):
    flux, speed = directional(cells, normal)
    fluxes_at = [lax.slice_in_dim(flux, k, k + count, axis=axis) for k in range(6)]
    states_at = [lax.slice_in_dim(cells, k, k + count, axis=axis) for k in range(6)]
    speeds_at = [lax.slice_in_dim(speed, k, k + count, axis=axis - 1) for k in range(6)]
    alpha = reduce(jnp.maximum, speeds_at)[None]
    central = (37.0 * (fluxes_at[2] + fluxes_at[3]) - 8.0 * (fluxes_at[1] + fluxes_at[4]) + (fluxes_at[0] + fluxes_at[5])) / 60.0
    plus_part = [0.5 * (fluxes_at[k] + alpha * states_at[k]) for k in range(6)]
    minus_part = [0.5 * (fluxes_at[k] - alpha * states_at[k]) for k in range(6)]
    upwind = upwind_edge(plus_part[0], plus_part[1], plus_part[2], plus_part[3], plus_part[4])
    upwind = upwind + upwind_edge(minus_part[5], minus_part[4], minus_part[3], minus_part[2], minus_part[1])
    return jnp.where(switch[None] > 0, upwind, central)

def reference(state, mask_x, mask_y, span_filter):
    span = state.shape[3]
    width = 128
    blocks = span // width

    def xy_block(number):
        start = number * width
        cells = lax.dynamic_slice_in_dim(state, start, width, 3)
        marks_x = lax.dynamic_slice_in_dim(mask_x, start, width, 2)
        marks_y = lax.dynamic_slice_in_dim(mask_y, start, width, 2)
        padded_x = jnp.pad(cells, ((0, 0), (3, 3), (0, 0), (0, 0)), mode='edge')
        faces_x = jnp.concatenate([marks_x, jnp.zeros((1,) + marks_x.shape[1:], marks_x.dtype)], 0)
        hat_x = face_flux(padded_x, 0, 1, NX + 1, faces_x)
        padded_y = jnp.pad(cells, ((0, 0), (0, 0), (3, 3), (0, 0)), mode='edge')
        faces_y = jnp.concatenate([marks_y, jnp.zeros((marks_y.shape[0], 1, marks_y.shape[2]), marks_y.dtype)], 1)
        hat_y = face_flux(padded_y, 1, 2, NY + 1, faces_y)
        return hat_x[:, 1:] - hat_x[:, :-1] + (hat_y[:, :, 1:] - hat_y[:, :, :-1])
    pieces = lax.map(xy_block, jnp.arange(blocks, dtype=jnp.int32))
    divergence = jnp.moveaxis(pieces, 0, 3).reshape(state.shape)
    modes = jnp.arange(span // 2 + 1, dtype=jnp.int32)
    response = jnp.concatenate([span_filter, jnp.zeros((1,), span_filter.dtype)], 0)
    wave = 2.0 * jnp.pi / span * modes.astype(span_filter.dtype) * response

    def z_plane(index):
        cells = lax.dynamic_index_in_dim(state, index, 1, keepdims=False)
        flux, speed = directional(cells, 2)
        spectrum = jnp.fft.rfft(flux, axis=-1)
        return jnp.fft.irfft(spectrum * (1j * wave), n=span, axis=-1)
    planes = lax.map(z_plane, jnp.arange(state.shape[1], dtype=jnp.int32))
    spanwise = jnp.moveaxis(planes, 0, 1).astype(state.dtype)
    return state - TIME_STEP * (divergence + spanwise)
```

```python
import functools

import jax
import jax.numpy as jnp
import numpy as np
from jax import lax
from jax.experimental import pallas as pl
from jax.experimental.pallas import tpu as pltpu
from jax.sharding import PartitionSpec as P

GAMMA_GAS = 1.4
SMALL_EPS = 1e-06
TIME_STEP = 0.1
ROWS = 8
LANES = 128
CHUNKS = 4
VMEM_BYTES = 40 * 1024 * 1024
FACE_SCALE = -TIME_STEP / 60.0


def params():
    return pltpu.CompilerParams(vmem_limit_bytes=VMEM_BYTES)


def cost(flops, nbytes):
    return pl.CostEstimate(flops=int(flops), bytes_accessed=int(nbytes), transcendentals=0)


def inverse(value):
    first = pl.reciprocal(value, approx=True)
    return first * (2.0 - value * first)


def flux_of(q, normal):
    thin = inverse(q[0])
    velocity = [q[1] * thin, q[2] * thin, q[3] * thin]
    pressure = (GAMMA_GAS - 1.0) * (
        q[4] - 0.5 * (q[1] * velocity[0] + q[2] * velocity[1] + q[3] * velocity[2])
    )
    along = velocity[normal]
    flux = [q[normal + 1], q[1] * along, q[2] * along, q[3] * along, (q[4] + pressure) * along]
    flux[normal + 1] = flux[normal + 1] + pressure
    return flux, pressure, thin, along


def speed_of(pressure, thin, along):
    return jnp.abs(along) + jnp.sqrt(GAMMA_GAS * pressure * thin)


def weno_rest(d1, d2, d3, d4):
    low = d2 * d2 * 0.609375 + 3.0 * SMALL_EPS
    high = d3 * d3 * 0.609375 + 3.0 * SMALL_EPS
    x0 = d1 - 1.375 * d2
    x1 = d2 - 0.625 * d3
    x2 = d4 - 1.375 * d3
    t0 = low + x0 * x0
    t1 = high + x1 * x1
    t2 = high + x2 * x2
    w0 = t1 * t2
    w1 = t0 * t2
    w2 = t0 * t1
    w0 = w0 * w0
    w1 = w1 * w1
    w2 = w2 * w2 * 1.5
    s1 = d2 - d1
    s2 = d3 - d2
    s3 = d4 - d3
    top = w0 * (s2 - s1) + w2 * (s3 - s2)
    bottom = 0.5 * w0 + 3.0 * w1 + w2
    return top * inverse(bottom)


def face_value(dq, df, both, alpha, upwind):
    aq = [alpha * value for value in dq]
    plus = [df[k] + aq[k] for k in range(4)]
    minus = [df[k] - aq[k] for k in range(1, 5)]
    bend = df[1] - df[3]
    central = 7.0 * bend + (df[4] - df[0])
    rest = weno_rest(minus[3], minus[2], minus[1], minus[0]) - weno_rest(*plus)
    biased = 5.0 * (bend + (aq[1] + aq[3]) - (aq[2] + aq[2]) + rest)
    return 30.0 * both + jnp.where(upwind, biased, central)


def wall_kernel(state_ref, mask_ref, out_ref, q_s, f_s, speed_s, dq_s, df_s, hat_s):
    rows_y = state_ref.shape[2]
    tiles = rows_y // ROWS
    end = ROWS + rows_y
    zero = jnp.zeros((5, ROWS, LANES), jnp.float32)
    for side in (dq_s, df_s):
        side[:, 0:ROWS, :] = zero
        side[:, end : end + ROWS, :] = zero

    def column(number, carry):
        lane = pl.ds(pl.multiple_of(number * LANES, LANES), LANES)

        def point(r, c):
            at = pl.ds(pl.multiple_of(r * ROWS, ROWS), ROWS)
            to = pl.ds(pl.multiple_of(r * ROWS + ROWS, ROWS), ROWS)
            q = [state_ref[k, 0, at, lane] for k in range(5)]
            flux, pressure, thin, along = flux_of(q, 1)
            for k in range(5):
                q_s[k, to, :] = q[k]
                f_s[k, to, :] = flux[k]
            speed_s[to, :] = speed_of(pressure, thin, along)
            return c

        lax.fori_loop(0, tiles, point, 0)
        for k in range(5):
            for ref in (q_s, f_s):
                ref[k, 0:ROWS, :] = jnp.broadcast_to(ref[k, ROWS : ROWS + 1, :], (ROWS, LANES))
        speed_s[0:ROWS, :] = jnp.broadcast_to(speed_s[ROWS : ROWS + 1, :], (ROWS, LANES))
        speed_s[end : end + ROWS, :] = jnp.broadcast_to(
            speed_s[end - 1 : end, :], (ROWS, LANES)
        )

        def differences(r, c):
            to = pl.ds(pl.multiple_of(r * ROWS + ROWS, ROWS), ROWS)
            before = pl.ds(r * ROWS + ROWS - 1, ROWS)
            for k in range(5):
                dq_s[k, to, :] = q_s[k, to, :] - q_s[k, before, :]
                df_s[k, to, :] = f_s[k, to, :] - f_s[k, before, :]
            return c

        lax.fori_loop(0, tiles, differences, 0)

        def faces(r, c):
            at = pl.ds(pl.multiple_of(r * ROWS, ROWS), ROWS)
            to = pl.ds(pl.multiple_of(r * ROWS + ROWS, ROWS), ROWS)
            shifted = [pl.ds(r * ROWS + ROWS + s, ROWS) for s in (-2, -1, 0, 1, 2)]
            alpha = speed_s[pl.ds(r * ROWS + ROWS - 3, ROWS), :]
            for place in shifted:
                alpha = jnp.maximum(alpha, speed_s[place, :])
            upwind = mask_ref[0, at, lane] > 0
            for k in range(5):
                dq = [dq_s[k, place, :] for place in shifted]
                df = [df_s[k, place, :] for place in shifted]
                both = f_s[k, to, :] + f_s[k, shifted[1], :]
                hat_s[k, to, :] = face_value(dq, df, both, alpha, upwind)
            return c

        lax.fori_loop(0, tiles, faces, 0)
        for k in range(5):
            top = (
                60.0 * f_s[k, end - 1 : end, :]
                + 7.0 * df_s[k, end - 1 : end, :]
                - df_s[k, end - 2 : end - 1, :]
            )
            hat_s[k, end : end + ROWS, :] = jnp.broadcast_to(top, (ROWS, LANES))

        def gather(r, c):
            at = pl.ds(pl.multiple_of(r * ROWS, ROWS), ROWS)
            to = pl.ds(pl.multiple_of(r * ROWS + ROWS, ROWS), ROWS)
            after = pl.ds(r * ROWS + ROWS + 1, ROWS)
            for k in range(5):
                out_ref[k, 0, at, lane] = q_s[k, to, :] + FACE_SCALE * (
                    hat_s[k, after, :] - hat_s[k, to, :]
                )
            return c

        lax.fori_loop(0, tiles, gather, 0)
        return carry

    lax.fori_loop(0, state_ref.shape[3] // LANES, column, 0)


def wall_part(state, mask_y):
    fields, depth, rows_y, width = state.shape
    tall = rows_y + 2 * ROWS
    return pl.pallas_call(
        wall_kernel,
        grid=(depth,),
        out_shape=jax.ShapeDtypeStruct(state.shape, jnp.float32),
        in_specs=[
            pl.BlockSpec((fields, 1, rows_y, width), lambda i: (0, i, 0, 0)),
            pl.BlockSpec((1, rows_y, width), lambda i: (i, 0, 0)),
        ],
        out_specs=pl.BlockSpec((fields, 1, rows_y, width), lambda i: (0, i, 0, 0)),
        scratch_shapes=[
            pltpu.VMEM((fields, tall, LANES), jnp.float32),
            pltpu.VMEM((fields, tall, LANES), jnp.float32),
            pltpu.VMEM((tall, LANES), jnp.float32),
            pltpu.VMEM((fields, tall, LANES), jnp.float32),
            pltpu.VMEM((fields, tall, LANES), jnp.float32),
            pltpu.VMEM((fields, tall, LANES), jnp.float32),
        ],
        compiler_params=params(),
        cost_estimate=cost(120 * state.size, 9 * state.size),
        name="wall_faces",
    )(state, mask_y)


def stream_kernel(flags_ref, state_ref, pair_ref, far_ref, mask_ref, next_ref, acc_ref, out_ref):
    fields, depth, rows_y, width = state_ref.shape
    even = flags_ref[0] > 0
    first = flags_ref[1] > 0
    last = flags_ref[2] > 0
    lane_tiles = width // LANES

    def tile(number, carry):
        row = pl.ds(pl.multiple_of((number // lane_tiles) * ROWS, ROWS), ROWS)
        lane = pl.ds(pl.multiple_of((number % lane_tiles) * LANES, LANES), LANES)
        own = [[state_ref[k, i, row, lane] for k in range(5)] for i in range(depth)]
        cells = []
        for i in range(3):
            cells.append(
                [
                    jnp.where(
                        first,
                        own[0][k],
                        jnp.where(
                            even,
                            far_ref[k, i, row, lane],
                            pair_ref[k, depth - 3 + i, row, lane],
                        ),
                    )
                    for k in range(5)
                ]
            )
        cells += own
        for i in range(3):
            cells.append(
                [
                    jnp.where(
                        last,
                        own[depth - 1][k],
                        jnp.where(even, pair_ref[k, i, row, lane], far_ref[k, i, row, lane]),
                    )
                    for k in range(5)
                ]
            )
        fluxes, speeds = [], []
        for q in cells:
            flux, pressure, thin, along = flux_of(q, 0)
            fluxes.append(flux)
            speeds.append(speed_of(pressure, thin, along))
        pairs = [jnp.maximum(speeds[i], speeds[i + 1]) for i in range(depth + 5)]
        alphas = [
            jnp.maximum(jnp.maximum(pairs[f], pairs[f + 2]), pairs[f + 4])
            for f in range(depth + 1)
        ]
        switches = [mask_ref[i, row, lane] > 0 for i in range(depth)] + [next_ref[row, lane] > 0]
        for k in range(5):
            dq = [cells[i + 1][k] - cells[i][k] for i in range(depth + 5)]
            df = [fluxes[i + 1][k] - fluxes[i][k] for i in range(depth + 5)]
            before = None
            for f in range(depth + 1):
                hat = face_value(
                    dq[f : f + 5],
                    df[f : f + 5],
                    fluxes[f + 2][k] + fluxes[f + 3][k],
                    alphas[f],
                    switches[f],
                )
                if f > 0:
                    out_ref[k, f - 1, row, lane] = acc_ref[k, f - 1, row, lane] + FACE_SCALE * (
                        hat - before
                    )
                before = hat
        return carry

    lax.fori_loop(0, (rows_y // ROWS) * lane_tiles, tile, 0)


def stream_part(flags, state, pair, far, mask_x, mask_next, acc, chunk, chunks):
    fields, depth, rows_all, width = state.shape
    rows_y = rows_all // chunks
    block = pl.BlockSpec((fields, depth, rows_y, width), lambda i, s: (0, 0, chunk, 0))
    whole = pl.BlockSpec((fields, depth, rows_y, width), lambda i, s: (0, 0, 0, 0))
    return pl.pallas_call(
        stream_kernel,
        grid_spec=pltpu.PrefetchScalarGridSpec(
            num_scalar_prefetch=1,
            grid=(1,),
            in_specs=[
                block,
                whole,
                pl.BlockSpec((fields, 3, rows_y, width), lambda i, s: (0, 0, 0, 0)),
                pl.BlockSpec((depth, rows_y, width), lambda i, s: (0, chunk, 0)),
                pl.BlockSpec((rows_y, width), lambda i, s: (chunk, 0)),
                block,
            ],
            out_specs=block,
        ),
        out_shape=jax.ShapeDtypeStruct(acc.shape, jnp.float32),
        input_output_aliases={6: 0},
        compiler_params=params(),
        cost_estimate=cost(150 * state.size // chunks, 16 * state.size // chunks),
        name="stream_faces",
    )(flags, state, pair, far, mask_x, mask_next, acc)


def circulant_tables(span):
    half = span // 2
    step = 1
    while step * step < half:
        step *= 2
    count = half // step
    places = np.arange(span)
    high = 2.0 * np.pi / span * ((np.arange(count)[:, None] * step * places[None]) % span)
    low = 2.0 * np.pi / span * ((np.arange(step)[:, None] * places[None]) % span)
    tables = [np.cos(high), np.sin(high), np.cos(low), np.sin(low)]
    return step, count, [jnp.asarray(t.astype(np.float32)) for t in tables]


def circulant_kernel(scale_ref, ch_ref, sh_ref, cl_ref, sl_ref, high_ref, low_ref, band):
    span = ch_ref.shape[1]
    tall, wide = high_ref.shape
    dot = functools.partial(
        jnp.dot, precision=lax.Precision.HIGHEST, preferred_element_type=jnp.float32
    )
    inner_cos = dot(scale_ref[...], ch_ref[...])
    inner_sin = dot(scale_ref[...], sh_ref[...])
    line = jnp.sum(sl_ref[...] * inner_cos + cl_ref[...] * inner_sin, axis=0, keepdims=True)
    base = jnp.broadcast_to(-line, (ROWS, span))
    place = lax.broadcasted_iota(jnp.int32, (ROWS, span), 0)
    skew = base
    for i in range(1, ROWS):
        skew = jnp.where(place == i, pltpu.roll(base, i, 1), skew)
    for b in range(LANES // ROWS):
        rows = skew if b == 0 else pltpu.roll(skew, b * ROWS, 1)
        for q in range(tall // LANES):
            at = q * LANES + b * ROWS
            first = q * LANES
            if first:
                band[at : at + ROWS, :first] = rows[:, span - first :]
            band[at : at + ROWS, first:span] = rows[:, : span - first]
    full = band[...]
    high = full.astype(jnp.bfloat16)
    low = (full - high.astype(jnp.float32)).astype(jnp.bfloat16)
    high_ref[:, :span] = high
    low_ref[:, :span] = low
    high_ref[:, span:] = high[:, : wide - span]
    low_ref[:, span:] = low[:, : wide - span]


def circulant(span_filter, span, width):
    tall = min(256, width)
    step, count, tables = circulant_tables(span)
    orders = jnp.arange(span // 2, dtype=jnp.int32).astype(jnp.float32)
    scale = 2.0 / span * (2.0 * jnp.pi / span) * orders * span_filter
    scale = scale.reshape(count, step).T
    band = jax.ShapeDtypeStruct((tall, span + width), jnp.bfloat16)
    return pl.pallas_call(
        circulant_kernel,
        out_shape=[band, band],
        scratch_shapes=[pltpu.VMEM((tall, span), jnp.float32)],
        compiler_params=params(),
        cost_estimate=cost(4e6, 5e6),
        name="circulant_band",
    )(scale, *tables)


def span_kernel(count, starts_ref, high_ref, low_ref, *refs):
    shards = refs[:count]
    acc_ref, out_ref, xh, xl, total = refs[count:]
    fields, depth, rows_y, width = acc_ref.shape
    tall = high_ref.shape[0]
    lines = depth * rows_y
    for number, shard in enumerate(shards):
        flux, _, _, _ = flux_of([shard[k] for k in range(5)], 2)
        for k in range(5):
            value = flux[k].reshape(lines, width)
            rounded = value.astype(jnp.bfloat16)
            xh[k * lines : (k + 1) * lines, :] = rounded
            xl[k * lines : (k + 1) * lines, :] = (value - rounded.astype(jnp.float32)).astype(
                jnp.bfloat16
            )
        for q in range(width // tall):
            start = pl.multiple_of(starts_ref[number * (width // tall) + q], LANES)
            high = high_ref[:, pl.ds(start, width)]
            low = low_ref[:, pl.ds(start, width)]
            left = xh[:, q * tall : (q + 1) * tall]
            right = xl[:, q * tall : (q + 1) * tall]
            part = (
                jnp.dot(left, high, preferred_element_type=jnp.float32)
                + jnp.dot(right, high, preferred_element_type=jnp.float32)
                + jnp.dot(left, low, preferred_element_type=jnp.float32)
            )
            if number == 0 and q == 0:
                total[...] = part
            else:
                total[...] += part
    out_ref[...] = acc_ref[...] - TIME_STEP * total[...].reshape(fields, depth, rows_y, width)


def span_part(masks, shards, band, acc, chunk, chunks):
    fields, depth, rows_all, width = acc.shape
    rows_y = rows_all // chunks
    high, low = band
    tall, wide = high.shape
    span = wide - width
    count = len(shards)
    me = lax.axis_index("gz")
    starts = [
        jnp.mod((me - jnp.bitwise_xor(me, m)) * width - q * tall, span)
        for m in masks
        for q in range(width // tall)
    ]
    starts = jnp.stack(starts).astype(jnp.int32)
    block = pl.BlockSpec((fields, depth, rows_y, width), lambda i, s: (0, 0, chunk, 0))
    shard_specs = [
        block if shard.shape[2] != rows_y else pl.BlockSpec(
            (fields, depth, rows_y, width), lambda i, s: (0, 0, 0, 0)
        )
        for shard in shards
    ]
    lines = fields * depth * rows_y
    return pl.pallas_call(
        functools.partial(span_kernel, count),
        grid_spec=pltpu.PrefetchScalarGridSpec(
            num_scalar_prefetch=1,
            grid=(1,),
            in_specs=[
                pl.BlockSpec((tall, wide), lambda i, s: (0, 0)),
                pl.BlockSpec((tall, wide), lambda i, s: (0, 0)),
            ]
            + shard_specs
            + [block],
            out_specs=block,
            scratch_shapes=[
                pltpu.VMEM((lines, width), jnp.bfloat16),
                pltpu.VMEM((lines, width), jnp.bfloat16),
                pltpu.VMEM((lines, width), jnp.float32),
            ],
        ),
        out_shape=jax.ShapeDtypeStruct(acc.shape, jnp.float32),
        input_output_aliases={3 + count: 0},
        compiler_params=params(),
        cost_estimate=cost(6 * count * lines * width * width, 12 * count * lines * width),
        name="span_lines",
    )(starts, high, low, *shards, acc)


def per_device(state, mask_x, mask_y, span_filter):
    fields, depth, rows_y, width = state.shape
    groups = lax.axis_size("gz")
    slabs = lax.axis_size("gx")
    span = width * groups
    rank = lax.axis_index("gx")
    odd = lax.rem(rank, 2)
    step = rows_y // CHUNKS

    swap = [(i, i ^ 1) for i in range(slabs)]
    carry = [(i, i + 2) for i in range(0, slabs - 2, 2)] + [
        (i, i - 2) for i in range(3, slabs, 2)
    ]
    bits = []
    bit = groups // 2
    while bit:
        bits.append(bit)
        bit //= 2

    mask_next = lax.ppermute(mask_x[0], "gx", [(i + 1, i) for i in range(slabs - 1)])
    pairs, fars, spans = [], [], []
    for c in range(CHUNKS):
        part = lax.slice_in_dim(state, c * step, (c + 1) * step, axis=2)
        pair = lax.ppermute(part, "gx", swap)
        shards = [(0, part)]
        for bit in bits:
            move = [(g, g ^ bit) for g in range(groups)]
            shards = shards + [(m | bit, lax.ppermute(a, "gz", move)) for m, a in shards]
        far = lax.ppermute(lax.dynamic_slice_in_dim(pair, 1 - odd, 3, axis=1), "gx", carry)
        pairs.append(pair)
        fars.append(far)
        spans.append(shards)

    flags = jnp.stack([odd == 0, rank == 0, rank == slabs - 1]).astype(jnp.int32)
    band = circulant(span_filter, span, width)
    acc = wall_part(state, mask_y)
    for c in range(CHUNKS):
        masks = [m for m, _ in spans[c]]
        arrays = [a for _, a in spans[c]]
        acc = span_part(masks, arrays, band, acc, c, CHUNKS)
        acc = stream_part(
            flags, state, pairs[c], fars[c], mask_x, mask_next, acc, c, CHUNKS
        )
    return acc


def solution(mesh):
    return jax.shard_map(
        per_device,
        mesh=mesh,
        in_specs=(P(None, "gx", None, "gz"), P("gx", None, "gz"), P("gx", None, "gz"), P()),
        out_specs=P(None, "gx", None, "gz"),
        check_vma=False,
    )
```

```python
import functools

import jax
import jax.numpy as jnp
import numpy as np
from jax import lax
from jax.experimental import pallas as pl
from jax.experimental.pallas import tpu as pltpu
from jax.sharding import PartitionSpec as P

GAMMA_GAS = 1.4
SMALL_EPS = 1e-06
TIME_STEP = 0.1
ROWS = 8
LANES = 128
BRICK_PARTS = 4
SUM_PARTS = 2
VMEM_BYTES = 24 * 1024 * 1024
FACE_SCALE = -TIME_STEP / 60.0
PLACE = pl.BlockSpec(memory_space=pltpu.VMEM)
ANYWHERE = pl.BlockSpec(memory_space=pl.ANY)


def call(kernel, name, micros, ins, outs, out_shape, scratch=(), aliases=None):
    return pl.pallas_call(
        kernel,
        out_shape=out_shape,
        in_specs=ins,
        out_specs=outs,
        scratch_shapes=list(scratch),
        input_output_aliases=aliases or {},
        compiler_params=pltpu.CompilerParams(vmem_limit_bytes=VMEM_BYTES),
        cost_estimate=pl.CostEstimate(
            flops=int(micros * 1e9), bytes_accessed=int(micros * 3e6), transcendentals=0
        ),
        name=name,
    )


def shape_of(*dims, dtype=jnp.float32):
    return jax.ShapeDtypeStruct(dims, dtype)


def inverse(value):
    first = pl.reciprocal(value, approx=True)
    return first * (2.0 - value * first)


def flux_of(q, normal):
    thin = inverse(q[0])
    velocity = [q[1] * thin, q[2] * thin, q[3] * thin]
    pressure = (GAMMA_GAS - 1.0) * (
        q[4] - 0.5 * (q[1] * velocity[0] + q[2] * velocity[1] + q[3] * velocity[2])
    )
    along = velocity[normal]
    flux = [q[normal + 1], q[1] * along, q[2] * along, q[3] * along, (q[4] + pressure) * along]
    flux[normal + 1] = flux[normal + 1] + pressure
    return flux, pressure, thin, along


def speed_of(pressure, thin, along):
    return jnp.abs(along) + jnp.sqrt(GAMMA_GAS * pressure * thin)


def weno_rest(d1, d2, d3, d4):
    low = d2 * d2 * 0.609375 + 3.0 * SMALL_EPS
    high = d3 * d3 * 0.609375 + 3.0 * SMALL_EPS
    x0 = d1 - 1.375 * d2
    x1 = d2 - 0.625 * d3
    x2 = d4 - 1.375 * d3
    t0 = low + x0 * x0
    t1 = high + x1 * x1
    t2 = high + x2 * x2
    w0 = t1 * t2
    w1 = t0 * t2
    w2 = t0 * t1
    w0 = w0 * w0
    w1 = w1 * w1
    w2 = w2 * w2 * 1.5
    s1 = d2 - d1
    s2 = d3 - d2
    s3 = d4 - d3
    top = w0 * (s2 - s1) + w2 * (s3 - s2)
    bottom = 0.5 * w0 + 3.0 * w1 + w2
    return top * inverse(bottom)


def face_value(dq, df, both, alpha, upwind):
    aq = [alpha * value for value in dq]
    plus = [df[k] + aq[k] for k in range(4)]
    minus = [df[k] - aq[k] for k in range(1, 5)]
    bend = df[1] - df[3]
    central = 7.0 * bend + (df[4] - df[0])
    rest = weno_rest(minus[3], minus[2], minus[1], minus[0]) - weno_rest(*plus)
    biased = 5.0 * (bend + (aq[1] + aq[3]) - (aq[2] + aq[2]) + rest)
    return 30.0 * both + jnp.where(upwind, biased, central)


def lanes(number):
    return pl.ds(pl.multiple_of(number * LANES, LANES), LANES)


def wall_kernel(low, state_ref, mask_ref, base_ref, out_ref, q_s, f_s, speed_s, dq_s, df_s):
    rows_y = state_ref.shape[2]
    width = state_ref.shape[3]
    tiles = rows_y // ROWS
    end = ROWS + rows_y
    zero = jnp.zeros((5, ROWS, LANES), jnp.float32)
    for side in (dq_s, df_s):
        side[:, 0:ROWS, :] = zero
        side[:, end : end + ROWS, :] = zero
    row = lax.broadcasted_iota(jnp.int32, (ROWS, LANES), 0)

    def column(number, carry):
        plane = number // (width // LANES)
        lane = lanes(number % (width // LANES))
        zero_row = jnp.minimum(number, 0)

        def at(r, shift):
            return pl.ds(zero_row + (r * ROWS + ROWS + shift), ROWS)

        def still(r):
            return slice(r * ROWS + ROWS, r * ROWS + 2 * ROWS)

        qs = []
        for r in range(tiles):
            mine = slice(r * ROWS, r * ROWS + ROWS)
            q = [state_ref[k, low + plane, mine, lane] for k in range(5)]
            flux, pressure, thin, along = flux_of(q, 1)
            speed = speed_of(pressure, thin, along)
            for k in range(5):
                q_s[k, still(r), :] = q[k]
                f_s[k, still(r), :] = flux[k]
            speed_s[still(r), :] = speed
            if r == 0:
                for k in range(5):
                    q_s[k, 0:ROWS, :] = jnp.broadcast_to(q[k][0:1], (ROWS, LANES))
                    f_s[k, 0:ROWS, :] = jnp.broadcast_to(flux[k][0:1], (ROWS, LANES))
                speed_s[0:ROWS, :] = jnp.broadcast_to(speed[0:1], (ROWS, LANES))
            if r == tiles - 1:
                speed_s[end : end + ROWS, :] = jnp.broadcast_to(
                    speed[ROWS - 1 : ROWS], (ROWS, LANES)
                )
        for k in range(5):
            changes = [
                (
                    q_s[k, still(r), :] - q_s[k, at(r, -1), :],
                    f_s[k, still(r), :] - f_s[k, at(r, -1), :],
                )
                for r in range(tiles)
            ]
            for r in range(tiles):
                dq_s[k, still(r), :] = changes[r][0]
                df_s[k, still(r), :] = changes[r][1]
        alphas, switches = [], []
        for r in range(tiles):
            alpha = speed_s[still(r), :]
            for shift in (-3, -2, -1, 1, 2):
                alpha = jnp.maximum(alpha, speed_s[at(r, shift), :])
            alphas.append(alpha)
            switches.append(mask_ref[low + plane, r * ROWS : r * ROWS + ROWS, lane] > 0)
        for k in range(5):
            hats = []
            for r in range(tiles):
                dq = [dq_s[k, at(r, s), :] for s in (-2, -1)]
                df = [df_s[k, at(r, s), :] for s in (-2, -1)]
                dq += [dq_s[k, still(r), :]]
                df += [df_s[k, still(r), :]]
                dq += [dq_s[k, at(r, s), :] for s in (1, 2)]
                df += [df_s[k, at(r, s), :] for s in (1, 2)]
                here = f_s[k, still(r), :]
                both = here + here - df[2]
                hats.append(face_value(dq, df, both, alphas[r], switches[r]))
            top = (
                60.0 * f_s[k, end - 1 : end, :]
                + 7.0 * df_s[k, end - 1 : end, :]
                - df_s[k, end - 2 : end - 1, :]
            )
            turned = [pltpu.roll(hat, ROWS - 1, 0) for hat in hats]
            turned.append(jnp.broadcast_to(top, (ROWS, LANES)))
            for r in range(tiles):
                after = jnp.where(row == ROWS - 1, turned[r + 1], turned[r])
                mine = slice(r * ROWS, r * ROWS + ROWS)
                out_ref[k, plane, mine, lane] = base_ref[k, low + plane, mine, lane] + FACE_SCALE * (
                    after - hats[r]
                )
        return carry

    lax.fori_loop(0, out_ref.shape[1] * (width // LANES), column, 0)


def wall_part(state, mask_y, base, low, count, after):
    fields, depth, rows_y, width = state.shape
    tall = rows_y + 2 * ROWS
    padded = pltpu.VMEM((fields, tall, LANES), jnp.float32)

    def kernel(state_ref, mask_ref, base_ref, after_ref, out_ref, *scratch):
        wall_kernel(low, state_ref, mask_ref, base_ref, out_ref, *scratch)

    return call(
        kernel,
        "wall_faces",
        5.0 * count / depth,
        [PLACE, PLACE, PLACE, ANYWHERE],
        PLACE,
        shape_of(fields, count, rows_y, width),
        [padded, padded, pltpu.VMEM((tall, LANES), jnp.float32), padded, padded],
    )(state, mask_y, base, after)


def pack_kernel(parts, state_ref, mask_ref, *refs):
    outs, (mask_s, sems) = refs[:parts], refs[parts:]
    planes, rows_all, width = state_ref.shape
    rows_y = rows_all // parts
    mask_copy = pltpu.make_async_copy(mask_ref.at[0], mask_s, sems.at[parts])
    mask_copy.start()
    copies = [
        pltpu.make_async_copy(
            state_ref.at[:, pl.ds(c * rows_y, rows_y), :], outs[c].at[pl.ds(0, planes)], sems.at[c]
        )
        for c in range(parts)
    ]
    for copy in copies:
        copy.start()
    mask_copy.wait()
    for c in range(parts):
        outs[c][planes] = mask_s[c * rows_y : (c + 1) * rows_y, :].astype(jnp.float32)
    for copy in copies:
        copy.wait()


def pack_part(state, mask_x, parts):
    fields, depth, rows_all, width = state.shape
    planes = fields * depth
    return call(
        functools.partial(pack_kernel, parts),
        "pack_bricks",
        1.0,
        [ANYWHERE, ANYWHERE],
        [PLACE] * parts,
        [shape_of(planes + 1, rows_all // parts, width)] * parts,
        [pltpu.VMEM((rows_all, width), jnp.int32), pltpu.SemaphoreType.DMA((parts + 1,))],
    )(state.reshape(planes, rows_all, width), mask_x)


def pass_kernel(depth, pair_ref, after_ref, out_ref):
    planes = pair_ref.shape[0] - 1
    skip = 1 - lax.rem(lax.axis_index("gx"), 2)
    for k in range(planes // depth):
        for i in range(3):
            out_ref[3 * k + i] = pair_ref[depth * k + i + skip * (depth - 3)]
    out_ref[3 * (planes // depth)] = pair_ref[planes]


def pass_part(pair, depth, after):
    planes, rows_y, width = pair.shape
    return call(
        functools.partial(pass_kernel, depth),
        "pass_planes",
        0.5,
        [PLACE, ANYWHERE],
        PLACE,
        shape_of(3 * (planes - 1) // depth + 1, rows_y, width),
    )(pair, after)


def stream_kernel(start, sum_start, counts, *refs):
    state_ref, pair_ref, far_ref, mask_ref, sum_ref = refs[:5]
    acc_refs = refs[5 : 5 + len(counts)]
    out_ref, dq_s, df_s, both_s, alpha_s, result, sem = refs[-7:]
    fields, depth, _, width = state_ref.shape
    rows_y = result.shape[2]
    rank = lax.axis_index("gx")
    even = lax.rem(rank, 2) == 0
    first = rank == 0
    last = rank == lax.axis_size("gx") - 1
    lane_tiles = width // LANES
    faces = depth + 1
    tiles = (rows_y // ROWS) * lane_tiles

    def place(number):
        row = (number // lane_tiles) * ROWS
        return row, lanes(number % lane_tiles)

    def rows(row, shift):
        return pl.ds(pl.multiple_of(row + shift, ROWS), ROWS)

    def point(number, carry):
        at, lane = place(number)
        row, mine = rows(at, 0), rows(at, start)
        own = [[state_ref[k, i, mine, lane] for k in range(5)] for i in range(depth)]
        cells = []
        for i in range(3):
            cells.append(
                [
                    jnp.where(
                        first,
                        own[0][k],
                        jnp.where(
                            even,
                            far_ref[3 * k + i, row, lane],
                            pair_ref[depth * k + depth - 3 + i, row, lane],
                        ),
                    )
                    for k in range(5)
                ]
            )
        cells += own
        for i in range(3):
            cells.append(
                [
                    jnp.where(
                        last,
                        own[depth - 1][k],
                        jnp.where(
                            even,
                            pair_ref[depth * k + i, row, lane],
                            far_ref[3 * k + i, row, lane],
                        ),
                    )
                    for k in range(5)
                ]
            )
        speeds, before = [], None
        for j, q in enumerate(cells):
            flux, pressure, thin, along = flux_of(q, 0)
            speeds.append(speed_of(pressure, thin, along))
            if j > 0:
                for k in range(5):
                    dq_s[number, k, j - 1] = q[k] - cells[j - 1][k]
                    df_s[number, k, j - 1] = flux[k] - before[k]
                    if 3 <= j < 3 + faces:
                        both_s[number, k, j - 3] = flux[k] + before[k]
            before = flux
        pairs = [jnp.maximum(speeds[i], speeds[i + 1]) for i in range(depth + 5)]
        for f in range(faces):
            alpha_s[number, f] = jnp.maximum(jnp.maximum(pairs[f], pairs[f + 2]), pairs[f + 4])
        return carry

    lax.fori_loop(0, tiles, point, 0)

    def faces_of(number, carry):
        at, lane = place(number)
        row, mine = rows(at, 0), rows(at, start)
        border = jnp.where(
            even, pair_ref[depth * fields, row, lane], far_ref[3 * fields, row, lane]
        )
        border = jnp.where(last, 0.0, border)
        switches = [mask_ref[i, mine, lane] > 0 for i in range(depth)] + [border > 0.0]
        results = []
        for k in range(5):
            dq = [dq_s[number, k, j] for j in range(depth + 5)]
            df = [df_s[number, k, j] for j in range(depth + 5)]
            hats = [
                face_value(
                    dq[f : f + 5], df[f : f + 5], both_s[number, k, f], alpha_s[number, f], switches[f]
                )
                for f in range(faces)
            ]
            plane = 0
            for acc_ref, count in zip(acc_refs, counts):
                for i in range(count):
                    results.append(
                        acc_ref[k, i, mine, lane]
                        - TIME_STEP * sum_ref[k, plane, rows(at, sum_start), lane]
                        + FACE_SCALE * (hats[plane + 1] - hats[plane])
                    )
                    plane += 1
        for k in range(5):
            for i in range(depth):
                result[k, i, row, lane] = results[k * depth + i]
        return carry

    lax.fori_loop(0, tiles, faces_of, 0)
    copy = pltpu.make_async_copy(result, out_ref.at[:, :, pl.ds(start, rows_y), :], sem)
    copy.start()
    copy.wait()


def stream_part(state, pair, far, mask_x, part_sum, sum_start, accs, out, start):
    fields, depth, rows_all, width = state.shape
    rows_y = pair.shape[1]
    tiles = rows_y * width // (ROWS * LANES)
    counts = [acc.shape[1] for acc in accs]
    extra = [] if out is None else [out]
    vregs = functools.partial(lambda *dims: pltpu.VMEM(dims + (ROWS, LANES), jnp.float32))
    return call(
        functools.partial(stream_kernel, start, sum_start, counts),
        "stream_faces",
        8.0 * rows_y / rows_all,
        [PLACE] * (5 + len(accs)) + [ANYWHERE] * len(extra),
        ANYWHERE,
        shape_of(*state.shape),
        [
            vregs(tiles, fields, depth + 5),
            vregs(tiles, fields, depth + 5),
            vregs(tiles, fields, depth + 1),
            vregs(tiles, depth + 1),
            pltpu.VMEM((fields, depth, rows_y, width), jnp.float32),
            pltpu.SemaphoreType.DMA,
        ],
        {5 + len(accs): 0} if extra else None,
    )(state, pair, far, mask_x, part_sum, *accs, *extra)


def circulant_tables(span):
    half = span // 2
    step = 1
    while step * step < half:
        step *= 2
    count = half // step
    places = np.arange(span)
    high = 2.0 * np.pi / span * ((np.arange(count)[:, None] * step * places[None]) % span)
    low = 2.0 * np.pi / span * ((np.arange(step)[:, None] * places[None]) % span)
    tables = np.concatenate([np.cos(high), np.sin(high), np.cos(low), np.sin(low)])
    return step, count, jnp.asarray(tables.astype(np.float32))


def circulant_kernel(count, step, scale_ref, table_ref, high_ref, low_ref, band):
    span = table_ref.shape[1]
    tall, wide = high_ref.shape
    dot = functools.partial(
        jnp.dot, precision=lax.Precision.HIGHEST, preferred_element_type=jnp.float32
    )
    inner_cos = dot(scale_ref[...], table_ref[0:count])
    inner_sin = dot(scale_ref[...], table_ref[count : 2 * count])
    low_cos = table_ref[2 * count : 2 * count + step]
    low_sin = table_ref[2 * count + step :]
    line = jnp.sum(low_sin * inner_cos + low_cos * inner_sin, axis=0, keepdims=True)
    base = jnp.broadcast_to(-line, (ROWS, span))
    place = lax.broadcasted_iota(jnp.int32, (ROWS, span), 0)
    skew = base
    for i in range(1, ROWS):
        skew = jnp.where(place == i, pltpu.roll(base, i, 1), skew)
    for b in range(LANES // ROWS):
        rows = skew if b == 0 else pltpu.roll(skew, b * ROWS, 1)
        for q in range(tall // LANES):
            at = q * LANES + b * ROWS
            first = q * LANES
            if first:
                band[at : at + ROWS, :first] = rows[:, span - first :]
            band[at : at + ROWS, first:span] = rows[:, : span - first]
    full = band[...]
    high = full.astype(jnp.bfloat16)
    low = (full - high.astype(jnp.float32)).astype(jnp.bfloat16)
    high_ref[:, :span] = high
    low_ref[:, :span] = low
    high_ref[:, span:] = high[:, : wide - span]
    low_ref[:, span:] = low[:, : wide - span]


def circulant(span_filter, span, width):
    tall = min(256, width)
    step, count, tables = circulant_tables(span)
    orders = jnp.arange(span // 2, dtype=jnp.int32).astype(jnp.float32)
    scale = 2.0 / span * (2.0 * jnp.pi / span) * orders * span_filter
    scale = scale.reshape(count, step).T
    band = shape_of(tall, span + width, dtype=jnp.bfloat16)
    return call(
        functools.partial(circulant_kernel, count, step),
        "circulant_band",
        1.0,
        [PLACE, PLACE],
        [PLACE, PLACE],
        [band, band],
        [pltpu.VMEM((tall, span), jnp.float32)],
    )(scale, tables)


def fill_lines(shards, x_refs):
    _, depth, rows_y, width = shards[0].shape
    xh, xl = x_refs
    for number, shard in enumerate(shards):

        def plane(index, carry):
            i = index // (width // LANES)
            t = index % (width // LANES)
            flux, _, _, _ = flux_of([shard[k, i, :, lanes(t)] for k in range(5)], 2)
            to = lanes(t + number * (width // LANES))
            for k in range(5):
                high = flux[k].astype(jnp.bfloat16)
                line = pl.ds(pl.multiple_of((k * depth + i) * rows_y, rows_y), rows_y)
                xh[line, to] = high
                xl[line, to] = (flux[k] - high.astype(jnp.float32)).astype(jnp.bfloat16)
            return carry

        lax.fori_loop(0, depth * (width // LANES), plane, 0)


def product(target, sources, high_ref, low_ref, xh, xl, w_s):
    tall, wide = high_ref.shape
    width = xh.shape[1] // len(sources)
    span = wide - width
    deep = xh.shape[1]
    for number, source in enumerate(sources):
        for q in range(width // tall):
            start = lax.rem((target - source) * width - q * tall + 2 * span, span)
            start = pl.multiple_of(start, LANES)
            at = number * width + q * tall
            w_s[at : at + tall, :] = high_ref[:, pl.ds(start, width)]
            w_s[deep + at : deep + at + tall, :] = low_ref[:, pl.ds(start, width)]
    dot = functools.partial(jnp.dot, preferred_element_type=jnp.float32)
    high = w_s[:deep, :]
    return dot(xh[...], high) + dot(xl[...], high) + dot(xh[...], w_s[deep:, :])


def away_kernel(masks, parts, high_ref, low_ref, own_ref, core_ref, after_ref, *refs):
    sums = refs[: len(masks) * parts]
    xh, xl, w_s = refs[len(masks) * parts :]
    fields, depth, rows_all, width = own_ref.shape
    rows_y = rows_all // parts
    me = lax.axis_index("gz")
    fill_lines([own_ref, core_ref], [xh, xl])
    for number, mask in enumerate(masks):
        total = product(me ^ mask, [me, me ^ 1], high_ref, low_ref, xh, xl, w_s)
        total = total.reshape(fields, depth, rows_all, width)
        for c in range(parts):
            sums[number * parts + c][...] = total[:, :, c * rows_y : (c + 1) * rows_y, :]


def away_part(band, state, core, masks, parts, after):
    fields, depth, rows_all, width = state.shape
    lines = fields * depth * rows_all
    line = shape_of(lines, 2 * width, dtype=jnp.bfloat16)
    count = len(masks) * parts
    outs = call(
        functools.partial(away_kernel, masks, parts),
        "span_away",
        3.0,
        [PLACE] * 4 + [ANYWHERE],
        [PLACE] * (count + 2),
        [shape_of(fields, depth, rows_all // parts, width)] * count + [line, line],
        [pltpu.VMEM((4 * width, width), jnp.bfloat16)],
    )(*band, state, core, after)
    return outs[:count], outs[count:]


def home_kernel(high_ref, low_ref, xh, xl, state_ref, out_ref, w_s):
    me = lax.axis_index("gz")
    total = product(me, [me, me ^ 1], high_ref, low_ref, xh, xl, w_s)
    out_ref[...] = state_ref[...] - TIME_STEP * total.reshape(state_ref.shape)


def home_part(band, lines, state):
    width = state.shape[3]
    return call(
        home_kernel,
        "span_home",
        2.0,
        [PLACE] * 5,
        PLACE,
        shape_of(*state.shape),
        [pltpu.VMEM((4 * width, width), jnp.bfloat16)],
    )(*band, *lines, state)


def per_device(state, mask_x, mask_y, span_filter):
    fields, depth, rows_all, width = state.shape
    groups = lax.axis_size("gz")
    slabs = lax.axis_size("gx")
    span = width * groups

    def flip(array, bit):
        return lax.ppermute(array, "gz", [(g, g ^ bit) for g in range(groups)])

    swap = [(i, i ^ 1) for i in range(slabs)]
    carry = [(i, i + 2) for i in range(0, slabs - 2, 2)] + [
        (i, i - 2) for i in range(3, slabs, 2)
    ]
    core = flip(state, 1)
    bricks = pack_part(state, mask_x, BRICK_PARTS)
    pairs = [lax.ppermute(brick, "gx", swap) for brick in bricks]
    band = circulant(span_filter, span, width)

    masks = list(range(2, groups, 2))
    sums, lines = away_part(band, state, core, masks, SUM_PARTS, bricks[0])
    arrived = [
        sum(
            flip(sums[n * SUM_PARTS + c], mask) for n, mask in enumerate(masks)
        )
        for c in range(SUM_PARTS)
    ]
    half = depth // 2
    fars = []

    def hand_on(c, after):
        fars.append(lax.ppermute(pass_part(pairs[c], depth, after), "gx", carry))

    hand_on(0, lines[0])
    base = home_part(band, lines, state)
    acc_low = wall_part(state, mask_y, base, 0, half, lines[0])
    hand_on(1, acc_low)
    acc_high = wall_part(state, mask_y, base, half, depth - half, acc_low)
    for c in range(2, BRICK_PARTS):
        hand_on(c, acc_high)

    out = None
    step = rows_all // BRICK_PARTS
    wide = rows_all // SUM_PARTS
    for c in range(BRICK_PARTS):
        out = stream_part(
            state,
            pairs[c],
            fars[c],
            mask_x,
            arrived[c * step // wide],
            c * step % wide,
            [acc_low, acc_high],
            out,
            c * step,
        )
    return out


def solution(mesh):
    return jax.shard_map(
        per_device,
        mesh=mesh,
        in_specs=(P(None, "gx", None, "gz"), P("gx", None, "gz"), P("gx", None, "gz"), P()),
        out_specs=P(None, "gx", None, "gz"),
        check_vma=False,
    )
```

```python
import functools

import jax
import jax.numpy as jnp
import numpy as np
from jax import lax
from jax.experimental import pallas as pl
from jax.experimental.pallas import tpu as pltpu
from jax.sharding import PartitionSpec as P

GAMMA_GAS = 1.4
SMALL_EPS = 1e-06
TIME_STEP = 0.1
ROWS = 8
LANES = 128
BRICK_PARTS = (2, 1, 1)
SUM_PARTS = 2
VMEM_BYTES = 24 * 1024 * 1024
FACE_SCALE = -TIME_STEP / 60.0
PLACE = pl.BlockSpec(memory_space=pltpu.VMEM)
ANYWHERE = pl.BlockSpec(memory_space=pl.ANY)
HBM = pl.BlockSpec(memory_space=pltpu.HBM)


def call(kernel, name, weight, ins, outs, out_shape, scratch=(), aliases=None):
    return pl.pallas_call(
        kernel,
        out_shape=out_shape,
        in_specs=ins,
        out_specs=outs,
        scratch_shapes=list(scratch),
        input_output_aliases=aliases or {},
        compiler_params=pltpu.CompilerParams(vmem_limit_bytes=VMEM_BYTES),
        cost_estimate=pl.CostEstimate(
            flops=int(weight * 1e8), bytes_accessed=int(weight * 3e5), transcendentals=0
        ),
        name=name,
    )


def shape_of(*dims, dtype=jnp.float32):
    return jax.ShapeDtypeStruct(dims, dtype)


def inverse(value):
    first = pl.reciprocal(value, approx=True)
    return first * (2.0 - value * first)


def flux_of(q, normal):
    thin = inverse(q[0])
    velocity = [q[1] * thin, q[2] * thin, q[3] * thin]
    pressure = (GAMMA_GAS - 1.0) * (
        q[4] - 0.5 * (q[1] * velocity[0] + q[2] * velocity[1] + q[3] * velocity[2])
    )
    along = velocity[normal]
    flux = [q[normal + 1], q[1] * along, q[2] * along, q[3] * along, (q[4] + pressure) * along]
    flux[normal + 1] = flux[normal + 1] + pressure
    return flux, pressure, thin, along


def speed_of(pressure, thin, along):
    return jnp.abs(along) + jnp.sqrt(GAMMA_GAS * pressure * thin)


def weno_rest(d1, d2, d3, d4):
    low = d2 * d2 * 0.609375 + 3.0 * SMALL_EPS
    high = d3 * d3 * 0.609375 + 3.0 * SMALL_EPS
    x0 = d1 - 1.375 * d2
    x1 = d2 - 0.625 * d3
    x2 = d4 - 1.375 * d3
    t0 = low + x0 * x0
    t1 = high + x1 * x1
    t2 = high + x2 * x2
    w0 = t1 * t2
    w1 = t0 * t2
    w2 = t0 * t1
    w0 = w0 * w0
    w1 = w1 * w1
    w2 = w2 * w2 * 1.5
    top = w0 * (x0 + (d3 - 0.625 * d2)) + w2 * (x1 + x2)
    bottom = 0.5 * w0 + 3.0 * w1 + w2
    return top * pl.reciprocal(bottom, approx=True)


def face_value(dq, df, both, alpha, upwind):
    aq = [alpha * value for value in dq]
    plus = [df[k] + aq[k] for k in range(4)]
    minus = [df[k] - aq[k] for k in range(1, 5)]
    bend = df[1] - df[3]
    central = 7.0 * bend + (df[4] - df[0])
    rest = weno_rest(minus[3], minus[2], minus[1], minus[0]) - weno_rest(*plus)
    biased = 5.0 * (bend + (aq[1] + aq[3]) - (aq[2] + aq[2]) + rest)
    return 30.0 * both + jnp.where(upwind, biased, central)


def lanes(number):
    return pl.ds(pl.multiple_of(number * LANES, LANES), LANES)


def wall_kernel(low, state_ref, mask_ref, base_ref, out_ref, q_s, f_s, speed_s, dq_s, df_s):
    rows_y = state_ref.shape[2]
    width = state_ref.shape[3]
    tiles = rows_y // ROWS
    end = ROWS + rows_y
    zero = jnp.zeros((5, ROWS, LANES), jnp.float32)
    for side in (dq_s, df_s):
        side[:, 0:ROWS, :] = zero
        side[:, end : end + ROWS, :] = zero
    row = lax.broadcasted_iota(jnp.int32, (ROWS, LANES), 0)

    def column(number, carry):
        plane = number // (width // LANES)
        lane = lanes(number % (width // LANES))
        zero_row = jnp.minimum(number, 0)

        def at(r, shift):
            return pl.ds(zero_row + (r * ROWS + ROWS + shift), ROWS)

        def still(r):
            return slice(r * ROWS + ROWS, r * ROWS + 2 * ROWS)

        qs = []
        for r in range(tiles):
            mine = slice(r * ROWS, r * ROWS + ROWS)
            q = [state_ref[k, low + plane, mine, lane] for k in range(5)]
            flux, pressure, thin, along = flux_of(q, 1)
            speed = speed_of(pressure, thin, along)
            for k in range(5):
                q_s[k, still(r), :] = q[k]
                f_s[k, still(r), :] = flux[k]
            speed_s[still(r), :] = speed
            if r == 0:
                for k in range(5):
                    q_s[k, 0:ROWS, :] = jnp.broadcast_to(q[k][0:1], (ROWS, LANES))
                    f_s[k, 0:ROWS, :] = jnp.broadcast_to(flux[k][0:1], (ROWS, LANES))
                speed_s[0:ROWS, :] = jnp.broadcast_to(speed[0:1], (ROWS, LANES))
            if r == tiles - 1:
                speed_s[end : end + ROWS, :] = jnp.broadcast_to(
                    speed[ROWS - 1 : ROWS], (ROWS, LANES)
                )
        for k in range(5):
            changes = [
                (
                    q_s[k, still(r), :] - q_s[k, at(r, -1), :],
                    f_s[k, still(r), :] - f_s[k, at(r, -1), :],
                )
                for r in range(tiles)
            ]
            for r in range(tiles):
                dq_s[k, still(r), :] = changes[r][0]
                df_s[k, still(r), :] = changes[r][1]
        alphas, switches = [], []
        for r in range(tiles):
            alpha = speed_s[still(r), :]
            for shift in (-3, -2, -1, 1, 2):
                alpha = jnp.maximum(alpha, speed_s[at(r, shift), :])
            alphas.append(alpha)
            switches.append(mask_ref[low + plane, r * ROWS : r * ROWS + ROWS, lane] > 0)
        for k in range(5):
            hats = []
            for r in range(tiles):
                dq = [dq_s[k, at(r, s), :] for s in (-2, -1)]
                df = [df_s[k, at(r, s), :] for s in (-2, -1)]
                dq += [dq_s[k, still(r), :]]
                df += [df_s[k, still(r), :]]
                dq += [dq_s[k, at(r, s), :] for s in (1, 2)]
                df += [df_s[k, at(r, s), :] for s in (1, 2)]
                here = f_s[k, still(r), :]
                both = here + here - df[2]
                hats.append(face_value(dq, df, both, alphas[r], switches[r]))
            top = (
                60.0 * f_s[k, end - 1 : end, :]
                + 7.0 * df_s[k, end - 1 : end, :]
                - df_s[k, end - 2 : end - 1, :]
            )
            turned = [pltpu.roll(hat, ROWS - 1, 0) for hat in hats]
            turned.append(jnp.broadcast_to(top, (ROWS, LANES)))
            for r in range(tiles):
                after = jnp.where(row == ROWS - 1, turned[r + 1], turned[r])
                mine = slice(r * ROWS, r * ROWS + ROWS)
                out_ref[k, plane, mine, lane] = base_ref[k, low + plane, mine, lane] + FACE_SCALE * (
                    after - hats[r]
                )
        return carry

    lax.fori_loop(0, out_ref.shape[1] * (width // LANES), column, 0)


def wall_part(state, mask_y, base, low, count, after):
    fields, depth, rows_y, width = state.shape
    tall = rows_y + 2 * ROWS
    padded = pltpu.VMEM((fields, tall, LANES), jnp.float32)

    def kernel(state_ref, mask_ref, base_ref, after_ref, out_ref, *scratch):
        wall_kernel(low, state_ref, mask_ref, base_ref, out_ref, *scratch)

    return call(
        kernel,
        "wall_faces",
        5.0 * count / depth,
        [PLACE, PLACE, PLACE, ANYWHERE],
        PLACE,
        shape_of(fields, count, rows_y, width),
        [padded, padded, pltpu.VMEM((tall, LANES), jnp.float32), padded, padded],
    )(state, mask_y, base, after)


def pack_kernel(parts, state_ref, mask_ref, *outs):
    planes = state_ref.shape[0]
    for (start, rows), out in zip(parts, outs):

        def plane(index, carry):
            out[index] = state_ref[index, start : start + rows, :]
            return carry

        lax.fori_loop(0, planes, plane, 0, unroll=2)
        out[planes] = mask_ref[start : start + rows, :].astype(jnp.float32)


def pack_part(state, mask_x, parts):
    fields, depth, rows_all, width = state.shape
    planes = fields * depth
    return call(
        functools.partial(pack_kernel, parts),
        "pack_bricks",
        0.5,
        [PLACE, PLACE],
        [PLACE] * len(parts),
        [shape_of(planes + 1, rows, width) for _, rows in parts],
    )(state.reshape(planes, rows_all, width), mask_x[0])


def pass_kernel(depth, pair_ref, after_ref, out_ref):
    planes = pair_ref.shape[0] - 1
    skip = 1 - lax.rem(lax.axis_index("gx"), 2)
    for k in range(planes // depth):
        for i in range(3):
            out_ref[3 * k + i] = pair_ref[depth * k + i + skip * (depth - 3)]
    out_ref[3 * (planes // depth)] = pair_ref[planes]


def pass_part(pair, depth, after):
    planes, rows_y, width = pair.shape
    return call(
        functools.partial(pass_kernel, depth),
        "pass_planes",
        0.5,
        [PLACE, ANYWHERE],
        PLACE,
        shape_of(3 * (planes - 1) // depth + 1, rows_y, width),
    )(pair, after)


def stream_kernel(start, sum_start, counts, *refs):
    state_ref, pair_ref, far_ref, mask_ref, sum_ref = refs[:5]
    acc_refs = refs[5 : 5 + len(counts)]
    out_ref, dq_s, df_s, both_s, alpha_s, result, sem = refs[-7:]
    fields, depth, _, width = state_ref.shape
    rows_y = result.shape[2]
    rank = lax.axis_index("gx")
    even = lax.rem(rank, 2) == 0
    first = rank == 0
    last = rank == lax.axis_size("gx") - 1
    lane_tiles = width // LANES
    faces = depth + 1
    tiles = (rows_y // ROWS) * lane_tiles

    def place(number):
        row = (number // lane_tiles) * ROWS
        return row, lanes(number % lane_tiles)

    def rows(row, shift):
        return pl.ds(pl.multiple_of(row + shift, ROWS), ROWS)

    def point(number, carry):
        at, lane = place(number)
        row, mine = rows(at, 0), rows(at, start)
        own = [[state_ref[k, i, mine, lane] for k in range(5)] for i in range(depth)]
        cells = []
        for i in range(3):
            cells.append(
                [
                    jnp.where(
                        first,
                        own[0][k],
                        jnp.where(
                            even,
                            far_ref[3 * k + i, row, lane],
                            pair_ref[depth * k + depth - 3 + i, row, lane],
                        ),
                    )
                    for k in range(5)
                ]
            )
        cells += own
        for i in range(3):
            cells.append(
                [
                    jnp.where(
                        last,
                        own[depth - 1][k],
                        jnp.where(
                            even,
                            pair_ref[depth * k + i, row, lane],
                            far_ref[3 * k + i, row, lane],
                        ),
                    )
                    for k in range(5)
                ]
            )
        speeds, before = [], None
        for j, q in enumerate(cells):
            flux, pressure, thin, along = flux_of(q, 0)
            speeds.append(speed_of(pressure, thin, along))
            if j > 0:
                for k in range(5):
                    dq_s[number, k, j - 1] = q[k] - cells[j - 1][k]
                    df_s[number, k, j - 1] = flux[k] - before[k]
                    if 3 <= j < 3 + faces:
                        both_s[number, k, j - 3] = flux[k] + before[k]
            before = flux
        pairs = [jnp.maximum(speeds[i], speeds[i + 1]) for i in range(depth + 5)]
        for f in range(faces):
            alpha_s[number, f] = jnp.maximum(jnp.maximum(pairs[f], pairs[f + 2]), pairs[f + 4])
        return carry

    lax.fori_loop(0, tiles, point, 0)

    def faces_of(number, carry):
        at, lane = place(number)
        row, mine = rows(at, 0), rows(at, start)
        border = jnp.where(
            even, pair_ref[depth * fields, row, lane], far_ref[3 * fields, row, lane]
        )
        border = jnp.where(last, 0.0, border)
        switches = [mask_ref[i, mine, lane] > 0 for i in range(depth)] + [border > 0.0]
        results = []
        for k in range(5):
            dq = [dq_s[number, k, j] for j in range(depth + 5)]
            df = [df_s[number, k, j] for j in range(depth + 5)]
            hats = [
                face_value(
                    dq[f : f + 5], df[f : f + 5], both_s[number, k, f], alpha_s[number, f], switches[f]
                )
                for f in range(faces)
            ]
            plane = 0
            for acc_ref, count in zip(acc_refs, counts):
                for i in range(count):
                    results.append(
                        acc_ref[k, i, mine, lane]
                        - TIME_STEP * sum_ref[k, plane, rows(at, sum_start), lane]
                        + FACE_SCALE * (hats[plane + 1] - hats[plane])
                    )
                    plane += 1
        for k in range(5):
            for i in range(depth):
                result[k, i, row, lane] = results[k * depth + i]
        hand_out(number).start()
        return carry

    def hand_out(number):
        at, lane = place(number)
        return pltpu.make_async_copy(
            result.at[:, :, rows(at, 0), lane], out_ref.at[:, :, rows(at, start), lane], sem.at[number]
        )

    def settle(number, carry):
        hand_out(number).wait()
        return carry

    lax.fori_loop(0, tiles, faces_of, 0)
    lax.fori_loop(0, tiles, settle, 0)


def stream_part(state, pair, far, mask_x, part_sum, sum_start, accs, out, start):
    fields, depth, rows_all, width = state.shape
    rows_y = pair.shape[1]
    tiles = rows_y * width // (ROWS * LANES)
    counts = [acc.shape[1] for acc in accs]
    extra = [] if out is None else [out]
    vregs = functools.partial(lambda *dims: pltpu.VMEM(dims + (ROWS, LANES), jnp.float32))
    return call(
        functools.partial(stream_kernel, start, sum_start, counts),
        "stream_faces",
        8.0 * rows_y / rows_all,
        [PLACE] * (5 + len(accs)) + [HBM] * len(extra),
        HBM,
        shape_of(*state.shape),
        [
            vregs(tiles, fields, depth + 5),
            vregs(tiles, fields, depth + 5),
            vregs(tiles, fields, depth + 1),
            vregs(tiles, depth + 1),
            pltpu.VMEM((fields, depth, rows_y, width), jnp.float32),
            pltpu.SemaphoreType.DMA((tiles,)),
        ],
        {5 + len(accs): 0} if extra else None,
    )(state, pair, far, mask_x, part_sum, *accs, *extra)


def circulant_tables(span):
    half = span // 2
    step = 1
    while step * step < half:
        step *= 2
    count = half // step
    places = np.arange(span)
    period = max(2 * count, LANES)
    high = 2.0 * np.pi / span * ((np.arange(count)[:, None] * step * places[None, :period]) % span)
    low = 2.0 * np.pi / span * ((np.arange(step)[:, None] * places[None]) % span)
    tables = [np.concatenate([np.cos(a), np.sin(a)]) for a in (high, low)]
    return step, count, [jnp.asarray(t.astype(np.float32)) for t in tables]


def circulant_kernel(count, step, scale_ref, inner_ref, outer_ref, high_ref, low_ref, band):
    period = inner_ref.shape[1]
    span = outer_ref.shape[1]
    tall, wide = high_ref.shape
    dot = functools.partial(
        jnp.dot, precision=lax.Precision.HIGHEST, preferred_element_type=jnp.float32
    )
    repeat = span // period
    inner_cos = jnp.concatenate([dot(scale_ref[...], inner_ref[:count])] * repeat, 1)
    inner_sin = jnp.concatenate([dot(scale_ref[...], inner_ref[count:])] * repeat, 1)
    line = jnp.sum(
        outer_ref[step:] * inner_cos + outer_ref[:step] * inner_sin, axis=0, keepdims=True
    )
    base = jnp.broadcast_to(-line, (ROWS, span))
    place = lax.broadcasted_iota(jnp.int32, (ROWS, span), 0)
    skew = base
    for i in range(1, ROWS):
        skew = jnp.where(place == i, pltpu.roll(base, i, 1), skew)
    for b in range(LANES // ROWS):
        rows = skew if b == 0 else pltpu.roll(skew, b * ROWS, 1)
        for q in range(tall // LANES):
            at = q * LANES + b * ROWS
            first = q * LANES
            if first:
                band[at : at + ROWS, :first] = rows[:, span - first :]
            band[at : at + ROWS, first:span] = rows[:, : span - first]
    full = band[...]
    high = full.astype(jnp.bfloat16)
    low = (full - high.astype(jnp.float32)).astype(jnp.bfloat16)
    high_ref[:, :span] = high
    low_ref[:, :span] = low
    high_ref[:, span:] = high[:, : wide - span]
    low_ref[:, span:] = low[:, : wide - span]


def circulant(span_filter, span, width):
    tall = min(256, width)
    step, count, tables = circulant_tables(span)
    orders = jnp.arange(span // 2, dtype=jnp.int32).astype(jnp.float32)
    scale = 2.0 / span * (2.0 * jnp.pi / span) * orders * span_filter
    scale = scale.reshape(count, step).T
    band = shape_of(tall, span + width, dtype=jnp.bfloat16)
    return call(
        functools.partial(circulant_kernel, count, step),
        "circulant_band",
        1.0,
        [PLACE, PLACE, PLACE],
        [PLACE, PLACE],
        [band, band],
        [pltpu.VMEM((tall, span), jnp.float32)],
    )(scale, *tables)


def fill_lines(shards, x_refs):
    _, depth, rows_y, width = shards[0].shape
    xh, xl = x_refs
    for number, shard in enumerate(shards):

        def plane(index, carry):
            i = index // (width // LANES)
            t = index % (width // LANES)
            flux, _, _, _ = flux_of([shard[k, i, :, lanes(t)] for k in range(5)], 2)
            to = lanes(t + number * (width // LANES))
            for k in range(5):
                high = flux[k].astype(jnp.bfloat16)
                line = pl.ds(pl.multiple_of((k * depth + i) * rows_y, rows_y), rows_y)
                xh[line, to] = high
                xl[line, to] = (flux[k] - high.astype(jnp.float32)).astype(jnp.bfloat16)
            return carry

        lax.fori_loop(0, depth * (width // LANES), plane, 0)


def product(target, sources, high_ref, low_ref, xh, xl, w_s):
    tall, wide = high_ref.shape
    width = xh.shape[1] // len(sources)
    span = wide - width
    deep = xh.shape[1]
    for number, source in enumerate(sources):
        for q in range(width // tall):
            start = lax.rem((target - source) * width - q * tall + 2 * span, span)
            start = pl.multiple_of(start, LANES)
            at = number * width + q * tall
            w_s[at : at + tall, :] = high_ref[:, pl.ds(start, width)]
            w_s[deep + at : deep + at + tall, :] = low_ref[:, pl.ds(start, width)]
    dot = functools.partial(jnp.dot, preferred_element_type=jnp.float32)
    high = w_s[:deep, :]
    return dot(xh[...], high) + dot(xl[...], high) + dot(xh[...], w_s[deep:, :])


def away_kernel(masks, parts, high_ref, low_ref, own_ref, core_ref, after_ref, *refs):
    sums = refs[: len(masks) * parts]
    xh, xl, w_s = refs[len(masks) * parts :]
    fields, depth, rows_all, width = own_ref.shape
    rows_y = rows_all // parts
    me = lax.axis_index("gz")
    fill_lines([own_ref, core_ref], [xh, xl])
    for number, mask in enumerate(masks):
        total = product(me ^ mask, [me, me ^ 1], high_ref, low_ref, xh, xl, w_s)
        total = total.reshape(fields, depth, rows_all, width)
        for c in range(parts):
            sums[number * parts + c][...] = total[:, :, c * rows_y : (c + 1) * rows_y, :]


def away_part(band, state, core, masks, parts, after):
    fields, depth, rows_all, width = state.shape
    lines = fields * depth * rows_all
    line = shape_of(lines, 2 * width, dtype=jnp.bfloat16)
    count = len(masks) * parts
    outs = call(
        functools.partial(away_kernel, masks, parts),
        "span_away",
        3.0,
        [PLACE] * 4 + [ANYWHERE],
        [PLACE] * (count + 2),
        [shape_of(fields, depth, rows_all // parts, width)] * count + [line, line],
        [pltpu.VMEM((4 * width, width), jnp.bfloat16)],
    )(*band, state, core, after)
    return outs[:count], outs[count:]


def home_kernel(high_ref, low_ref, xh, xl, state_ref, out_ref, w_s):
    me = lax.axis_index("gz")
    total = product(me, [me, me ^ 1], high_ref, low_ref, xh, xl, w_s)
    out_ref[...] = state_ref[...] - TIME_STEP * total.reshape(state_ref.shape)


def home_part(band, lines, state):
    width = state.shape[3]
    return call(
        home_kernel,
        "span_home",
        2.0,
        [PLACE] * 5,
        PLACE,
        shape_of(*state.shape),
        [pltpu.VMEM((4 * width, width), jnp.bfloat16)],
    )(*band, *lines, state)


def per_device(state, mask_x, mask_y, span_filter):
    fields, depth, rows_all, width = state.shape
    groups = lax.axis_size("gz")
    slabs = lax.axis_size("gx")
    span = width * groups

    def flip(array, bit):
        return lax.ppermute(array, "gz", [(g, g ^ bit) for g in range(groups)])

    swap = [(i, i ^ 1) for i in range(slabs)]
    carry = [(i, i + 2) for i in range(0, slabs - 2, 2)] + [
        (i, i - 2) for i in range(3, slabs, 2)
    ]
    core = flip(state, 1)
    unit = rows_all // sum(BRICK_PARTS)
    parts, start = [], 0
    for share in BRICK_PARTS:
        parts.append((start, share * unit))
        start += share * unit
    bricks = pack_part(state, mask_x, parts)
    pairs = [lax.ppermute(brick, "gx", swap) for brick in bricks]
    band = circulant(span_filter, span, width)

    masks = list(range(2, groups, 2))
    sums, lines = away_part(band, state, core, masks, SUM_PARTS, bricks[0])
    arrived = [
        sum(flip(sums[n * SUM_PARTS + c], mask) for n, mask in enumerate(masks))
        for c in range(SUM_PARTS)
    ]
    half = depth // 2
    wide = rows_all // SUM_PARTS

    def hand_on(c, after):
        return lax.ppermute(pass_part(pairs[c], depth, after), "gx", carry)

    base = home_part(band, lines, state)
    acc_low = wall_part(state, mask_y, base, 0, half, lines[0])
    fars = [hand_on(0, acc_low)]
    acc_high = wall_part(state, mask_y, base, half, depth - half, acc_low)
    fars += [hand_on(c, acc_high) for c in range(1, len(parts))]

    out = None
    for c, (start, _) in enumerate(parts):
        out = stream_part(
            state,
            pairs[c],
            fars[c],
            mask_x,
            arrived[start // wide],
            start % wide,
            [acc_low, acc_high],
            out,
            start,
        )
    return out


def solution(mesh):
    return jax.shard_map(
        per_device,
        mesh=mesh,
        in_specs=(P(None, "gx", None, "gz"), P("gx", None, "gz"), P("gx", None, "gz"), P()),
        out_specs=P(None, "gx", None, "gz"),
        check_vma=False,
    )
```

```python
import functools

import jax
import jax.numpy as jnp
import numpy as np
from jax import lax
from jax.experimental import pallas as pl
from jax.experimental.pallas import tpu as pltpu
from jax.sharding import PartitionSpec as P

GAMMA_GAS = 1.4
SMALL_EPS = 1e-06
TIME_STEP = 0.1
ROWS = 8
LANES = 128
SUM_PARTS = 2
VMEM_BYTES = 24 * 1024 * 1024
PACK_BYTES = 60 * 1024 * 1024
FACE_SCALE = -TIME_STEP / 60.0
PLACE = pl.BlockSpec(memory_space=pltpu.VMEM)
ANYWHERE = pl.BlockSpec(memory_space=pl.ANY)
HBM = pl.BlockSpec(memory_space=pltpu.HBM)


def call(kernel, name, weight, ins, outs, out_shape, scratch=(), aliases=None, vmem=VMEM_BYTES):
    return pl.pallas_call(
        kernel,
        out_shape=out_shape,
        in_specs=ins,
        out_specs=outs,
        scratch_shapes=list(scratch),
        input_output_aliases=aliases or {},
        compiler_params=pltpu.CompilerParams(vmem_limit_bytes=vmem),
        cost_estimate=pl.CostEstimate(
            flops=int(weight * 1e8), bytes_accessed=int(weight * 3e5), transcendentals=0
        ),
        name=name,
    )


def shape_of(*dims, dtype=jnp.float32):
    return jax.ShapeDtypeStruct(dims, dtype)


def flux_of(q, normal):
    thin = pl.reciprocal(q[0], approx=True)
    velocity = [q[1] * thin, q[2] * thin, q[3] * thin]
    pressure = (GAMMA_GAS - 1.0) * (
        q[4] - 0.5 * (q[1] * velocity[0] + q[2] * velocity[1] + q[3] * velocity[2])
    )
    along = velocity[normal]
    flux = [q[normal + 1], q[1] * along, q[2] * along, q[3] * along, (q[4] + pressure) * along]
    flux[normal + 1] = flux[normal + 1] + pressure
    return flux, pressure, thin, along


def speed_of(pressure, thin, along):
    return jnp.abs(along) + jnp.sqrt(GAMMA_GAS * pressure * thin)


def weno_rest(d1, d2, d3, d4):
    low = d2 * d2 * 0.609375 + 3.0 * SMALL_EPS
    high = d3 * d3 * 0.609375 + 3.0 * SMALL_EPS
    x0 = d1 - 1.375 * d2
    x1 = d2 - 0.625 * d3
    x2 = d4 - 1.375 * d3
    t0 = low + x0 * x0
    t1 = high + x1 * x1
    t2 = high + x2 * x2
    w0 = t1 * t2
    w1 = t0 * t2
    w2 = t0 * t1
    w0 = w0 * w0
    w1 = w1 * w1
    w2 = w2 * w2 * 1.5
    top = w0 * (x0 + (d3 - 0.625 * d2)) + w2 * (x1 + x2)
    bottom = 0.5 * w0 + 3.0 * w1 + w2
    return top * pl.reciprocal(bottom, approx=True)


def face_value(dq, df, both, alpha, upwind):
    aq = [alpha * value for value in dq]
    plus = [df[k] + aq[k] for k in range(4)]
    minus = [df[k] - aq[k] for k in range(1, 5)]
    bend = df[1] - df[3]
    central = 7.0 * bend + (df[4] - df[0])
    rest = weno_rest(minus[3], minus[2], minus[1], minus[0]) - weno_rest(*plus)
    biased = 5.0 * (bend + (aq[1] + aq[3]) - (aq[2] + aq[2]) + rest)
    return 30.0 * both + jnp.where(upwind, biased, central)


def lanes(number):
    return pl.ds(pl.multiple_of(number * LANES, LANES), LANES)


def wall_kernel(low, state_ref, mask_ref, base_ref, out_ref, q_s, f_s, speed_s, dq_s, df_s):
    rows_y = state_ref.shape[2]
    width = state_ref.shape[3]
    tiles = rows_y // ROWS
    end = ROWS + rows_y
    zero = jnp.zeros((5, ROWS, LANES), jnp.float32)
    for side in (dq_s, df_s):
        side[:, 0:ROWS, :] = zero
        side[:, end : end + ROWS, :] = zero
    row = lax.broadcasted_iota(jnp.int32, (ROWS, LANES), 0)

    def column(number, carry):
        plane = number // (width // LANES)
        lane = lanes(number % (width // LANES))
        zero_row = jnp.minimum(number, 0)

        def at(r, shift):
            return pl.ds(zero_row + (r * ROWS + ROWS + shift), ROWS)

        def still(r):
            return slice(r * ROWS + ROWS, r * ROWS + 2 * ROWS)

        qs = []
        for r in range(tiles):
            mine = slice(r * ROWS, r * ROWS + ROWS)
            q = [state_ref[k, low + plane, mine, lane] for k in range(5)]
            flux, pressure, thin, along = flux_of(q, 1)
            speed = speed_of(pressure, thin, along)
            for k in range(5):
                q_s[k, still(r), :] = q[k]
                f_s[k, still(r), :] = flux[k]
            speed_s[still(r), :] = speed
            if r == 0:
                for k in range(5):
                    q_s[k, 0:ROWS, :] = jnp.broadcast_to(q[k][0:1], (ROWS, LANES))
                    f_s[k, 0:ROWS, :] = jnp.broadcast_to(flux[k][0:1], (ROWS, LANES))
                speed_s[0:ROWS, :] = jnp.broadcast_to(speed[0:1], (ROWS, LANES))
            if r == tiles - 1:
                speed_s[end : end + ROWS, :] = jnp.broadcast_to(
                    speed[ROWS - 1 : ROWS], (ROWS, LANES)
                )
        for k in range(5):
            changes = [
                (
                    q_s[k, still(r), :] - q_s[k, at(r, -1), :],
                    f_s[k, still(r), :] - f_s[k, at(r, -1), :],
                )
                for r in range(tiles)
            ]
            for r in range(tiles):
                dq_s[k, still(r), :] = changes[r][0]
                df_s[k, still(r), :] = changes[r][1]
        alphas, switches = [], []
        for r in range(tiles):
            alpha = speed_s[still(r), :]
            for shift in (-3, -2, -1, 1, 2):
                alpha = jnp.maximum(alpha, speed_s[at(r, shift), :])
            alphas.append(alpha)
            switches.append(mask_ref[low + plane, r * ROWS : r * ROWS + ROWS, lane] > 0)
        for k in range(5):
            hats = []
            for r in range(tiles):
                dq = [dq_s[k, at(r, s), :] for s in (-2, -1)]
                df = [df_s[k, at(r, s), :] for s in (-2, -1)]
                dq += [dq_s[k, still(r), :]]
                df += [df_s[k, still(r), :]]
                dq += [dq_s[k, at(r, s), :] for s in (1, 2)]
                df += [df_s[k, at(r, s), :] for s in (1, 2)]
                here = f_s[k, still(r), :]
                both = here + here - df[2]
                hats.append(face_value(dq, df, both, alphas[r], switches[r]))
            top = (
                60.0 * f_s[k, end - 1 : end, :]
                + 7.0 * df_s[k, end - 1 : end, :]
                - df_s[k, end - 2 : end - 1, :]
            )
            turned = [pltpu.roll(hat, ROWS - 1, 0) for hat in hats]
            turned.append(jnp.broadcast_to(top, (ROWS, LANES)))
            for r in range(tiles):
                after = jnp.where(row == ROWS - 1, turned[r + 1], turned[r])
                mine = slice(r * ROWS, r * ROWS + ROWS)
                out_ref[k, plane, mine, lane] = base_ref[k, low + plane, mine, lane] + FACE_SCALE * (
                    after - hats[r]
                )
        return carry

    lax.fori_loop(0, out_ref.shape[1] * (width // LANES), column, 0)


def wall_part(state, mask_y, base, low, count, after):
    fields, depth, rows_y, width = state.shape
    tall = rows_y + 2 * ROWS
    padded = pltpu.VMEM((fields, tall, LANES), jnp.float32)

    def kernel(state_ref, mask_ref, base_ref, after_ref, out_ref, *scratch):
        wall_kernel(low, state_ref, mask_ref, base_ref, out_ref, *scratch)

    return call(
        kernel,
        "wall_faces",
        5.0 * count / depth,
        [PLACE, PLACE, PLACE, ANYWHERE],
        PLACE,
        shape_of(fields, count, rows_y, width),
        [padded, padded, pltpu.VMEM((tall, LANES), jnp.float32), padded, padded],
    )(state, mask_y, base, after)


def pack_kernel(parts, state_ref, mask_ref, *refs):
    outs = refs[: len(parts)]
    mask_s, float_s, sems, mask_sems = refs[len(parts) :]
    planes = state_ref.shape[0]
    mask_copy = pltpu.make_async_copy(mask_ref.at[0], mask_s, mask_sems.at[len(parts)])
    mask_copy.start()
    copies = [
        pltpu.make_async_copy(
            state_ref.at[:, pl.ds(row, rows), pl.ds(lane, width)],
            out.at[pl.ds(0, planes)],
            sems.at[c],
        )
        for c, ((row, rows, lane, width), out) in enumerate(zip(parts, outs))
    ]
    for copy in copies:
        copy.start()
    mask_copy.wait()
    float_s[...] = mask_s[...].astype(jnp.float32)
    mask_copies = [
        pltpu.make_async_copy(
            float_s.at[pl.ds(row, rows), pl.ds(lane, width)], out.at[planes], mask_sems.at[c]
        )
        for c, ((row, rows, lane, width), out) in enumerate(zip(parts, outs))
    ]
    for copy in mask_copies:
        copy.start()
    for copy in copies + mask_copies:
        copy.wait()


def pack_part(state, mask_x, parts):
    fields, depth, rows_all, width = state.shape
    planes = fields * depth
    return call(
        functools.partial(pack_kernel, parts),
        "pack_bricks",
        1.0,
        [HBM, HBM],
        [HBM] * len(parts),
        [shape_of(planes + 1, rows, lane_count) for _, rows, _, lane_count in parts],
        [
            pltpu.VMEM((rows_all, width), jnp.int32),
            pltpu.VMEM((rows_all, width), jnp.float32),
            pltpu.SemaphoreType.DMA((len(parts),)),
            pltpu.SemaphoreType.DMA((len(parts) + 1,)),
        ],
        vmem=PACK_BYTES,
    )(state.reshape(planes, rows_all, width), mask_x)


def pass_kernel(depth, pair_ref, after_ref, out_ref):
    planes = pair_ref.shape[0] - 1
    skip = 1 - lax.rem(lax.axis_index("gx"), 2)
    for k in range(planes // depth):
        for i in range(3):
            out_ref[3 * k + i] = pair_ref[depth * k + i + skip * (depth - 3)]
    out_ref[3 * (planes // depth)] = pair_ref[planes]


def pass_part(pair, depth, after):
    planes, rows_y, width = pair.shape
    return call(
        functools.partial(pass_kernel, depth),
        "pass_planes",
        0.5,
        [PLACE, ANYWHERE],
        PLACE,
        shape_of(3 * (planes - 1) // depth + 1, rows_y, width),
    )(pair, after)


def stream_kernel(part, segments, counts, *refs):
    state_ref, pair_ref, far_ref, mask_ref = refs[:4]
    sum_refs = refs[4 : 4 + len(segments)]
    acc_refs = refs[4 + len(segments) : 4 + len(segments) + len(counts)]
    out_ref, token_ref, dq_s, df_s, both_s, alpha_s, result, sem = refs[-8:]
    token_ref[...] = jnp.zeros_like(token_ref)
    fields, depth, _, _ = state_ref.shape
    start, rows_y, start_lane, width = part
    rank = lax.axis_index("gx")
    even = lax.rem(rank, 2) == 0
    first = rank == 0
    last = rank == lax.axis_size("gx") - 1
    lane_tiles = width // LANES
    faces = depth + 1
    tiles = (rows_y // ROWS) * lane_tiles

    def rows(row, shift):
        return pl.ds(pl.multiple_of(row + shift, ROWS), ROWS)

    def place(number):
        lane = (number % lane_tiles) * LANES
        return (
            (number // lane_tiles) * ROWS,
            pl.ds(pl.multiple_of(lane, LANES), LANES),
            pl.ds(pl.multiple_of(lane + start_lane, LANES), LANES),
        )

    def point(number, carry):
        at, lane, there = place(number)
        row, mine = rows(at, 0), rows(at, start)
        own = [[state_ref[k, i, mine, there] for k in range(5)] for i in range(depth)]
        cells = []
        for i in range(3):
            cells.append(
                [
                    jnp.where(
                        first,
                        own[0][k],
                        jnp.where(
                            even,
                            far_ref[3 * k + i, row, lane],
                            pair_ref[depth * k + depth - 3 + i, row, lane],
                        ),
                    )
                    for k in range(5)
                ]
            )
        cells += own
        for i in range(3):
            cells.append(
                [
                    jnp.where(
                        last,
                        own[depth - 1][k],
                        jnp.where(
                            even,
                            pair_ref[depth * k + i, row, lane],
                            far_ref[3 * k + i, row, lane],
                        ),
                    )
                    for k in range(5)
                ]
            )
        speeds, before = [], None
        for j, q in enumerate(cells):
            flux, pressure, thin, along = flux_of(q, 0)
            speeds.append(speed_of(pressure, thin, along))
            if j > 0:
                for k in range(5):
                    dq_s[number, k, j - 1] = q[k] - cells[j - 1][k]
                    df_s[number, k, j - 1] = flux[k] - before[k]
                    if 3 <= j < 3 + faces:
                        both_s[number, k, j - 3] = flux[k] + before[k]
            before = flux
        pairs = [jnp.maximum(speeds[i], speeds[i + 1]) for i in range(depth + 5)]
        for f in range(faces):
            alpha_s[number, f] = jnp.maximum(jnp.maximum(pairs[f], pairs[f + 2]), pairs[f + 4])
        return carry

    lax.fori_loop(0, tiles, point, 0)

    def faces_of(sum_ref, sum_shift, number, carry):
        at, lane, there = place(number)
        row, mine = rows(at, 0), rows(at, start)
        border = jnp.where(
            even, pair_ref[depth * fields, row, lane], far_ref[3 * fields, row, lane]
        )
        border = jnp.where(last, 0.0, border)
        switches = [mask_ref[i, mine, there] > 0 for i in range(depth)] + [border > 0.0]
        results = []
        for k in range(5):
            dq = [dq_s[number, k, j] for j in range(depth + 5)]
            df = [df_s[number, k, j] for j in range(depth + 5)]
            hats = [
                face_value(
                    dq[f : f + 5], df[f : f + 5], both_s[number, k, f], alpha_s[number, f], switches[f]
                )
                for f in range(faces)
            ]
            plane = 0
            for acc_ref, count in zip(acc_refs, counts):
                for i in range(count):
                    results.append(
                        acc_ref[k, i, mine, there]
                        - TIME_STEP * sum_ref[k, plane, rows(at, sum_shift), there]
                        + FACE_SCALE * (hats[plane + 1] - hats[plane])
                    )
                    plane += 1
        for k in range(5):
            for i in range(depth):
                result[k, i, row, lane] = results[k * depth + i]
        hand_out(number).start()
        return carry

    def hand_out(number):
        at, lane, there = place(number)
        return pltpu.make_async_copy(
            result.at[:, :, rows(at, 0), lane],
            out_ref.at[:, :, rows(at, start), there],
            sem.at[number],
        )

    def settle(number, carry):
        hand_out(number).wait()
        return carry

    for sum_ref, (low, high, sum_shift) in zip(sum_refs, segments):
        lax.fori_loop(
            low // ROWS * lane_tiles,
            high // ROWS * lane_tiles,
            functools.partial(faces_of, sum_ref, sum_shift),
            0,
        )
    lax.fori_loop(0, tiles, settle, 0)


def stream_part(state, pair, far, mask_x, part, arrived, accs, out):
    fields, depth, rows_all, _ = state.shape
    start, rows_y, _, width = part
    tiles = rows_y * width // (ROWS * LANES)
    counts = [acc.shape[1] for acc in accs]
    extra = [] if out is None else [out]
    wide = rows_all // len(arrived)
    sums, segments = [], []
    for number, array in enumerate(arrived):
        low = max(start, number * wide)
        high = min(start + rows_y, (number + 1) * wide)
        if low < high:
            sums.append(array)
            segments.append((low - start, high - start, start - number * wide))
    count = 4 + len(sums) + len(accs)

    def vregs(*dims):
        return pltpu.VMEM(dims + (ROWS, LANES), jnp.float32)

    return call(
        functools.partial(stream_kernel, part, segments, counts),
        "stream_faces",
        0.6 * tiles,
        [PLACE] * count + [HBM] * len(extra),
        [HBM, PLACE],
        [shape_of(*state.shape), shape_of(ROWS, LANES)],
        [
            vregs(tiles, fields, depth + 5),
            vregs(tiles, fields, depth + 5),
            vregs(tiles, fields, depth + 1),
            vregs(tiles, depth + 1),
            pltpu.VMEM((fields, depth, rows_y, width), jnp.float32),
            pltpu.SemaphoreType.DMA((tiles,)),
        ],
        {count: 0} if extra else None,
    )(state, pair, far, mask_x, *sums, *accs, *extra)


def circulant_tables(span):
    half = span // 2
    step = 1
    while step * step < half:
        step *= 2
    count = half // step
    places = np.arange(span)
    period = max(2 * count, LANES)
    high = 2.0 * np.pi / span * ((np.arange(count)[:, None] * step * places[None, :period]) % span)
    low = 2.0 * np.pi / span * ((np.arange(step)[:, None] * places[None]) % span)
    tables = [np.concatenate([np.cos(a), np.sin(a)]) for a in (high, low)]
    return step, count, [jnp.asarray(t.astype(np.float32)) for t in tables]


def circulant_kernel(
    count, step, filter_ref, inner_ref, outer_ref, after_ref, high_ref, low_ref, band
):
    period = inner_ref.shape[1]
    span = outer_ref.shape[1]
    tall, wide = high_ref.shape
    order = step * lax.broadcasted_iota(
        jnp.int32, (count, step), 0
    ) + lax.broadcasted_iota(jnp.int32, (count, step), 1)
    scale = 2.0 / span * (2.0 * np.pi / span) * order.astype(jnp.float32) * filter_ref[...]

    def dot(table):
        return lax.dot_general(
            scale,
            table,
            (((0,), (0,)), ((), ())),
            precision=lax.Precision.HIGHEST,
            preferred_element_type=jnp.float32,
        )

    repeat = span // period
    inner_cos = jnp.concatenate([dot(inner_ref[:count])] * repeat, 1)
    inner_sin = jnp.concatenate([dot(inner_ref[count:])] * repeat, 1)
    line = jnp.sum(
        outer_ref[step:] * inner_cos + outer_ref[:step] * inner_sin, axis=0, keepdims=True
    )
    base = jnp.broadcast_to(-line, (ROWS, span))
    place = lax.broadcasted_iota(jnp.int32, (ROWS, span), 0)
    skew = base
    for i in range(1, ROWS):
        skew = jnp.where(place == i, pltpu.roll(base, i, 1), skew)
    for b in range(LANES // ROWS):
        rows = skew if b == 0 else pltpu.roll(skew, b * ROWS, 1)
        for q in range(tall // LANES):
            at = q * LANES + b * ROWS
            first = q * LANES
            if first:
                band[at : at + ROWS, :first] = rows[:, span - first :]
            band[at : at + ROWS, first:span] = rows[:, : span - first]
    full = band[...]
    high = full.astype(jnp.bfloat16)
    low = (full - high.astype(jnp.float32)).astype(jnp.bfloat16)
    high_ref[:, :span] = high
    low_ref[:, :span] = low
    high_ref[:, span:] = high[:, : wide - span]
    low_ref[:, span:] = low[:, : wide - span]


def circulant(span_filter, span, width, after):
    tall = min(256, width)
    step, count, tables = circulant_tables(span)
    band = shape_of(tall, span + width, dtype=jnp.bfloat16)
    return call(
        functools.partial(circulant_kernel, count, step),
        "circulant_band",
        1.0,
        [PLACE, PLACE, PLACE, ANYWHERE],
        [PLACE, PLACE],
        [band, band],
        [pltpu.VMEM((tall, span), jnp.float32)],
    )(span_filter.reshape(count, step), *tables, after)


def fill_lines(shards, x_refs):
    _, depth, rows_y, width = shards[0].shape
    xh, xl = x_refs
    for number, shard in enumerate(shards):

        def plane(index, carry):
            i = index // (width // LANES)
            t = index % (width // LANES)
            flux, _, _, _ = flux_of([shard[k, i, :, lanes(t)] for k in range(5)], 2)
            to = lanes(t + number * (width // LANES))
            for k in range(5):
                high = flux[k].astype(jnp.bfloat16)
                line = pl.ds(pl.multiple_of((k * depth + i) * rows_y, rows_y), rows_y)
                xh[line, to] = high
                xl[line, to] = (flux[k] - high.astype(jnp.float32)).astype(jnp.bfloat16)
            return carry

        lax.fori_loop(0, depth * (width // LANES), plane, 0)


def product(target, sources, high_ref, low_ref, xh, xl, w_s):
    tall, wide = high_ref.shape
    width = xh.shape[1] // len(sources)
    span = wide - width
    deep = xh.shape[1]
    for number, source in enumerate(sources):
        for q in range(width // tall):
            start = lax.rem((target - source) * width - q * tall + 2 * span, span)
            start = pl.multiple_of(start, LANES)
            at = number * width + q * tall
            w_s[at : at + tall, :] = high_ref[:, pl.ds(start, width)]
            w_s[deep + at : deep + at + tall, :] = low_ref[:, pl.ds(start, width)]
    dot = functools.partial(jnp.dot, preferred_element_type=jnp.float32)
    high = w_s[:deep, :]
    return dot(xh[...], high) + dot(xl[...], high) + dot(xh[...], w_s[deep:, :])


def away_kernel(masks, parts, high_ref, low_ref, own_ref, core_ref, after_ref, *refs):
    sums = refs[: len(masks) * parts]
    xh, xl, w_s = refs[len(masks) * parts :]
    fields, depth, rows_all, width = own_ref.shape
    rows_y = rows_all // parts
    me = lax.axis_index("gz")
    fill_lines([own_ref, core_ref], [xh, xl])
    for number, mask in enumerate(masks):
        total = product(me ^ mask, [me, me ^ 1], high_ref, low_ref, xh, xl, w_s)
        total = total.reshape(fields, depth, rows_all, width)
        for c in range(parts):
            sums[number * parts + c][...] = total[:, :, c * rows_y : (c + 1) * rows_y, :]


def away_part(band, state, core, masks, parts, after):
    fields, depth, rows_all, width = state.shape
    lines = fields * depth * rows_all
    line = shape_of(lines, 2 * width, dtype=jnp.bfloat16)
    count = len(masks) * parts
    outs = call(
        functools.partial(away_kernel, masks, parts),
        "span_away",
        3.0,
        [PLACE] * 4 + [ANYWHERE],
        [PLACE] * (count + 2),
        [shape_of(fields, depth, rows_all // parts, width)] * count + [line, line],
        [pltpu.VMEM((4 * width, width), jnp.bfloat16)],
    )(*band, state, core, after)
    return outs[:count], outs[count:]


def home_kernel(high_ref, low_ref, xh, xl, state_ref, out_ref, w_s):
    me = lax.axis_index("gz")
    total = product(me, [me, me ^ 1], high_ref, low_ref, xh, xl, w_s)
    out_ref[...] = state_ref[...] - TIME_STEP * total.reshape(state_ref.shape)


def home_part(band, lines, state):
    width = state.shape[3]
    return call(
        home_kernel,
        "span_home",
        2.0,
        [PLACE] * 5,
        PLACE,
        shape_of(*state.shape),
        [pltpu.VMEM((4 * width, width), jnp.bfloat16)],
    )(*band, *lines, state)


def per_device(state, mask_x, mask_y, span_filter):
    fields, depth, rows_all, width = state.shape
    groups = lax.axis_size("gz")
    slabs = lax.axis_size("gx")
    span = width * groups

    def flip(array, bit):
        return lax.ppermute(array, "gz", [(g, g ^ bit) for g in range(groups)])

    swap = [(i, i ^ 1) for i in range(slabs)]
    carry = [(i, i + 2) for i in range(0, slabs - 2, 2)] + [
        (i, i - 2) for i in range(3, slabs, 2)
    ]
    core = flip(state, 1)
    if width % (4 * LANES) == 0:
        narrow = width // 4
        parts = [
            (0, rows_all // 2, 0, width - narrow),
            (rows_all // 2, rows_all // 2, 0, width - narrow),
            (0, rows_all, width - narrow, narrow),
        ]
    else:
        part = rows_all // 4
        parts = [(0, 2 * part, 0, width), (2 * part, part, 0, width), (3 * part, part, 0, width)]
    bricks = pack_part(state, mask_x, parts)
    pairs = [lax.ppermute(brick, "gx", swap) for brick in bricks]
    band = circulant(span_filter, span, width, core)

    masks = list(range(2, groups, 2))
    sums, lines = away_part(band, state, core, masks, SUM_PARTS, bricks[0])
    arrived = [
        sum(flip(sums[n * SUM_PARTS + c], mask) for n, mask in enumerate(masks))
        for c in range(SUM_PARTS)
    ]
    half = depth // 2

    def hand_on(c, after):
        return lax.ppermute(pass_part(pairs[c], depth, after), "gx", carry)

    def stream(c, out):
        return stream_part(
            state, pairs[c], fars[c], mask_x, parts[c], arrived, [acc_low, acc_high], out
        )

    base = home_part(band, lines, state)
    fars = [hand_on(0, base)]
    acc_low = wall_part(state, mask_y, base, 0, half, base)
    acc_high = wall_part(state, mask_y, base, half, depth - half, acc_low)
    fars.append(hand_on(1, acc_high))
    out, token = stream(0, None)
    fars.append(hand_on(2, token))
    out, _ = stream(1, out)
    out, _ = stream(2, out)
    return out


def solution(mesh):
    return jax.shard_map(
        per_device,
        mesh=mesh,
        in_specs=(P(None, "gx", None, "gz"), P("gx", None, "gz"), P("gx", None, "gz"), P()),
        out_specs=P(None, "gx", None, "gz"),
        check_vma=False,
    )
```

```python
import functools

import jax
import jax.numpy as jnp
import numpy as np
from jax import lax
from jax.experimental import pallas as pl
from jax.experimental.pallas import tpu as pltpu
from jax.sharding import PartitionSpec as P

GAMMA_GAS = 1.4
SMALL_EPS = 1e-06
TIME_STEP = 0.1
ROWS = 8
LANES = 128
SUM_PARTS = 2
VMEM_BYTES = 24 * 1024 * 1024
PACK_BYTES = 60 * 1024 * 1024
FACE_SCALE = -TIME_STEP / 60.0
PLACE = pl.BlockSpec(memory_space=pltpu.VMEM)
ANYWHERE = pl.BlockSpec(memory_space=pl.ANY)
HBM = pl.BlockSpec(memory_space=pltpu.HBM)


def call(kernel, name, weight, ins, outs, out_shape, scratch=(), aliases=None, vmem=VMEM_BYTES):
    return pl.pallas_call(
        kernel,
        out_shape=out_shape,
        in_specs=ins,
        out_specs=outs,
        scratch_shapes=list(scratch),
        input_output_aliases=aliases or {},
        compiler_params=pltpu.CompilerParams(vmem_limit_bytes=vmem),
        cost_estimate=pl.CostEstimate(
            flops=int(weight * 1e8), bytes_accessed=int(weight * 3e5), transcendentals=0
        ),
        name=name,
    )


def shape_of(*dims, dtype=jnp.float32):
    return jax.ShapeDtypeStruct(dims, dtype)


def flux_of(q, normal):
    thin = pl.reciprocal(q[0], approx=True)
    velocity = [q[1] * thin, q[2] * thin, q[3] * thin]
    pressure = (GAMMA_GAS - 1.0) * (
        q[4] - 0.5 * (q[1] * velocity[0] + q[2] * velocity[1] + q[3] * velocity[2])
    )
    along = velocity[normal]
    flux = [q[normal + 1], q[1] * along, q[2] * along, q[3] * along, (q[4] + pressure) * along]
    flux[normal + 1] = flux[normal + 1] + pressure
    return flux, pressure, thin, along


def speed_of(pressure, thin, along):
    return jnp.abs(along) + jnp.sqrt(GAMMA_GAS * pressure * thin)


def weno_rest(d1, d2, d3, d4):
    low = d2 * d2 * 0.609375 + 3.0 * SMALL_EPS
    high = d3 * d3 * 0.609375 + 3.0 * SMALL_EPS
    x0 = d1 - 1.375 * d2
    x1 = d2 - 0.625 * d3
    x2 = d4 - 1.375 * d3
    t0 = low + x0 * x0
    t1 = high + x1 * x1
    t2 = high + x2 * x2
    w0 = t1 * t2
    w1 = t0 * t2
    w2 = t0 * t1
    w0 = w0 * w0
    w1 = w1 * w1
    w2 = w2 * w2 * 1.5
    top = w0 * (x0 + (d3 - 0.625 * d2)) + w2 * (x1 + x2)
    bottom = 0.5 * w0 + 3.0 * w1 + w2
    return top * pl.reciprocal(bottom, approx=True)


def face_value(dq, df, both, alpha, upwind):
    aq = [alpha * value for value in dq]
    plus = [df[k] + aq[k] for k in range(4)]
    minus = [df[k] - aq[k] for k in range(1, 5)]
    bend = df[1] - df[3]
    central = 7.0 * bend + (df[4] - df[0])
    rest = weno_rest(minus[3], minus[2], minus[1], minus[0]) - weno_rest(*plus)
    biased = 5.0 * (bend + (aq[1] + aq[3]) - (aq[2] + aq[2]) + rest)
    return 30.0 * both + jnp.where(upwind, biased, central)


def lanes(number):
    return pl.ds(pl.multiple_of(number * LANES, LANES), LANES)


def wall_kernel(low, state_ref, mask_ref, base_ref, out_ref, q_s, f_s, speed_s, dq_s, df_s):
    rows_y = state_ref.shape[2]
    width = state_ref.shape[3]
    tiles = rows_y // ROWS
    end = ROWS + rows_y
    zero = jnp.zeros((5, ROWS, LANES), jnp.float32)
    for side in (dq_s, df_s):
        side[:, 0:ROWS, :] = zero
        side[:, end : end + ROWS, :] = zero
    row = lax.broadcasted_iota(jnp.int32, (ROWS, LANES), 0)

    def column(number, carry):
        plane = number // (width // LANES)
        lane = lanes(number % (width // LANES))
        zero_row = jnp.minimum(number, 0)

        def at(r, shift):
            return pl.ds(zero_row + (r * ROWS + ROWS + shift), ROWS)

        def still(r):
            return slice(r * ROWS + ROWS, r * ROWS + 2 * ROWS)

        qs = []
        for r in range(tiles):
            mine = slice(r * ROWS, r * ROWS + ROWS)
            q = [state_ref[k, low + plane, mine, lane] for k in range(5)]
            flux, pressure, thin, along = flux_of(q, 1)
            speed = speed_of(pressure, thin, along)
            for k in range(5):
                q_s[k, still(r), :] = q[k]
                f_s[k, still(r), :] = flux[k]
            speed_s[still(r), :] = speed
            if r == 0:
                for k in range(5):
                    q_s[k, 0:ROWS, :] = jnp.broadcast_to(q[k][0:1], (ROWS, LANES))
                    f_s[k, 0:ROWS, :] = jnp.broadcast_to(flux[k][0:1], (ROWS, LANES))
                speed_s[0:ROWS, :] = jnp.broadcast_to(speed[0:1], (ROWS, LANES))
            if r == tiles - 1:
                speed_s[end : end + ROWS, :] = jnp.broadcast_to(
                    speed[ROWS - 1 : ROWS], (ROWS, LANES)
                )
        for k in range(5):
            changes = [
                (
                    q_s[k, still(r), :] - q_s[k, at(r, -1), :],
                    f_s[k, still(r), :] - f_s[k, at(r, -1), :],
                )
                for r in range(tiles)
            ]
            for r in range(tiles):
                dq_s[k, still(r), :] = changes[r][0]
                df_s[k, still(r), :] = changes[r][1]
        alphas, switches = [], []
        for r in range(tiles):
            alpha = speed_s[still(r), :]
            for shift in (-3, -2, -1, 1, 2):
                alpha = jnp.maximum(alpha, speed_s[at(r, shift), :])
            alphas.append(alpha)
            switches.append(mask_ref[low + plane, r * ROWS : r * ROWS + ROWS, lane] > 0)
        for k in range(5):
            hats = []
            for r in range(tiles):
                dq = [dq_s[k, at(r, s), :] for s in (-2, -1)]
                df = [df_s[k, at(r, s), :] for s in (-2, -1)]
                dq += [dq_s[k, still(r), :]]
                df += [df_s[k, still(r), :]]
                dq += [dq_s[k, at(r, s), :] for s in (1, 2)]
                df += [df_s[k, at(r, s), :] for s in (1, 2)]
                here = f_s[k, still(r), :]
                both = here + here - df[2]
                hats.append(face_value(dq, df, both, alphas[r], switches[r]))
            top = (
                60.0 * f_s[k, end - 1 : end, :]
                + 7.0 * df_s[k, end - 1 : end, :]
                - df_s[k, end - 2 : end - 1, :]
            )
            turned = [pltpu.roll(hat, ROWS - 1, 0) for hat in hats]
            turned.append(jnp.broadcast_to(top, (ROWS, LANES)))
            for r in range(tiles):
                after = jnp.where(row == ROWS - 1, turned[r + 1], turned[r])
                mine = slice(r * ROWS, r * ROWS + ROWS)
                out_ref[k, plane, mine, lane] = base_ref[k, low + plane, mine, lane] + FACE_SCALE * (
                    after - hats[r]
                )
        return carry

    lax.fori_loop(0, out_ref.shape[1] * (width // LANES), column, 0)


def wall_part(state, mask_y, base, low, count, after):
    fields, depth, rows_y, width = state.shape
    tall = rows_y + 2 * ROWS
    padded = pltpu.VMEM((fields, tall, LANES), jnp.float32)

    def kernel(state_ref, mask_ref, base_ref, after_ref, out_ref, *scratch):
        wall_kernel(low, state_ref, mask_ref, base_ref, out_ref, *scratch)

    return call(
        kernel,
        "wall_faces",
        5.0 * count / depth,
        [PLACE, PLACE, PLACE, ANYWHERE],
        PLACE,
        shape_of(fields, count, rows_y, width),
        [padded, padded, pltpu.VMEM((tall, LANES), jnp.float32), padded, padded],
    )(state, mask_y, base, after)


def pack_kernel(parts, state_ref, mask_ref, *refs):
    outs = refs[: len(parts)]
    mask_s, sems = refs[len(parts) :]
    planes = state_ref.shape[0]
    mask_copy = pltpu.make_async_copy(mask_ref.at[0], mask_s, sems.at[len(parts)])
    mask_copy.start()
    copies = [
        pltpu.make_async_copy(
            state_ref.at[:, pl.ds(row, rows), pl.ds(lane, width)],
            out.at[pl.ds(0, planes)],
            sems.at[c],
        )
        for c, ((row, rows, lane, width), out) in enumerate(zip(parts, outs))
    ]
    for copy in copies:
        copy.start()
    mask_copy.wait()
    for (row, rows, lane, width), out in zip(parts, outs):
        out[planes] = mask_s[row : row + rows, lane : lane + width].astype(jnp.float32)
    for copy in copies:
        copy.wait()


def pack_part(state, mask_x, parts):
    fields, depth, rows_all, width = state.shape
    planes = fields * depth
    return call(
        functools.partial(pack_kernel, parts),
        "pack_bricks",
        1.0,
        [HBM, HBM],
        [PLACE] * len(parts),
        [shape_of(planes + 1, rows, lane_count) for _, rows, _, lane_count in parts],
        [
            pltpu.VMEM((rows_all, width), jnp.int32),
            pltpu.SemaphoreType.DMA((len(parts) + 1,)),
        ],
        vmem=PACK_BYTES,
    )(state.reshape(planes, rows_all, width), mask_x)


def pass_kernel(depth, pair_ref, after_ref, out_ref):
    planes = pair_ref.shape[0] - 1
    skip = 1 - lax.rem(lax.axis_index("gx"), 2)
    for k in range(planes // depth):
        for i in range(3):
            out_ref[3 * k + i] = pair_ref[depth * k + i + skip * (depth - 3)]
    out_ref[3 * (planes // depth)] = pair_ref[planes]


def pass_part(pair, depth, after):
    planes, rows_y, width = pair.shape
    return call(
        functools.partial(pass_kernel, depth),
        "pass_planes",
        0.5,
        [PLACE, ANYWHERE],
        PLACE,
        shape_of(3 * (planes - 1) // depth + 1, rows_y, width),
    )(pair, after)


def stream_kernel(part, segments, counts, *refs):
    state_ref, pair_ref, far_ref, mask_ref = refs[:4]
    sum_refs = refs[4 : 4 + len(segments)]
    acc_refs = refs[4 + len(segments) : 4 + len(segments) + len(counts)]
    out_ref, token_ref, dq_s, df_s, both_s, alpha_s, result, sem = refs[-8:]
    token_ref[...] = jnp.zeros_like(token_ref)
    fields, depth, _, _ = state_ref.shape
    start, rows_y, start_lane, width = part
    rank = lax.axis_index("gx")
    even = lax.rem(rank, 2) == 0
    first = rank == 0
    last = rank == lax.axis_size("gx") - 1
    lane_tiles = width // LANES
    faces = depth + 1
    tiles = (rows_y // ROWS) * lane_tiles

    def rows(row, shift):
        return pl.ds(pl.multiple_of(row + shift, ROWS), ROWS)

    def place(number):
        lane = (number % lane_tiles) * LANES
        return (
            (number // lane_tiles) * ROWS,
            pl.ds(pl.multiple_of(lane, LANES), LANES),
            pl.ds(pl.multiple_of(lane + start_lane, LANES), LANES),
        )

    def point(number, carry):
        at, lane, there = place(number)
        row, mine = rows(at, 0), rows(at, start)
        own = [[state_ref[k, i, mine, there] for k in range(5)] for i in range(depth)]
        cells = []
        for i in range(3):
            cells.append(
                [
                    jnp.where(
                        first,
                        own[0][k],
                        jnp.where(
                            even,
                            far_ref[3 * k + i, row, lane],
                            pair_ref[depth * k + depth - 3 + i, row, lane],
                        ),
                    )
                    for k in range(5)
                ]
            )
        cells += own
        for i in range(3):
            cells.append(
                [
                    jnp.where(
                        last,
                        own[depth - 1][k],
                        jnp.where(
                            even,
                            pair_ref[depth * k + i, row, lane],
                            far_ref[3 * k + i, row, lane],
                        ),
                    )
                    for k in range(5)
                ]
            )
        speeds, before = [], None
        for j, q in enumerate(cells):
            flux, pressure, thin, along = flux_of(q, 0)
            speeds.append(speed_of(pressure, thin, along))
            if j > 0:
                for k in range(5):
                    dq_s[number, k, j - 1] = q[k] - cells[j - 1][k]
                    df_s[number, k, j - 1] = flux[k] - before[k]
                    if 3 <= j < 3 + faces:
                        both_s[number, k, j - 3] = flux[k] + before[k]
            before = flux
        pairs = [jnp.maximum(speeds[i], speeds[i + 1]) for i in range(depth + 5)]
        for f in range(faces):
            alpha_s[number, f] = jnp.maximum(jnp.maximum(pairs[f], pairs[f + 2]), pairs[f + 4])
        return carry

    lax.fori_loop(0, tiles, point, 0)

    def faces_of(sum_ref, sum_shift, number, carry):
        at, lane, there = place(number)
        row, mine = rows(at, 0), rows(at, start)
        border = jnp.where(
            even, pair_ref[depth * fields, row, lane], far_ref[3 * fields, row, lane]
        )
        border = jnp.where(last, 0.0, border)
        switches = [mask_ref[i, mine, there] > 0 for i in range(depth)] + [border > 0.0]
        results = []
        for k in range(5):
            dq = [dq_s[number, k, j] for j in range(depth + 5)]
            df = [df_s[number, k, j] for j in range(depth + 5)]
            hats = [
                face_value(
                    dq[f : f + 5], df[f : f + 5], both_s[number, k, f], alpha_s[number, f], switches[f]
                )
                for f in range(faces)
            ]
            plane = 0
            for acc_ref, count in zip(acc_refs, counts):
                for i in range(count):
                    results.append(
                        acc_ref[k, i, mine, there]
                        - TIME_STEP * sum_ref[k, plane, rows(at, sum_shift), there]
                        + FACE_SCALE * (hats[plane + 1] - hats[plane])
                    )
                    plane += 1
        for k in range(5):
            for i in range(depth):
                result[k, i, row, lane] = results[k * depth + i]
        hand_out(number).start()
        return carry

    def hand_out(number):
        at, lane, there = place(number)
        return pltpu.make_async_copy(
            result.at[:, :, rows(at, 0), lane],
            out_ref.at[:, :, rows(at, start), there],
            sem.at[number],
        )

    def settle(number, carry):
        hand_out(number).wait()
        return carry

    for sum_ref, (low, high, sum_shift) in zip(sum_refs, segments):
        lax.fori_loop(
            low // ROWS * lane_tiles,
            high // ROWS * lane_tiles,
            functools.partial(faces_of, sum_ref, sum_shift),
            0,
        )
    lax.fori_loop(0, tiles, settle, 0)


def stream_part(state, pair, far, mask_x, part, arrived, accs, out):
    fields, depth, rows_all, _ = state.shape
    start, rows_y, _, width = part
    tiles = rows_y * width // (ROWS * LANES)
    counts = [acc.shape[1] for acc in accs]
    extra = [] if out is None else [out]
    wide = rows_all // len(arrived)
    sums, segments = [], []
    for number, array in enumerate(arrived):
        low = max(start, number * wide)
        high = min(start + rows_y, (number + 1) * wide)
        if low < high:
            sums.append(array)
            segments.append((low - start, high - start, start - number * wide))
    count = 4 + len(sums) + len(accs)

    def vregs(*dims):
        return pltpu.VMEM(dims + (ROWS, LANES), jnp.float32)

    return call(
        functools.partial(stream_kernel, part, segments, counts),
        "stream_faces",
        0.6 * tiles,
        [PLACE] * count + [HBM] * len(extra),
        [HBM, PLACE],
        [shape_of(*state.shape), shape_of(ROWS, LANES)],
        [
            vregs(tiles, fields, depth + 5),
            vregs(tiles, fields, depth + 5),
            vregs(tiles, fields, depth + 1),
            vregs(tiles, depth + 1),
            pltpu.VMEM((fields, depth, rows_y, width), jnp.float32),
            pltpu.SemaphoreType.DMA((tiles,)),
        ],
        {count: 0} if extra else None,
    )(state, pair, far, mask_x, *sums, *accs, *extra)


def circulant_tables(span):
    half = span // 2
    step = 1
    while step * step < half:
        step *= 2
    count = half // step
    places = np.arange(span)
    period = max(2 * count, LANES)
    high = 2.0 * np.pi / span * ((np.arange(count)[:, None] * step * places[None, :period]) % span)
    low = 2.0 * np.pi / span * ((np.arange(step)[:, None] * places[None]) % span)
    tables = [np.concatenate([np.cos(a), np.sin(a)]) for a in (high, low)]
    return step, count, [jnp.asarray(t.astype(np.float32)) for t in tables]


def circulant_kernel(
    count, step, filter_ref, inner_ref, outer_ref, after_ref, high_ref, low_ref, band
):
    period = inner_ref.shape[1]
    span = outer_ref.shape[1]
    tall, wide = high_ref.shape
    order = step * lax.broadcasted_iota(
        jnp.int32, (count, step), 0
    ) + lax.broadcasted_iota(jnp.int32, (count, step), 1)
    scale = 2.0 / span * (2.0 * np.pi / span) * order.astype(jnp.float32) * filter_ref[...]

    def dot(table):
        return lax.dot_general(
            scale,
            table,
            (((0,), (0,)), ((), ())),
            precision=lax.Precision.HIGHEST,
            preferred_element_type=jnp.float32,
        )

    repeat = span // period
    inner_cos = jnp.concatenate([dot(inner_ref[:count])] * repeat, 1)
    inner_sin = jnp.concatenate([dot(inner_ref[count:])] * repeat, 1)
    line = jnp.sum(
        outer_ref[step:] * inner_cos + outer_ref[:step] * inner_sin, axis=0, keepdims=True
    )
    base = jnp.broadcast_to(-line, (ROWS, span))
    place = lax.broadcasted_iota(jnp.int32, (ROWS, span), 0)
    skew = base
    for i in range(1, ROWS):
        skew = jnp.where(place == i, pltpu.roll(base, i, 1), skew)
    for b in range(LANES // ROWS):
        rows = skew if b == 0 else pltpu.roll(skew, b * ROWS, 1)
        for q in range(tall // LANES):
            at = q * LANES + b * ROWS
            first = q * LANES
            if first:
                band[at : at + ROWS, :first] = rows[:, span - first :]
            band[at : at + ROWS, first:span] = rows[:, : span - first]
    full = band[...]
    high = full.astype(jnp.bfloat16)
    low = (full - high.astype(jnp.float32)).astype(jnp.bfloat16)
    high_ref[:, :span] = high
    low_ref[:, :span] = low
    high_ref[:, span:] = high[:, : wide - span]
    low_ref[:, span:] = low[:, : wide - span]


def circulant(span_filter, span, width, after):
    tall = min(256, width)
    step, count, tables = circulant_tables(span)
    band = shape_of(tall, span + width, dtype=jnp.bfloat16)
    return call(
        functools.partial(circulant_kernel, count, step),
        "circulant_band",
        1.0,
        [PLACE, PLACE, PLACE, ANYWHERE],
        [PLACE, PLACE],
        [band, band],
        [pltpu.VMEM((tall, span), jnp.float32)],
    )(span_filter.reshape(count, step), *tables, after)


def fill_lines(shards, x_refs):
    _, depth, rows_y, width = shards[0].shape
    xh, xl = x_refs
    for number, shard in enumerate(shards):

        def plane(index, carry):
            i = index // (width // LANES)
            t = index % (width // LANES)
            flux, _, _, _ = flux_of([shard[k, i, :, lanes(t)] for k in range(5)], 2)
            to = lanes(t + number * (width // LANES))
            for k in range(5):
                high = flux[k].astype(jnp.bfloat16)
                line = pl.ds(pl.multiple_of((k * depth + i) * rows_y, rows_y), rows_y)
                xh[line, to] = high
                xl[line, to] = (flux[k] - high.astype(jnp.float32)).astype(jnp.bfloat16)
            return carry

        lax.fori_loop(0, depth * (width // LANES), plane, 0)


def product(target, sources, high_ref, low_ref, xh, xl, w_s):
    tall, wide = high_ref.shape
    width = xh.shape[1] // len(sources)
    span = wide - width
    deep = xh.shape[1]
    for number, source in enumerate(sources):
        for q in range(width // tall):
            start = lax.rem((target - source) * width - q * tall + 2 * span, span)
            start = pl.multiple_of(start, LANES)
            at = number * width + q * tall
            w_s[at : at + tall, :] = high_ref[:, pl.ds(start, width)]
            w_s[deep + at : deep + at + tall, :] = low_ref[:, pl.ds(start, width)]
    dot = functools.partial(jnp.dot, preferred_element_type=jnp.float32)
    high = w_s[:deep, :]
    return dot(xh[...], high) + dot(xl[...], high) + dot(xh[...], w_s[deep:, :])


def away_kernel(masks, parts, high_ref, low_ref, own_ref, core_ref, after_ref, *refs):
    sums = refs[: len(masks) * parts]
    xh, xl, w_s = refs[len(masks) * parts :]
    fields, depth, rows_all, width = own_ref.shape
    rows_y = rows_all // parts
    me = lax.axis_index("gz")
    fill_lines([own_ref, core_ref], [xh, xl])
    for number, mask in enumerate(masks):
        total = product(me ^ mask, [me, me ^ 1], high_ref, low_ref, xh, xl, w_s)
        total = total.reshape(fields, depth, rows_all, width)
        for c in range(parts):
            sums[number * parts + c][...] = total[:, :, c * rows_y : (c + 1) * rows_y, :]


def away_part(band, state, core, masks, parts, after):
    fields, depth, rows_all, width = state.shape
    lines = fields * depth * rows_all
    line = shape_of(lines, 2 * width, dtype=jnp.bfloat16)
    count = len(masks) * parts
    outs = call(
        functools.partial(away_kernel, masks, parts),
        "span_away",
        3.0,
        [PLACE] * 4 + [ANYWHERE],
        [PLACE] * (count + 2),
        [shape_of(fields, depth, rows_all // parts, width)] * count + [line, line],
        [pltpu.VMEM((4 * width, width), jnp.bfloat16)],
    )(*band, state, core, after)
    return outs[:count], outs[count:]


def home_kernel(high_ref, low_ref, xh, xl, state_ref, out_ref, w_s):
    me = lax.axis_index("gz")
    total = product(me, [me, me ^ 1], high_ref, low_ref, xh, xl, w_s)
    out_ref[...] = state_ref[...] - TIME_STEP * total.reshape(state_ref.shape)


def home_part(band, lines, state):
    width = state.shape[3]
    return call(
        home_kernel,
        "span_home",
        2.0,
        [PLACE] * 5,
        PLACE,
        shape_of(*state.shape),
        [pltpu.VMEM((4 * width, width), jnp.bfloat16)],
    )(*band, *lines, state)


def per_device(state, mask_x, mask_y, span_filter):
    fields, depth, rows_all, width = state.shape
    groups = lax.axis_size("gz")
    slabs = lax.axis_size("gx")
    span = width * groups

    def flip(array, bit):
        return lax.ppermute(array, "gz", [(g, g ^ bit) for g in range(groups)])

    swap = [(i, i ^ 1) for i in range(slabs)]
    carry = [(i, i + 2) for i in range(0, slabs - 2, 2)] + [
        (i, i - 2) for i in range(3, slabs, 2)
    ]
    core = flip(state, 1)
    if width % (4 * LANES) == 0:
        narrow = width // 4
        parts = [
            (0, rows_all // 2, 0, width - narrow),
            (rows_all // 2, rows_all // 2, 0, width - narrow),
            (0, rows_all, width - narrow, narrow),
        ]
    else:
        part = rows_all // 4
        parts = [(0, 2 * part, 0, width), (2 * part, part, 0, width), (3 * part, part, 0, width)]
    bricks = pack_part(state, mask_x, parts)
    pairs = [lax.ppermute(brick, "gx", swap) for brick in bricks]
    band = circulant(span_filter, span, width, core)

    masks = list(range(2, groups, 2))
    sums, lines = away_part(band, state, core, masks, SUM_PARTS, bricks[0])
    arrived = [
        sum(flip(sums[n * SUM_PARTS + c], mask) for n, mask in enumerate(masks))
        for c in range(SUM_PARTS)
    ]
    half = depth // 2

    def hand_on(c, after):
        return lax.ppermute(pass_part(pairs[c], depth, after), "gx", carry)

    def stream(c, out):
        return stream_part(
            state, pairs[c], fars[c], mask_x, parts[c], arrived, [acc_low, acc_high], out
        )

    base = home_part(band, lines, state)
    fars = [hand_on(0, base)]
    acc_low = wall_part(state, mask_y, base, 0, half, base)
    acc_high = wall_part(state, mask_y, base, half, depth - half, acc_low)
    fars.append(hand_on(1, acc_high))
    out, token = stream(0, None)
    fars.append(hand_on(2, token))
    out, _ = stream(1, out)
    out, _ = stream(2, out)
    return out


def solution(mesh):
    return jax.shard_map(
        per_device,
        mesh=mesh,
        in_specs=(P(None, "gx", None, "gz"), P("gx", None, "gz"), P("gx", None, "gz"), P()),
        out_specs=P(None, "gx", None, "gz"),
        check_vma=False,
    )
```

```python
import functools

import jax
import jax.numpy as jnp
import numpy as np
from jax import lax
from jax.experimental import pallas as pl
from jax.experimental.pallas import tpu as pltpu
from jax.sharding import PartitionSpec as P

GAMMA_GAS = 1.4
SMALL_EPS = 1e-06
TIME_STEP = 0.1
ROWS = 8
LANES = 128
VMEM_BYTES = 24 * 1024 * 1024
PACK_BYTES = 60 * 1024 * 1024
FACE_SCALE = -TIME_STEP / 60.0
PLACE = pl.BlockSpec(memory_space=pltpu.VMEM)
ANYWHERE = pl.BlockSpec(memory_space=pl.ANY)
HBM = pl.BlockSpec(memory_space=pltpu.HBM)


def call(kernel, name, weight, ins, outs, out_shape, scratch=(), aliases=None, vmem=VMEM_BYTES):
    return pl.pallas_call(
        kernel,
        out_shape=out_shape,
        in_specs=ins,
        out_specs=outs,
        scratch_shapes=list(scratch),
        input_output_aliases=aliases or {},
        compiler_params=pltpu.CompilerParams(vmem_limit_bytes=vmem),
        cost_estimate=pl.CostEstimate(
            flops=int(weight * 1e9), bytes_accessed=int(weight * 3e6), transcendentals=0
        ),
        name=name,
    )


def shape_of(*dims, dtype=jnp.float32):
    return jax.ShapeDtypeStruct(dims, dtype)


def flux_of(q, normal):
    thin = pl.reciprocal(q[0], approx=True)
    velocity = [q[1] * thin, q[2] * thin, q[3] * thin]
    pressure = (GAMMA_GAS - 1.0) * (
        q[4] - 0.5 * (q[1] * velocity[0] + q[2] * velocity[1] + q[3] * velocity[2])
    )
    along = velocity[normal]
    flux = [q[normal + 1], q[1] * along, q[2] * along, q[3] * along, (q[4] + pressure) * along]
    flux[normal + 1] = flux[normal + 1] + pressure
    return flux, pressure, thin, along


def speed_of(pressure, thin, along):
    return jnp.abs(along) + jnp.sqrt(GAMMA_GAS * pressure * thin)


def weno_rest(d1, d2, d3, d4):
    low = d2 * d2 * 0.609375 + 3.0 * SMALL_EPS
    high = d3 * d3 * 0.609375 + 3.0 * SMALL_EPS
    x0 = d1 - 1.375 * d2
    x1 = d2 - 0.625 * d3
    x2 = d4 - 1.375 * d3
    t0 = low + x0 * x0
    t1 = high + x1 * x1
    t2 = high + x2 * x2
    w0 = t1 * t2
    w1 = t0 * t2
    w2 = t0 * t1
    w0 = w0 * w0
    w1 = w1 * w1
    w2 = w2 * w2 * 1.5
    top = w0 * (x0 + (d3 - 0.625 * d2)) + w2 * (x1 + x2)
    bottom = 0.5 * w0 + 3.0 * w1 + w2
    return top * pl.reciprocal(bottom, approx=True)


def face_value(dq, df, both, alpha, upwind):
    aq = [alpha * value for value in dq]
    plus = [df[k] + aq[k] for k in range(4)]
    minus = [df[k] - aq[k] for k in range(1, 5)]
    bend = df[1] - df[3]
    central = 7.0 * bend + (df[4] - df[0])
    rest = weno_rest(minus[3], minus[2], minus[1], minus[0]) - weno_rest(*plus)
    biased = 5.0 * (bend + (aq[1] + aq[3]) - (aq[2] + aq[2]) + rest)
    return 30.0 * both + jnp.where(upwind, biased, central)


def lanes(number):
    return pl.ds(pl.multiple_of(number * LANES, LANES), LANES)


def wall_kernel(low, state_ref, mask_ref, base_ref, out_ref, q_s, f_s, speed_s, dq_s, df_s):
    rows_y = state_ref.shape[2]
    width = state_ref.shape[3]
    tiles = rows_y // ROWS
    end = ROWS + rows_y
    zero = jnp.zeros((5, ROWS, LANES), jnp.float32)
    for side in (dq_s, df_s):
        side[:, 0:ROWS, :] = zero
        side[:, end : end + ROWS, :] = zero
    row = lax.broadcasted_iota(jnp.int32, (ROWS, LANES), 0)

    def column(number, carry):
        plane = number // (width // LANES)
        lane = lanes(number % (width // LANES))
        zero_row = jnp.minimum(number, 0)

        def at(r, shift):
            return pl.ds(zero_row + (r * ROWS + ROWS + shift), ROWS)

        def still(r):
            return slice(r * ROWS + ROWS, r * ROWS + 2 * ROWS)

        qs = []
        for r in range(tiles):
            mine = slice(r * ROWS, r * ROWS + ROWS)
            q = [state_ref[k, low + plane, mine, lane] for k in range(5)]
            flux, pressure, thin, along = flux_of(q, 1)
            speed = speed_of(pressure, thin, along)
            for k in range(5):
                q_s[k, still(r), :] = q[k]
                f_s[k, still(r), :] = flux[k]
            speed_s[still(r), :] = speed
            if r == 0:
                for k in range(5):
                    q_s[k, 0:ROWS, :] = jnp.broadcast_to(q[k][0:1], (ROWS, LANES))
                    f_s[k, 0:ROWS, :] = jnp.broadcast_to(flux[k][0:1], (ROWS, LANES))
                speed_s[0:ROWS, :] = jnp.broadcast_to(speed[0:1], (ROWS, LANES))
            if r == tiles - 1:
                speed_s[end : end + ROWS, :] = jnp.broadcast_to(
                    speed[ROWS - 1 : ROWS], (ROWS, LANES)
                )
        for k in range(5):
            changes = [
                (
                    q_s[k, still(r), :] - q_s[k, at(r, -1), :],
                    f_s[k, still(r), :] - f_s[k, at(r, -1), :],
                )
                for r in range(tiles)
            ]
            for r in range(tiles):
                dq_s[k, still(r), :] = changes[r][0]
                df_s[k, still(r), :] = changes[r][1]
        alphas, switches = [], []
        for r in range(tiles):
            alpha = speed_s[still(r), :]
            for shift in (-3, -2, -1, 1, 2):
                alpha = jnp.maximum(alpha, speed_s[at(r, shift), :])
            alphas.append(alpha)
            switches.append(mask_ref[low + plane, r * ROWS : r * ROWS + ROWS, lane] > 0)
        for k in range(5):
            hats = []
            for r in range(tiles):
                dq = [dq_s[k, at(r, s), :] for s in (-2, -1)]
                df = [df_s[k, at(r, s), :] for s in (-2, -1)]
                dq += [dq_s[k, still(r), :]]
                df += [df_s[k, still(r), :]]
                dq += [dq_s[k, at(r, s), :] for s in (1, 2)]
                df += [df_s[k, at(r, s), :] for s in (1, 2)]
                here = f_s[k, still(r), :]
                both = here + here - df[2]
                hats.append(face_value(dq, df, both, alphas[r], switches[r]))
            top = (
                60.0 * f_s[k, end - 1 : end, :]
                + 7.0 * df_s[k, end - 1 : end, :]
                - df_s[k, end - 2 : end - 1, :]
            )
            turned = [pltpu.roll(hat, ROWS - 1, 0) for hat in hats]
            turned.append(jnp.broadcast_to(top, (ROWS, LANES)))
            for r in range(tiles):
                after = jnp.where(row == ROWS - 1, turned[r + 1], turned[r])
                mine = slice(r * ROWS, r * ROWS + ROWS)
                out_ref[k, plane, mine, lane] = base_ref[k, low + plane, mine, lane] + FACE_SCALE * (
                    after - hats[r]
                )
        return carry

    lax.fori_loop(0, out_ref.shape[1] * (width // LANES), column, 0)


def wall_part(state, mask_y, base, low, count, after):
    fields, depth, rows_y, width = state.shape
    tall = rows_y + 2 * ROWS
    padded = pltpu.VMEM((fields, tall, LANES), jnp.float32)

    def kernel(state_ref, mask_ref, base_ref, after_ref, out_ref, *scratch):
        wall_kernel(low, state_ref, mask_ref, base_ref, out_ref, *scratch)

    return call(
        kernel,
        "wall_faces",
        5.0 * count / depth,
        [PLACE, PLACE, PLACE, ANYWHERE],
        PLACE,
        shape_of(fields, count, rows_y, width),
        [padded, padded, pltpu.VMEM((tall, LANES), jnp.float32), padded, padded],
    )(state, mask_y, base, after)


def pack_kernel(parts, state_ref, mask_ref, *refs):
    outs = refs[: len(parts)]
    mask_s, sems = refs[len(parts) :]
    planes = state_ref.shape[0]
    mask_copy = pltpu.make_async_copy(mask_ref.at[0], mask_s, sems.at[len(parts)])
    mask_copy.start()
    copies = [
        pltpu.make_async_copy(
            state_ref.at[:, pl.ds(row, rows), pl.ds(lane, width)],
            out.at[pl.ds(0, planes)],
            sems.at[c],
        )
        for c, ((row, rows, lane, width), out) in enumerate(zip(parts, outs))
    ]
    for copy in copies:
        copy.start()
    mask_copy.wait()
    for (row, rows, lane, width), out in zip(parts, outs):
        out[planes] = mask_s[row : row + rows, lane : lane + width].astype(jnp.float32)
    for copy in copies:
        copy.wait()


def pack_part(state, mask_x, parts):
    fields, depth, rows_all, width = state.shape
    planes = fields * depth
    return call(
        functools.partial(pack_kernel, parts),
        "pack_bricks",
        1.0,
        [HBM, HBM],
        [PLACE] * len(parts),
        [shape_of(planes + 1, rows, lane_count) for _, rows, _, lane_count in parts],
        [
            pltpu.VMEM((rows_all, width), jnp.int32),
            pltpu.SemaphoreType.DMA((len(parts) + 1,)),
        ],
        vmem=PACK_BYTES,
    )(state.reshape(planes, rows_all, width), mask_x)


def bring_kernel(part, pieces, state_ref, mask_ref, after_ref, *outs):
    row, rows, lane, width = part
    fields, depth, _, _ = state_ref.shape
    odd = lax.rem(lax.axis_index("gx"), 2)
    for piece, out in zip(pieces, outs):
        count = depth if piece == "all" else 3
        skip = {"all": 0, "pair": 1 - odd, "across": odd}[piece] * (depth - 3)
        for k in range(fields):
            for i in range(count):
                out[count * k + i] = state_ref[k, i + skip, row : row + rows, lane : lane + width]
        switches = mask_ref[0, row : row + rows, lane : lane + width]
        out[count * fields] = switches.astype(jnp.float32)


def bring_part(state, mask_x, part, pieces, after):
    fields, depth, _, _ = state.shape
    _, rows, _, width = part
    return call(
        functools.partial(bring_kernel, part, pieces),
        "bring_planes",
        0.5,
        [PLACE, PLACE, ANYWHERE],
        [PLACE] * len(pieces),
        [
            shape_of((depth if piece == "all" else 3) * fields + 1, rows, width)
            for piece in pieces
        ],
    )(state, mask_x, after)


def pass_kernel(depth, pair_ref, after_ref, out_ref):
    planes = pair_ref.shape[0] - 1
    skip = 1 - lax.rem(lax.axis_index("gx"), 2)
    for k in range(planes // depth):
        for i in range(3):
            out_ref[3 * k + i] = pair_ref[depth * k + i + skip * (depth - 3)]
    out_ref[3 * (planes // depth)] = pair_ref[planes]


def pass_part(pair, depth, after):
    planes, rows_y, width = pair.shape
    return call(
        functools.partial(pass_kernel, depth),
        "pass_planes",
        0.5,
        [PLACE, ANYWHERE],
        PLACE,
        shape_of(3 * (planes - 1) // depth + 1, rows_y, width),
    )(pair, after)


def stream_kernel(part, others, counts, *refs):
    state_ref, pair_ref, far_ref, mask_ref = refs[:4]
    acc_refs, refs = refs[4 : 4 + len(counts)], refs[4 + len(counts) :]
    if others is None:
        _, out_ref, dq_s, df_s, both_s, alpha_s = refs
        result = out_ref
    else:
        sum_ref, other_refs, refs = refs[0], refs[1 : 1 + len(others)], refs[1 + len(others) :]
        out_ref, dq_s, df_s, both_s, alpha_s, result, sem, other_sem = refs[:8]
        staged = refs[8:]
    fields, depth, _, _ = state_ref.shape
    start, rows_y, start_lane, width = part
    stride = (pair_ref.shape[0] - 1) // fields
    rank = lax.axis_index("gx")
    even = lax.rem(rank, 2) == 0
    first = rank == 0
    last = rank == lax.axis_size("gx") - 1
    lane_tiles = width // LANES
    faces = depth + 1
    tiles = (rows_y // ROWS) * lane_tiles

    def rows(row, shift):
        return pl.ds(pl.multiple_of(row + shift, ROWS), ROWS)

    def place(number):
        lane = (number % lane_tiles) * LANES
        return (
            (number // lane_tiles) * ROWS,
            pl.ds(pl.multiple_of(lane, LANES), LANES),
            pl.ds(pl.multiple_of(lane + start_lane, LANES), LANES),
        )

    def point(number, carry):
        at, lane, there = place(number)
        row, mine = rows(at, 0), rows(at, start)
        own = [[state_ref[k, i, mine, there] for k in range(5)] for i in range(depth)]
        cells = []
        for i in range(3):
            cells.append(
                [
                    jnp.where(
                        first,
                        own[0][k],
                        jnp.where(
                            even,
                            far_ref[3 * k + i, row, lane],
                            pair_ref[stride * k + stride - 3 + i, row, lane],
                        ),
                    )
                    for k in range(5)
                ]
            )
        cells += own
        for i in range(3):
            cells.append(
                [
                    jnp.where(
                        last,
                        own[depth - 1][k],
                        jnp.where(
                            even,
                            pair_ref[stride * k + i, row, lane],
                            far_ref[3 * k + i, row, lane],
                        ),
                    )
                    for k in range(5)
                ]
            )
        speeds, before = [], None
        for j, q in enumerate(cells):
            flux, pressure, thin, along = flux_of(q, 0)
            speeds.append(speed_of(pressure, thin, along))
            if j > 0:
                for k in range(5):
                    dq_s[number, k, j - 1] = q[k] - cells[j - 1][k]
                    df_s[number, k, j - 1] = flux[k] - before[k]
                    if 3 <= j < 3 + faces:
                        both_s[number, k, j - 3] = flux[k] + before[k]
            before = flux
        pairs = [jnp.maximum(speeds[i], speeds[i + 1]) for i in range(depth + 5)]
        for f in range(faces):
            alpha_s[number, f] = jnp.maximum(jnp.maximum(pairs[f], pairs[f + 2]), pairs[f + 4])
        return carry

    lax.fori_loop(0, tiles, point, 0)

    def faces_of(number, carry):
        at, lane, there = place(number)
        row, mine = rows(at, 0), rows(at, start)
        border = jnp.where(
            even, pair_ref[stride * fields, row, lane], far_ref[3 * fields, row, lane]
        )
        border = jnp.where(last, 0.0, border)
        switches = [mask_ref[i, mine, there] > 0 for i in range(depth)] + [border > 0.0]
        results = []
        for k in range(5):
            dq = [dq_s[number, k, j] for j in range(depth + 5)]
            df = [df_s[number, k, j] for j in range(depth + 5)]
            hats = [
                face_value(
                    dq[f : f + 5], df[f : f + 5], both_s[number, k, f], alpha_s[number, f], switches[f]
                )
                for f in range(faces)
            ]
            plane = 0
            for acc_ref, count in zip(acc_refs, counts):
                for i in range(count):
                    value = acc_ref[k, i, mine, there] + FACE_SCALE * (hats[plane + 1] - hats[plane])
                    if others is not None:
                        value = value - TIME_STEP * sum_ref[k, plane, mine, there]
                    results.append(value)
                    plane += 1
        for k in range(5):
            for i in range(depth):
                result[k, i, row, lane] = results[k * depth + i]
        if others is not None:
            hand_out(number).start()
        return carry

    def hand_out(number):
        at, lane, there = place(number)
        return pltpu.make_async_copy(
            result.at[:, :, rows(at, 0), lane],
            out_ref.at[:, :, rows(at, start), there],
            sem.at[number],
        )

    def settle(number, carry):
        hand_out(number).wait()
        return carry

    copies = []
    for number, other in enumerate(others or []):
        top, tall, left, wide = other

        def line(index, carry, number=number, top=top, tall=tall, left=left, wide=wide):
            k, i = index // depth, index % depth
            staged[number][k, i] = other_refs[number][k, i] - TIME_STEP * (
                sum_ref[k, i, top : top + tall, left : left + wide]
            )
            return carry

        lax.fori_loop(0, fields * depth, line, 0)
        copy = pltpu.make_async_copy(
            staged[number],
            out_ref.at[:, :, pl.ds(top, tall), pl.ds(left, wide)],
            other_sem.at[number],
        )
        copy.start()
        copies.append(copy)
    lax.fori_loop(0, tiles, faces_of, 0)
    if others is not None:
        lax.fori_loop(0, tiles, settle, 0)
    for copy in copies:
        copy.wait()


def stream_part(state, pair, far, mask_x, part, accs, after=None, arrived=None, others=None):
    fields, depth, _, _ = state.shape
    _, rows_y, _, width = part
    tiles = rows_y * width // (ROWS * LANES)
    counts = [acc.shape[1] for acc in accs]

    def vregs(*dims):
        return pltpu.VMEM(dims + (ROWS, LANES), jnp.float32)

    def cells(part):
        return (fields, depth, part[1], part[3])

    scratch = [
        vregs(tiles, fields, depth + 5),
        vregs(tiles, fields, depth + 5),
        vregs(tiles, fields, depth + 1),
        vregs(tiles, depth + 1),
    ]
    inputs = [state, pair, far, mask_x, *accs]
    places_in = [PLACE] * len(inputs)
    if others is None:
        inputs.append(after)
        places_in.append(ANYWHERE)
        places = None
        target, target_shape = PLACE, shape_of(*cells(part))
    else:
        places = [place for place, _ in others]
        inputs += [arrived] + [array for _, array in others]
        places_in = [PLACE] * len(inputs)
        target, target_shape = HBM, shape_of(*state.shape)
        scratch += [
            pltpu.VMEM(cells(part), jnp.float32),
            pltpu.SemaphoreType.DMA((tiles,)),
            pltpu.SemaphoreType.DMA((len(others),)),
        ] + [pltpu.VMEM(cells(place), jnp.float32) for place in places]
    return call(
        functools.partial(stream_kernel, part, places, counts),
        "stream_faces",
        0.6 * tiles,
        places_in,
        target,
        target_shape,
        scratch,
    )(*inputs)


def circulant_tables(span):
    half = span // 2
    step = 1
    while step * step < half:
        step *= 2
    count = half // step
    places = np.arange(span)
    period = max(2 * count, LANES)
    high = 2.0 * np.pi / span * ((np.arange(count)[:, None] * step * places[None, :period]) % span)
    low = 2.0 * np.pi / span * ((np.arange(step)[:, None] * places[None]) % span)
    tables = [np.concatenate([np.cos(a), np.sin(a)]) for a in (high, low)]
    return step, count, [jnp.asarray(t.astype(np.float32)) for t in tables]


def circulant_kernel(
    count, step, filter_ref, inner_ref, outer_ref, after_ref, high_ref, low_ref, band
):
    period = inner_ref.shape[1]
    span = outer_ref.shape[1]
    tall, wide = high_ref.shape
    order = step * lax.broadcasted_iota(
        jnp.int32, (count, step), 0
    ) + lax.broadcasted_iota(jnp.int32, (count, step), 1)
    scale = 2.0 / span * (2.0 * np.pi / span) * order.astype(jnp.float32) * filter_ref[...]

    def dot(table):
        return lax.dot_general(
            scale,
            table,
            (((0,), (0,)), ((), ())),
            precision=lax.Precision.HIGHEST,
            preferred_element_type=jnp.float32,
        )

    repeat = span // period
    inner_cos = jnp.concatenate([dot(inner_ref[:count])] * repeat, 1)
    inner_sin = jnp.concatenate([dot(inner_ref[count:])] * repeat, 1)
    line = jnp.sum(
        outer_ref[step:] * inner_cos + outer_ref[:step] * inner_sin, axis=0, keepdims=True
    )
    base = jnp.broadcast_to(-line, (ROWS, span))
    place = lax.broadcasted_iota(jnp.int32, (ROWS, span), 0)
    skew = base
    for i in range(1, ROWS):
        skew = jnp.where(place == i, pltpu.roll(base, i, 1), skew)
    for b in range(LANES // ROWS):
        rows = skew if b == 0 else pltpu.roll(skew, b * ROWS, 1)
        for q in range(tall // LANES):
            at = q * LANES + b * ROWS
            first = q * LANES
            if first:
                band[at : at + ROWS, :first] = rows[:, span - first :]
            band[at : at + ROWS, first:span] = rows[:, : span - first]
    full = band[...]
    high = full.astype(jnp.bfloat16)
    low = (full - high.astype(jnp.float32)).astype(jnp.bfloat16)
    high_ref[:, :span] = high
    low_ref[:, :span] = low
    high_ref[:, span:] = high[:, : wide - span]
    low_ref[:, span:] = low[:, : wide - span]


def circulant(span_filter, span, width, after):
    tall = min(256, width)
    step, count, tables = circulant_tables(span)
    band = shape_of(tall, span + width, dtype=jnp.bfloat16)
    return call(
        functools.partial(circulant_kernel, count, step),
        "circulant_band",
        1.0,
        [PLACE, PLACE, PLACE, ANYWHERE],
        [PLACE, PLACE],
        [band, band],
        [pltpu.VMEM((tall, span), jnp.float32)],
    )(span_filter.reshape(count, step), *tables, after)


def fill_lines(shards, x_refs):
    _, depth, rows_y, width = shards[0].shape
    xh, xl = x_refs
    for number, shard in enumerate(shards):

        def plane(index, carry):
            i = index // (width // LANES)
            t = index % (width // LANES)
            flux, _, _, _ = flux_of([shard[k, i, :, lanes(t)] for k in range(5)], 2)
            to = lanes(t + number * (width // LANES))
            for k in range(5):
                high = flux[k].astype(jnp.bfloat16)
                line = pl.ds(pl.multiple_of((k * depth + i) * rows_y, rows_y), rows_y)
                xh[line, to] = high
                xl[line, to] = (flux[k] - high.astype(jnp.float32)).astype(jnp.bfloat16)
            return carry

        lax.fori_loop(0, depth * (width // LANES), plane, 0)


def product(target, sources, high_ref, low_ref, xh, xl, w_s):
    tall, wide = high_ref.shape
    width = xh.shape[1] // len(sources)
    span = wide - width
    deep = xh.shape[1]
    for number, source in enumerate(sources):
        for q in range(width // tall):
            start = lax.rem((target - source) * width - q * tall + 2 * span, span)
            start = pl.multiple_of(start, LANES)
            at = number * width + q * tall
            w_s[at : at + tall, :] = high_ref[:, pl.ds(start, width)]
            w_s[deep + at : deep + at + tall, :] = low_ref[:, pl.ds(start, width)]
    dot = functools.partial(jnp.dot, preferred_element_type=jnp.float32)
    high = w_s[:deep, :]
    return dot(xh[...], high) + dot(xl[...], high) + dot(xh[...], w_s[deep:, :])


def away_kernel(masks, high_ref, low_ref, own_ref, core_ref, *refs):
    sums = refs[: len(masks)]
    xh, xl, w_s = refs[len(masks) :]
    me = lax.axis_index("gz")
    fill_lines([own_ref, core_ref], [xh, xl])
    for mask, sum_ref in zip(masks, sums):
        total = product(me ^ mask, [me, me ^ 1], high_ref, low_ref, xh, xl, w_s)
        sum_ref[...] = total.reshape(own_ref.shape)


def away_part(band, state, core, masks):
    fields, depth, rows_all, width = state.shape
    line = shape_of(fields * depth * rows_all, 2 * width, dtype=jnp.bfloat16)
    outs = call(
        functools.partial(away_kernel, masks),
        "span_away",
        3.0,
        [PLACE] * 4,
        [PLACE] * (len(masks) + 2),
        [shape_of(*state.shape)] * len(masks) + [line, line],
        [pltpu.VMEM((4 * width, width), jnp.bfloat16)],
    )(*band, state, core)
    return outs[: len(masks)], outs[len(masks) :]


def home_kernel(high_ref, low_ref, xh, xl, state_ref, out_ref, w_s):
    me = lax.axis_index("gz")
    total = product(me, [me, me ^ 1], high_ref, low_ref, xh, xl, w_s)
    out_ref[...] = state_ref[...] - TIME_STEP * total.reshape(state_ref.shape)


def home_part(band, lines, state):
    width = state.shape[3]
    return call(
        home_kernel,
        "span_home",
        2.0,
        [PLACE] * 5,
        PLACE,
        shape_of(*state.shape),
        [pltpu.VMEM((4 * width, width), jnp.bfloat16)],
    )(*band, *lines, state)


def per_device(state, mask_x, mask_y, span_filter):
    fields, depth, rows_all, width = state.shape
    groups = lax.axis_size("gz")
    slabs = lax.axis_size("gx")
    span = width * groups

    def flip(array, bit):
        return lax.ppermute(array, "gz", [(g, g ^ bit) for g in range(groups)])

    swap = [(i, i ^ 1) for i in range(slabs)]
    carry = [(i, i + 2) for i in range(0, slabs - 2, 2)] + [
        (i, i - 2) for i in range(3, slabs, 2)
    ]
    core = flip(state, 1)
    if width % (4 * LANES) == 0:
        narrow = width // 4
        parts = [
            (0, rows_all // 2, 0, width - narrow),
            (rows_all // 2, rows_all // 2, 0, width - narrow),
            (0, rows_all, width - narrow, narrow),
        ]
    else:
        part = rows_all // 4
        parts = [(0, 2 * part, 0, width), (2 * part, part, 0, width), (3 * part, part, 0, width)]
    across = [(i, i + 1) for i in range(1, slabs - 1, 2)]
    across += [(target, source) for source, target in across]

    (brick,) = pack_part(state, mask_x, parts[:1])
    pairs = [lax.ppermute(brick, "gx", swap)]
    band = circulant(span_filter, span, width, core)

    masks = list(range(2, groups, 2))
    sums, lines = away_part(band, state, core, masks)
    arrived = sum(flip(part_sum, mask) for part_sum, mask in zip(sums, masks))
    half = depth // 2
    (brick,) = bring_part(state, mask_x, parts[1], ["all"], lines[0])
    pairs.append(lax.ppermute(brick, "gx", swap))
    base = home_part(band, lines, state)
    inner, outer = bring_part(state, mask_x, parts[2], ["pair", "across"], base)
    pairs.append(lax.ppermute(inner, "gx", swap))
    last = lax.ppermute(outer, "gx", across)

    planes = pass_part(pairs[0], depth, inner)
    fars = [lax.ppermute(planes, "gx", carry)]
    acc_low = wall_part(state, mask_y, base, 0, half, planes)
    planes = pass_part(pairs[1], depth, acc_low)
    fars += [lax.ppermute(planes, "gx", carry), last]
    acc_high = wall_part(state, mask_y, base, half, depth - half, planes)

    accs = [acc_low, acc_high]
    ready, after = [], acc_high
    for c in (0, 2):
        after = stream_part(state, pairs[c], fars[c], mask_x, parts[c], accs, after)
        ready.append((parts[c], after))
    return stream_part(
        state, pairs[1], fars[1], mask_x, parts[1], accs, arrived=arrived, others=ready
    )


def solution(mesh):
    return jax.shard_map(
        per_device,
        mesh=mesh,
        in_specs=(P(None, "gx", None, "gz"), P("gx", None, "gz"), P("gx", None, "gz"), P()),
        out_specs=P(None, "gx", None, "gz"),
        check_vma=False,
    )
```

```python
import functools

import jax
import jax.numpy as jnp
import numpy as np
from jax import lax
from jax.experimental import pallas as pl
from jax.experimental.pallas import tpu as pltpu
from jax.sharding import PartitionSpec as P

GAMMA_GAS = 1.4
SMALL_EPS = 1e-06
TIME_STEP = 0.1
ROWS = 8
LANES = 128
VMEM_BYTES = 24 * 1024 * 1024
PACK_BYTES = 60 * 1024 * 1024
FACE_SCALE = -TIME_STEP / 60.0
PLACE = pl.BlockSpec(memory_space=pltpu.VMEM)
ANYWHERE = pl.BlockSpec(memory_space=pl.ANY)
HBM = pl.BlockSpec(memory_space=pltpu.HBM)


def call(kernel, name, weight, ins, outs, out_shape, scratch=(), aliases=None, vmem=VMEM_BYTES):
    return pl.pallas_call(
        kernel,
        out_shape=out_shape,
        in_specs=ins,
        out_specs=outs,
        scratch_shapes=list(scratch),
        input_output_aliases=aliases or {},
        compiler_params=pltpu.CompilerParams(vmem_limit_bytes=vmem),
        cost_estimate=pl.CostEstimate(
            flops=int(weight * 1e9), bytes_accessed=int(weight * 3e6), transcendentals=0
        ),
        name=name,
    )


def shape_of(*dims, dtype=jnp.float32):
    return jax.ShapeDtypeStruct(dims, dtype)


def flux_of(q, normal):
    thin = pl.reciprocal(q[0], approx=True)
    velocity = [q[1] * thin, q[2] * thin, q[3] * thin]
    pressure = (GAMMA_GAS - 1.0) * (
        q[4] - 0.5 * (q[1] * velocity[0] + q[2] * velocity[1] + q[3] * velocity[2])
    )
    along = velocity[normal]
    flux = [q[normal + 1], q[1] * along, q[2] * along, q[3] * along, (q[4] + pressure) * along]
    flux[normal + 1] = flux[normal + 1] + pressure
    return flux, pressure, thin, along


def speed_of(pressure, thin, along):
    return jnp.abs(along) + jnp.sqrt(GAMMA_GAS * pressure * thin)


def weno_rest(d1, d2, d3, d4):
    low = d2 * d2 * 0.609375 + 3.0 * SMALL_EPS
    high = d3 * d3 * 0.609375 + 3.0 * SMALL_EPS
    x0 = d1 - 1.375 * d2
    x1 = d2 - 0.625 * d3
    x2 = d4 - 1.375 * d3
    t0 = low + x0 * x0
    t1 = high + x1 * x1
    t2 = high + x2 * x2
    w0 = t1 * t2
    w1 = t0 * t2
    w2 = t0 * t1
    w0 = w0 * w0
    w1 = w1 * w1
    w2 = w2 * w2 * 1.5
    top = w0 * (x0 + (d3 - 0.625 * d2)) + w2 * (x1 + x2)
    bottom = 0.5 * w0 + 3.0 * w1 + w2
    return top * pl.reciprocal(bottom, approx=True)


def face_value(dq, df, both, alpha, upwind):
    aq = [alpha * value for value in dq]
    plus = [df[k] + aq[k] for k in range(4)]
    minus = [df[k] - aq[k] for k in range(1, 5)]
    bend = df[1] - df[3]
    central = 7.0 * bend + (df[4] - df[0])
    rest = weno_rest(minus[3], minus[2], minus[1], minus[0]) - weno_rest(*plus)
    biased = 5.0 * (bend + (aq[1] + aq[3]) - (aq[2] + aq[2]) + rest)
    return 30.0 * both + jnp.where(upwind, biased, central)


def lanes(number):
    return pl.ds(pl.multiple_of(number * LANES, LANES), LANES)


def wall_kernel(low, state_ref, mask_ref, base_ref, out_ref, q_s, f_s, speed_s, dq_s, df_s):
    rows_y = state_ref.shape[2]
    width = state_ref.shape[3]
    tiles = rows_y // ROWS
    end = ROWS + rows_y
    zero = jnp.zeros((5, ROWS, LANES), jnp.float32)
    for side in (dq_s, df_s):
        side[:, 0:ROWS, :] = zero
        side[:, end : end + ROWS, :] = zero
    row = lax.broadcasted_iota(jnp.int32, (ROWS, LANES), 0)

    def column(number, carry):
        plane = number // (width // LANES)
        lane = lanes(number % (width // LANES))
        zero_row = jnp.minimum(number, 0)

        def at(r, shift):
            return pl.ds(zero_row + (r * ROWS + ROWS + shift), ROWS)

        def still(r):
            return slice(r * ROWS + ROWS, r * ROWS + 2 * ROWS)

        qs = []
        for r in range(tiles):
            mine = slice(r * ROWS, r * ROWS + ROWS)
            q = [state_ref[k, low + plane, mine, lane] for k in range(5)]
            flux, pressure, thin, along = flux_of(q, 1)
            speed = speed_of(pressure, thin, along)
            for k in range(5):
                q_s[k, still(r), :] = q[k]
                f_s[k, still(r), :] = flux[k]
            speed_s[still(r), :] = speed
            if r == 0:
                for k in range(5):
                    q_s[k, 0:ROWS, :] = jnp.broadcast_to(q[k][0:1], (ROWS, LANES))
                    f_s[k, 0:ROWS, :] = jnp.broadcast_to(flux[k][0:1], (ROWS, LANES))
                speed_s[0:ROWS, :] = jnp.broadcast_to(speed[0:1], (ROWS, LANES))
            if r == tiles - 1:
                speed_s[end : end + ROWS, :] = jnp.broadcast_to(
                    speed[ROWS - 1 : ROWS], (ROWS, LANES)
                )
        for k in range(5):
            changes = [
                (
                    q_s[k, still(r), :] - q_s[k, at(r, -1), :],
                    f_s[k, still(r), :] - f_s[k, at(r, -1), :],
                )
                for r in range(tiles)
            ]
            for r in range(tiles):
                dq_s[k, still(r), :] = changes[r][0]
                df_s[k, still(r), :] = changes[r][1]
        alphas, switches = [], []
        for r in range(tiles):
            alpha = speed_s[still(r), :]
            for shift in (-3, -2, -1, 1, 2):
                alpha = jnp.maximum(alpha, speed_s[at(r, shift), :])
            alphas.append(alpha)
            switches.append(mask_ref[low + plane, r * ROWS : r * ROWS + ROWS, lane] > 0)
        for k in range(5):
            hats = []
            for r in range(tiles):
                dq = [dq_s[k, at(r, s), :] for s in (-2, -1)]
                df = [df_s[k, at(r, s), :] for s in (-2, -1)]
                dq += [dq_s[k, still(r), :]]
                df += [df_s[k, still(r), :]]
                dq += [dq_s[k, at(r, s), :] for s in (1, 2)]
                df += [df_s[k, at(r, s), :] for s in (1, 2)]
                here = f_s[k, still(r), :]
                both = here + here - df[2]
                hats.append(face_value(dq, df, both, alphas[r], switches[r]))
            top = (
                60.0 * f_s[k, end - 1 : end, :]
                + 7.0 * df_s[k, end - 1 : end, :]
                - df_s[k, end - 2 : end - 1, :]
            )
            turned = [pltpu.roll(hat, ROWS - 1, 0) for hat in hats]
            turned.append(jnp.broadcast_to(top, (ROWS, LANES)))
            for r in range(tiles):
                after = jnp.where(row == ROWS - 1, turned[r + 1], turned[r])
                mine = slice(r * ROWS, r * ROWS + ROWS)
                out_ref[k, plane, mine, lane] = base_ref[k, low + plane, mine, lane] + FACE_SCALE * (
                    after - hats[r]
                )
        return carry

    lax.fori_loop(0, out_ref.shape[1] * (width // LANES), column, 0)


def wall_part(state, mask_y, base, low, count, after):
    fields, depth, rows_y, width = state.shape
    tall = rows_y + 2 * ROWS
    padded = pltpu.VMEM((fields, tall, LANES), jnp.float32)

    def kernel(state_ref, mask_ref, base_ref, after_ref, out_ref, *scratch):
        wall_kernel(low, state_ref, mask_ref, base_ref, out_ref, *scratch)

    return call(
        kernel,
        "wall_faces",
        5.0 * count / depth,
        [PLACE, PLACE, PLACE, ANYWHERE],
        PLACE,
        shape_of(fields, count, rows_y, width),
        [padded, padded, pltpu.VMEM((tall, LANES), jnp.float32), padded, padded],
    )(state, mask_y, base, after)


def pack_kernel(parts, state_ref, mask_ref, *refs):
    outs = refs[: len(parts)]
    mask_s, sems = refs[len(parts) :]
    planes = state_ref.shape[0]
    mask_copy = pltpu.make_async_copy(mask_ref.at[0], mask_s, sems.at[len(parts)])
    mask_copy.start()
    copies = [
        pltpu.make_async_copy(
            state_ref.at[:, pl.ds(row, rows), pl.ds(lane, width)],
            out.at[pl.ds(0, planes)],
            sems.at[c],
        )
        for c, ((row, rows, lane, width), out) in enumerate(zip(parts, outs))
    ]
    for copy in copies:
        copy.start()
    mask_copy.wait()
    for (row, rows, lane, width), out in zip(parts, outs):
        out[planes] = mask_s[row : row + rows, lane : lane + width].astype(jnp.float32)
    for copy in copies:
        copy.wait()


def pack_part(state, mask_x, parts):
    fields, depth, rows_all, width = state.shape
    planes = fields * depth
    return call(
        functools.partial(pack_kernel, parts),
        "pack_bricks",
        1.0,
        [HBM, HBM],
        [PLACE] * len(parts),
        [shape_of(planes + 1, rows, lane_count) for _, rows, _, lane_count in parts],
        [
            pltpu.VMEM((rows_all, width), jnp.int32),
            pltpu.SemaphoreType.DMA((len(parts) + 1,)),
        ],
        vmem=PACK_BYTES,
    )(state.reshape(planes, rows_all, width), mask_x)


def bring_kernel(part, pieces, state_ref, mask_ref, after_ref, *outs):
    row, rows, lane, width = part
    fields, depth, _, _ = state_ref.shape
    odd = lax.rem(lax.axis_index("gx"), 2)
    for piece, out in zip(pieces, outs):
        count = depth if piece == "all" else 3
        skip = {"all": 0, "pair": 1 - odd, "across": odd}[piece] * (depth - 3)
        for k in range(fields):
            for i in range(count):
                out[count * k + i] = state_ref[k, i + skip, row : row + rows, lane : lane + width]
        switches = mask_ref[0, row : row + rows, lane : lane + width]
        out[count * fields] = switches.astype(jnp.float32)


def bring_part(state, mask_x, part, pieces, after):
    fields, depth, _, _ = state.shape
    _, rows, _, width = part
    return call(
        functools.partial(bring_kernel, part, pieces),
        "bring_planes",
        0.5,
        [PLACE, PLACE, ANYWHERE],
        [PLACE] * len(pieces),
        [
            shape_of((depth if piece == "all" else 3) * fields + 1, rows, width)
            for piece in pieces
        ],
    )(state, mask_x, after)


def pass_kernel(depth, pair_ref, after_ref, out_ref):
    planes = pair_ref.shape[0] - 1
    skip = 1 - lax.rem(lax.axis_index("gx"), 2)
    for k in range(planes // depth):
        for i in range(3):
            out_ref[3 * k + i] = pair_ref[depth * k + i + skip * (depth - 3)]
    out_ref[3 * (planes // depth)] = pair_ref[planes]


def pass_part(pair, depth, after):
    planes, rows_y, width = pair.shape
    return call(
        functools.partial(pass_kernel, depth),
        "pass_planes",
        0.5,
        [PLACE, ANYWHERE],
        PLACE,
        shape_of(3 * (planes - 1) // depth + 1, rows_y, width),
    )(pair, after)


def stream_kernel(part, others, counts, *refs):
    state_ref, pair_ref, far_ref, mask_ref = refs[:4]
    acc_refs, refs = refs[4 : 4 + len(counts)], refs[4 + len(counts) :]
    if others is None:
        _, out_ref, dq_s, df_s, both_s, alpha_s = refs
        result = out_ref
    else:
        sum_ref, other_refs, refs = refs[0], refs[1 : 1 + len(others)], refs[1 + len(others) :]
        out_ref, dq_s, df_s, both_s, alpha_s, result, sem, other_sem = refs[:8]
        staged = refs[8:]
    fields, depth, _, _ = state_ref.shape
    start, rows_y, start_lane, width = part
    stride = (pair_ref.shape[0] - 1) // fields
    rank = lax.axis_index("gx")
    even = lax.rem(rank, 2) == 0
    first = rank == 0
    last = rank == lax.axis_size("gx") - 1
    lane_tiles = width // LANES
    faces = depth + 1
    tiles = (rows_y // ROWS) * lane_tiles

    def rows(row, shift):
        return pl.ds(pl.multiple_of(row + shift, ROWS), ROWS)

    def place(number):
        lane = (number % lane_tiles) * LANES
        return (
            (number // lane_tiles) * ROWS,
            pl.ds(pl.multiple_of(lane, LANES), LANES),
            pl.ds(pl.multiple_of(lane + start_lane, LANES), LANES),
        )

    def point(number, carry):
        at, lane, there = place(number)
        row, mine = rows(at, 0), rows(at, start)
        own = [[state_ref[k, i, mine, there] for k in range(5)] for i in range(depth)]
        cells = []
        for i in range(3):
            cells.append(
                [
                    jnp.where(
                        first,
                        own[0][k],
                        jnp.where(
                            even,
                            far_ref[3 * k + i, row, lane],
                            pair_ref[stride * k + stride - 3 + i, row, lane],
                        ),
                    )
                    for k in range(5)
                ]
            )
        cells += own
        for i in range(3):
            cells.append(
                [
                    jnp.where(
                        last,
                        own[depth - 1][k],
                        jnp.where(
                            even,
                            pair_ref[stride * k + i, row, lane],
                            far_ref[3 * k + i, row, lane],
                        ),
                    )
                    for k in range(5)
                ]
            )
        speeds, before = [], None
        for j, q in enumerate(cells):
            flux, pressure, thin, along = flux_of(q, 0)
            speeds.append(speed_of(pressure, thin, along))
            if j > 0:
                for k in range(5):
                    dq_s[number, k, j - 1] = q[k] - cells[j - 1][k]
                    df_s[number, k, j - 1] = flux[k] - before[k]
                    if 3 <= j < 3 + faces:
                        both_s[number, k, j - 3] = flux[k] + before[k]
            before = flux
        pairs = [jnp.maximum(speeds[i], speeds[i + 1]) for i in range(depth + 5)]
        for f in range(faces):
            alpha_s[number, f] = jnp.maximum(jnp.maximum(pairs[f], pairs[f + 2]), pairs[f + 4])
        return carry

    lax.fori_loop(0, tiles, point, 0)

    def faces_of(number, carry):
        at, lane, there = place(number)
        row, mine = rows(at, 0), rows(at, start)
        border = jnp.where(
            even, pair_ref[stride * fields, row, lane], far_ref[3 * fields, row, lane]
        )
        border = jnp.where(last, 0.0, border)
        switches = [mask_ref[i, mine, there] > 0 for i in range(depth)] + [border > 0.0]
        results = []
        for k in range(5):
            dq = [dq_s[number, k, j] for j in range(depth + 5)]
            df = [df_s[number, k, j] for j in range(depth + 5)]
            hats = [
                face_value(
                    dq[f : f + 5], df[f : f + 5], both_s[number, k, f], alpha_s[number, f], switches[f]
                )
                for f in range(faces)
            ]
            plane = 0
            for acc_ref, count in zip(acc_refs, counts):
                for i in range(count):
                    value = acc_ref[k, i, mine, there] + FACE_SCALE * (hats[plane + 1] - hats[plane])
                    if others is not None:
                        value = value - TIME_STEP * sum_ref[k, plane, mine, there]
                    results.append(value)
                    plane += 1
        for k in range(5):
            for i in range(depth):
                result[k, i, row, lane] = results[k * depth + i]
        if others is not None:
            hand_out(number).start()
        return carry

    def hand_out(number):
        at, lane, there = place(number)
        return pltpu.make_async_copy(
            result.at[:, :, rows(at, 0), lane],
            out_ref.at[:, :, rows(at, start), there],
            sem.at[number],
        )

    def settle(number, carry):
        hand_out(number).wait()
        return carry

    copies = []
    for number, other in enumerate(others or []):
        top, tall, left, wide = other

        def line(index, carry, number=number, top=top, tall=tall, left=left, wide=wide):
            k, i = index // depth, index % depth
            staged[number][k, i] = other_refs[number][k, i] - TIME_STEP * (
                sum_ref[k, i, top : top + tall, left : left + wide]
            )
            return carry

        lax.fori_loop(0, fields * depth, line, 0)
        copy = pltpu.make_async_copy(
            staged[number],
            out_ref.at[:, :, pl.ds(top, tall), pl.ds(left, wide)],
            other_sem.at[number],
        )
        copy.start()
        copies.append(copy)
    lax.fori_loop(0, tiles, faces_of, 0)
    if others is not None:
        lax.fori_loop(0, tiles, settle, 0)
    for copy in copies:
        copy.wait()


def stream_part(state, pair, far, mask_x, part, accs, after=None, arrived=None, others=None):
    fields, depth, _, _ = state.shape
    _, rows_y, _, width = part
    tiles = rows_y * width // (ROWS * LANES)
    counts = [acc.shape[1] for acc in accs]

    def vregs(*dims):
        return pltpu.VMEM(dims + (ROWS, LANES), jnp.float32)

    def cells(part):
        return (fields, depth, part[1], part[3])

    scratch = [
        vregs(tiles, fields, depth + 5),
        vregs(tiles, fields, depth + 5),
        vregs(tiles, fields, depth + 1),
        vregs(tiles, depth + 1),
    ]
    inputs = [state, pair, far, mask_x, *accs]
    places_in = [PLACE] * len(inputs)
    if others is None:
        inputs.append(after)
        places_in.append(ANYWHERE)
        places = None
        target, target_shape = PLACE, shape_of(*cells(part))
    else:
        places = [place for place, _ in others]
        inputs += [arrived] + [array for _, array in others]
        places_in = [PLACE] * len(inputs)
        target, target_shape = HBM, shape_of(*state.shape)
        scratch += [
            pltpu.VMEM(cells(part), jnp.float32),
            pltpu.SemaphoreType.DMA((tiles,)),
            pltpu.SemaphoreType.DMA((len(others),)),
        ] + [pltpu.VMEM(cells(place), jnp.float32) for place in places]
    return call(
        functools.partial(stream_kernel, part, places, counts),
        "stream_faces",
        0.6 * tiles,
        places_in,
        target,
        target_shape,
        scratch,
    )(*inputs)


def circulant_tables(span):
    half = span // 2
    step = 1
    while step * step < half:
        step *= 2
    count = half // step
    places = np.arange(span)
    period = max(2 * count, LANES)
    high = 2.0 * np.pi / span * ((np.arange(count)[:, None] * step * places[None, :period]) % span)
    low = 2.0 * np.pi / span * ((np.arange(step)[:, None] * places[None]) % span)
    tables = [np.concatenate([np.cos(a), np.sin(a)]) for a in (high, low)]
    return step, count, [jnp.asarray(t.astype(np.float32)) for t in tables]


def circulant_kernel(
    count, step, filter_ref, inner_ref, outer_ref, after_ref, high_ref, low_ref, band
):
    period = inner_ref.shape[1]
    span = outer_ref.shape[1]
    tall, wide = high_ref.shape
    order = step * lax.broadcasted_iota(
        jnp.int32, (count, step), 0
    ) + lax.broadcasted_iota(jnp.int32, (count, step), 1)
    scale = 2.0 / span * (2.0 * np.pi / span) * order.astype(jnp.float32) * filter_ref[...]

    def dot(table):
        return lax.dot_general(
            scale,
            table,
            (((0,), (0,)), ((), ())),
            precision=lax.Precision.HIGHEST,
            preferred_element_type=jnp.float32,
        )

    repeat = span // period
    inner_cos = jnp.concatenate([dot(inner_ref[:count])] * repeat, 1)
    inner_sin = jnp.concatenate([dot(inner_ref[count:])] * repeat, 1)
    line = jnp.sum(
        outer_ref[step:] * inner_cos + outer_ref[:step] * inner_sin, axis=0, keepdims=True
    )
    base = jnp.broadcast_to(-line, (ROWS, span))
    place = lax.broadcasted_iota(jnp.int32, (ROWS, span), 0)
    skew = base
    for i in range(1, ROWS):
        skew = jnp.where(place == i, pltpu.roll(base, i, 1), skew)
    for b in range(LANES // ROWS):
        rows = skew if b == 0 else pltpu.roll(skew, b * ROWS, 1)
        for q in range(tall // LANES):
            at = q * LANES + b * ROWS
            first = q * LANES
            if first:
                band[at : at + ROWS, :first] = rows[:, span - first :]
            band[at : at + ROWS, first:span] = rows[:, : span - first]
    full = band[...]
    high = full.astype(jnp.bfloat16)
    low = (full - high.astype(jnp.float32)).astype(jnp.bfloat16)
    high_ref[:, :span] = high
    low_ref[:, :span] = low
    high_ref[:, span:] = high[:, : wide - span]
    low_ref[:, span:] = low[:, : wide - span]


def circulant(span_filter, span, width, after):
    tall = min(256, width)
    step, count, tables = circulant_tables(span)
    band = shape_of(tall, span + width, dtype=jnp.bfloat16)
    return call(
        functools.partial(circulant_kernel, count, step),
        "circulant_band",
        1.0,
        [PLACE, PLACE, PLACE, ANYWHERE],
        [PLACE, PLACE],
        [band, band],
        [pltpu.VMEM((tall, span), jnp.float32)],
    )(span_filter.reshape(count, step), *tables, after)


def fill_lines(shards, x_refs):
    _, depth, rows_y, width = shards[0].shape
    xh, xl = x_refs
    for number, shard in enumerate(shards):

        def plane(index, carry):
            i = index // (width // LANES)
            t = index % (width // LANES)
            flux, _, _, _ = flux_of([shard[k, i, :, lanes(t)] for k in range(5)], 2)
            to = lanes(t + number * (width // LANES))
            for k in range(5):
                high = flux[k].astype(jnp.bfloat16)
                line = pl.ds(pl.multiple_of((k * depth + i) * rows_y, rows_y), rows_y)
                xh[line, to] = high
                xl[line, to] = (flux[k] - high.astype(jnp.float32)).astype(jnp.bfloat16)
            return carry

        lax.fori_loop(0, depth * (width // LANES), plane, 0)


def product(target, sources, high_ref, low_ref, xh, xl, w_s):
    tall, wide = high_ref.shape
    width = xh.shape[1] // len(sources)
    span = wide - width
    deep = xh.shape[1]
    for number, source in enumerate(sources):
        for q in range(width // tall):
            start = lax.rem((target - source) * width - q * tall + 2 * span, span)
            start = pl.multiple_of(start, LANES)
            at = number * width + q * tall
            w_s[at : at + tall, :] = high_ref[:, pl.ds(start, width)]
            w_s[deep + at : deep + at + tall, :] = low_ref[:, pl.ds(start, width)]
    dot = functools.partial(jnp.dot, preferred_element_type=jnp.float32)
    high = w_s[:deep, :]
    return dot(xh[...], high) + dot(xl[...], high) + dot(xh[...], w_s[deep:, :])


def away_kernel(masks, high_ref, low_ref, own_ref, core_ref, *refs):
    sums = refs[: len(masks)]
    xh, xl, w_s = refs[len(masks) :]
    me = lax.axis_index("gz")
    fill_lines([own_ref, core_ref], [xh, xl])
    for mask, sum_ref in zip(masks, sums):
        total = product(me ^ mask, [me, me ^ 1], high_ref, low_ref, xh, xl, w_s)
        sum_ref[...] = total.reshape(own_ref.shape)


def away_part(band, state, core, masks):
    fields, depth, rows_all, width = state.shape
    line = shape_of(fields * depth * rows_all, 2 * width, dtype=jnp.bfloat16)
    outs = call(
        functools.partial(away_kernel, masks),
        "span_away",
        3.0,
        [PLACE] * 4,
        [PLACE] * (len(masks) + 2),
        [shape_of(*state.shape)] * len(masks) + [line, line],
        [pltpu.VMEM((4 * width, width), jnp.bfloat16)],
    )(*band, state, core)
    return outs[: len(masks)], outs[len(masks) :]


def home_kernel(high_ref, low_ref, xh, xl, state_ref, out_ref, w_s):
    me = lax.axis_index("gz")
    total = product(me, [me, me ^ 1], high_ref, low_ref, xh, xl, w_s)
    out_ref[...] = state_ref[...] - TIME_STEP * total.reshape(state_ref.shape)


def home_part(band, lines, state):
    width = state.shape[3]
    return call(
        home_kernel,
        "span_home",
        2.0,
        [PLACE] * 5,
        PLACE,
        shape_of(*state.shape),
        [pltpu.VMEM((4 * width, width), jnp.bfloat16)],
    )(*band, *lines, state)


def per_device(state, mask_x, mask_y, span_filter):
    fields, depth, rows_all, width = state.shape
    groups = lax.axis_size("gz")
    slabs = lax.axis_size("gx")
    span = width * groups

    def flip(array, bit):
        return lax.ppermute(array, "gz", [(g, g ^ bit) for g in range(groups)])

    swap = [(i, i ^ 1) for i in range(slabs)]
    carry = [(i, i + 2) for i in range(0, slabs - 2, 2)] + [
        (i, i - 2) for i in range(3, slabs, 2)
    ]
    core = flip(state, 1)
    if width % (4 * LANES) == 0:
        narrow = width // 4
        parts = [
            (0, rows_all // 2, 0, width - narrow),
            (rows_all // 2, rows_all // 2, 0, width - narrow),
            (0, rows_all, width - narrow, narrow),
        ]
    else:
        part = rows_all // 4
        parts = [(0, 2 * part, 0, width), (2 * part, part, 0, width), (3 * part, part, 0, width)]
    across = [(i, i + 1) for i in range(1, slabs - 1, 2)]
    across += [(target, source) for source, target in across]

    (brick,) = pack_part(state, mask_x, parts[:1])
    pairs = [lax.ppermute(brick, "gx", swap)]
    band = circulant(span_filter, span, width, core)

    masks = list(range(2, groups, 2))
    sums, lines = away_part(band, state, core, masks)
    arrived = sum(flip(part_sum, mask) for part_sum, mask in zip(sums, masks))
    half = depth // 2
    (brick,) = bring_part(state, mask_x, parts[1], ["all"], lines[0])
    pairs.append(lax.ppermute(brick, "gx", swap))
    base = home_part(band, lines, state)
    planes = pass_part(pairs[0], depth, base)
    fars = [lax.ppermute(planes, "gx", carry)]
    acc_low = wall_part(state, mask_y, base, 0, half, planes)
    (outer,) = bring_part(state, mask_x, parts[2], ["across"], acc_low)
    last = lax.ppermute(outer, "gx", across)
    planes = pass_part(pairs[1], depth, outer)
    fars += [lax.ppermute(planes, "gx", carry), last]
    (inner,) = bring_part(state, mask_x, parts[2], ["pair"], planes)
    pairs.append(lax.ppermute(inner, "gx", swap))
    acc_high = wall_part(state, mask_y, base, half, depth - half, planes)

    accs = [acc_low, acc_high]
    ready, after = [], acc_high
    for c in (0, 2):
        after = stream_part(state, pairs[c], fars[c], mask_x, parts[c], accs, after)
        ready.append((parts[c], after))
    return stream_part(
        state, pairs[1], fars[1], mask_x, parts[1], accs, arrived=arrived, others=ready
    )


def solution(mesh):
    return jax.shard_map(
        per_device,
        mesh=mesh,
        in_specs=(P(None, "gx", None, "gz"), P("gx", None, "gz"), P("gx", None, "gz"), P()),
        out_specs=P(None, "gx", None, "gz"),
        check_vma=False,
    )
```

```python
import functools

import jax
import jax.numpy as jnp
import numpy as np
from jax import lax
from jax.experimental import pallas as pl
from jax.experimental.pallas import tpu as pltpu
from jax.sharding import PartitionSpec as P

GAMMA_GAS = 1.4
SMALL_EPS = 1e-06
TIME_STEP = 0.1
ROWS = 8
LANES = 128
VMEM_BYTES = 24 * 1024 * 1024
PACK_BYTES = 60 * 1024 * 1024
FACE_SCALE = -TIME_STEP / 60.0
PLACE = pl.BlockSpec(memory_space=pltpu.VMEM)
ANYWHERE = pl.BlockSpec(memory_space=pl.ANY)
HBM = pl.BlockSpec(memory_space=pltpu.HBM)


def call(kernel, name, weight, ins, outs, out_shape, scratch=(), aliases=None, vmem=VMEM_BYTES):
    return pl.pallas_call(
        kernel,
        out_shape=out_shape,
        in_specs=ins,
        out_specs=outs,
        scratch_shapes=list(scratch),
        input_output_aliases=aliases or {},
        compiler_params=pltpu.CompilerParams(vmem_limit_bytes=vmem),
        cost_estimate=pl.CostEstimate(
            flops=int(weight * 1e9), bytes_accessed=int(weight * 3e6), transcendentals=0
        ),
        name=name,
    )


def shape_of(*dims, dtype=jnp.float32):
    return jax.ShapeDtypeStruct(dims, dtype)


def flux_of(q, normal):
    thin = pl.reciprocal(q[0], approx=True)
    velocity = [q[1] * thin, q[2] * thin, q[3] * thin]
    pressure = (GAMMA_GAS - 1.0) * (
        q[4] - 0.5 * (q[1] * velocity[0] + q[2] * velocity[1] + q[3] * velocity[2])
    )
    along = velocity[normal]
    flux = [q[normal + 1], q[1] * along, q[2] * along, q[3] * along, (q[4] + pressure) * along]
    flux[normal + 1] = flux[normal + 1] + pressure
    return flux, pressure, thin, along


def speed_of(pressure, thin, along):
    return jnp.abs(along) + jnp.sqrt(GAMMA_GAS * pressure * thin)


def weno_rest(d1, d2, d3, d4):
    low = d2 * d2 * 0.609375 + 3.0 * SMALL_EPS
    high = d3 * d3 * 0.609375 + 3.0 * SMALL_EPS
    x0 = d1 - 1.375 * d2
    x1 = d2 - 0.625 * d3
    x2 = d4 - 1.375 * d3
    t0 = low + x0 * x0
    t1 = high + x1 * x1
    t2 = high + x2 * x2
    w0 = t1 * t2
    w1 = t0 * t2
    w2 = t0 * t1
    w0 = w0 * w0
    w1 = w1 * w1
    w2 = w2 * w2 * 1.5
    top = w0 * (x0 + (d3 - 0.625 * d2)) + w2 * (x1 + x2)
    bottom = 0.5 * w0 + 3.0 * w1 + w2
    return top * pl.reciprocal(bottom, approx=True)


def face_value(dq, df, both, alpha, upwind):
    aq = [alpha * value for value in dq]
    plus = [df[k] + aq[k] for k in range(4)]
    minus = [df[k] - aq[k] for k in range(1, 5)]
    bend = df[1] - df[3]
    central = 7.0 * bend + (df[4] - df[0])
    rest = weno_rest(minus[3], minus[2], minus[1], minus[0]) - weno_rest(*plus)
    biased = 5.0 * (bend + (aq[1] + aq[3]) - (aq[2] + aq[2]) + rest)
    return 30.0 * both + jnp.where(upwind, biased, central)


def lanes(number):
    return pl.ds(pl.multiple_of(number * LANES, LANES), LANES)


def wall_kernel(low, state_ref, mask_ref, out_ref, q_s, f_s, speed_s, dq_s, df_s):
    rows_y = state_ref.shape[2]
    width = state_ref.shape[3]
    tiles = rows_y // ROWS
    end = ROWS + rows_y
    zero = jnp.zeros((5, ROWS, LANES), jnp.float32)
    for side in (dq_s, df_s):
        side[:, 0:ROWS, :] = zero
        side[:, end : end + ROWS, :] = zero
    row = lax.broadcasted_iota(jnp.int32, (ROWS, LANES), 0)

    def column(number, carry):
        plane = number // (width // LANES)
        lane = lanes(number % (width // LANES))
        zero_row = jnp.minimum(number, 0)

        def at(r, shift):
            return pl.ds(zero_row + (r * ROWS + ROWS + shift), ROWS)

        def still(r):
            return slice(r * ROWS + ROWS, r * ROWS + 2 * ROWS)

        qs = []
        for r in range(tiles):
            mine = slice(r * ROWS, r * ROWS + ROWS)
            q = [state_ref[k, low + plane, mine, lane] for k in range(5)]
            flux, pressure, thin, along = flux_of(q, 1)
            speed = speed_of(pressure, thin, along)
            for k in range(5):
                q_s[k, still(r), :] = q[k]
                f_s[k, still(r), :] = flux[k]
            speed_s[still(r), :] = speed
            if r == 0:
                for k in range(5):
                    q_s[k, 0:ROWS, :] = jnp.broadcast_to(q[k][0:1], (ROWS, LANES))
                    f_s[k, 0:ROWS, :] = jnp.broadcast_to(flux[k][0:1], (ROWS, LANES))
                speed_s[0:ROWS, :] = jnp.broadcast_to(speed[0:1], (ROWS, LANES))
            if r == tiles - 1:
                speed_s[end : end + ROWS, :] = jnp.broadcast_to(
                    speed[ROWS - 1 : ROWS], (ROWS, LANES)
                )
        for k in range(5):
            changes = [
                (
                    q_s[k, still(r), :] - q_s[k, at(r, -1), :],
                    f_s[k, still(r), :] - f_s[k, at(r, -1), :],
                )
                for r in range(tiles)
            ]
            for r in range(tiles):
                dq_s[k, still(r), :] = changes[r][0]
                df_s[k, still(r), :] = changes[r][1]
        alphas, switches = [], []
        for r in range(tiles):
            alpha = speed_s[still(r), :]
            for shift in (-3, -2, -1, 1, 2):
                alpha = jnp.maximum(alpha, speed_s[at(r, shift), :])
            alphas.append(alpha)
            switches.append(mask_ref[low + plane, r * ROWS : r * ROWS + ROWS, lane] > 0)
        for k in range(5):
            hats = []
            for r in range(tiles):
                dq = [dq_s[k, at(r, s), :] for s in (-2, -1)]
                df = [df_s[k, at(r, s), :] for s in (-2, -1)]
                dq += [dq_s[k, still(r), :]]
                df += [df_s[k, still(r), :]]
                dq += [dq_s[k, at(r, s), :] for s in (1, 2)]
                df += [df_s[k, at(r, s), :] for s in (1, 2)]
                here = f_s[k, still(r), :]
                both = here + here - df[2]
                hats.append(face_value(dq, df, both, alphas[r], switches[r]))
            top = (
                60.0 * f_s[k, end - 1 : end, :]
                + 7.0 * df_s[k, end - 1 : end, :]
                - df_s[k, end - 2 : end - 1, :]
            )
            turned = [pltpu.roll(hat, ROWS - 1, 0) for hat in hats]
            turned.append(jnp.broadcast_to(top, (ROWS, LANES)))
            for r in range(tiles):
                after = jnp.where(row == ROWS - 1, turned[r + 1], turned[r])
                mine = slice(r * ROWS, r * ROWS + ROWS)
                out_ref[k, plane, mine, lane] = q_s[k, still(r), :] + FACE_SCALE * (after - hats[r])
        return carry

    lax.fori_loop(0, out_ref.shape[1] * (width // LANES), column, 0)


def wall_part(state, mask_y, low, count, after):
    fields, depth, rows_y, width = state.shape
    tall = rows_y + 2 * ROWS
    padded = pltpu.VMEM((fields, tall, LANES), jnp.float32)

    def kernel(state_ref, mask_ref, after_ref, out_ref, *scratch):
        wall_kernel(low, state_ref, mask_ref, out_ref, *scratch)

    return call(
        kernel,
        "wall_faces",
        5.0 * count / depth,
        [PLACE, PLACE, ANYWHERE],
        PLACE,
        shape_of(fields, count, rows_y, width),
        [padded, padded, pltpu.VMEM((tall, LANES), jnp.float32), padded, padded],
    )(state, mask_y, after)


def pack_kernel(parts, state_ref, mask_ref, *refs):
    outs = refs[: len(parts)]
    mask_s, sems = refs[len(parts) :]
    planes = state_ref.shape[0]
    mask_copy = pltpu.make_async_copy(mask_ref.at[0], mask_s, sems.at[len(parts)])
    mask_copy.start()
    copies = [
        pltpu.make_async_copy(
            state_ref.at[:, pl.ds(row, rows), pl.ds(lane, width)],
            out.at[pl.ds(0, planes)],
            sems.at[c],
        )
        for c, ((row, rows, lane, width), out) in enumerate(zip(parts, outs))
    ]
    for copy in copies:
        copy.start()
    mask_copy.wait()
    for (row, rows, lane, width), out in zip(parts, outs):
        out[planes] = mask_s[row : row + rows, lane : lane + width].astype(jnp.float32)
    for copy in copies:
        copy.wait()


def pack_part(state, mask_x, parts):
    fields, depth, rows_all, width = state.shape
    planes = fields * depth
    return call(
        functools.partial(pack_kernel, parts),
        "pack_bricks",
        1.0,
        [HBM, HBM],
        [PLACE] * len(parts),
        [shape_of(planes + 1, rows, lane_count) for _, rows, _, lane_count in parts],
        [
            pltpu.VMEM((rows_all, width), jnp.int32),
            pltpu.SemaphoreType.DMA((len(parts) + 1,)),
        ],
        vmem=PACK_BYTES,
    )(state.reshape(planes, rows_all, width), mask_x)


def bring_kernel(part, state_ref, mask_ref, after_ref, out):
    row, rows, lane, width = part
    fields, depth, _, _ = state_ref.shape
    for k in range(fields):
        for i in range(depth):
            out[depth * k + i] = state_ref[k, i, row : row + rows, lane : lane + width]
    switches = mask_ref[0, row : row + rows, lane : lane + width]
    out[depth * fields] = switches.astype(jnp.float32)


def bring_part(state, mask_x, part, after):
    fields, depth, _, _ = state.shape
    _, rows, _, width = part
    return call(
        functools.partial(bring_kernel, part),
        "bring_planes",
        0.5,
        [PLACE, PLACE, ANYWHERE],
        PLACE,
        shape_of(depth * fields + 1, rows, width),
    )(state, mask_x, after)


def pass_kernel(depth, pair_ref, after_ref, out_ref):
    planes = pair_ref.shape[0] - 1
    skip = 1 - lax.rem(lax.axis_index("gx"), 2)
    for k in range(planes // depth):
        for i in range(3):
            out_ref[3 * k + i] = pair_ref[depth * k + i + skip * (depth - 3)]
    out_ref[3 * (planes // depth)] = pair_ref[planes]


def pass_part(pair, depth, after):
    planes, rows_y, width = pair.shape
    return call(
        functools.partial(pass_kernel, depth),
        "pass_planes",
        0.5,
        [PLACE, ANYWHERE],
        PLACE,
        shape_of(3 * (planes - 1) // depth + 1, rows_y, width),
    )(pair, after)


def stream_kernel(part, others, *refs):
    (state_ref, pair_ref, far_ref, mask_ref, base_ref), refs = refs[:5], refs[5:]
    if others is None:
        _, out_ref, dq_s, df_s, both_s, alpha_s = refs
        result = out_ref
    else:
        sum_ref, other_refs, refs = refs[0], refs[1 : 1 + len(others)], refs[1 + len(others) :]
        out_ref, dq_s, df_s, both_s, alpha_s, result, sem, other_sem = refs[:8]
        staged = refs[8:]
    fields, depth, _, _ = state_ref.shape
    start, rows_y, start_lane, width = part
    stride = depth
    rank = lax.axis_index("gx")
    even = lax.rem(rank, 2) == 0
    first = rank == 0
    last = rank == lax.axis_size("gx") - 1
    lane_tiles = width // LANES
    faces = depth + 1
    tiles = (rows_y // ROWS) * lane_tiles

    def rows(row, shift):
        return pl.ds(pl.multiple_of(row + shift, ROWS), ROWS)

    def place(number):
        lane = (number % lane_tiles) * LANES
        return (
            (number // lane_tiles) * ROWS,
            pl.ds(pl.multiple_of(lane, LANES), LANES),
            pl.ds(pl.multiple_of(lane + start_lane, LANES), LANES),
        )

    def point(number, carry):
        at, lane, there = place(number)
        row, mine = rows(at, 0), rows(at, start)
        own = [[state_ref[k, i, mine, there] for k in range(5)] for i in range(depth)]
        cells = []
        for i in range(3):
            cells.append(
                [
                    jnp.where(
                        first,
                        own[0][k],
                        jnp.where(
                            even,
                            far_ref[3 * k + i, row, lane],
                            pair_ref[stride * k + stride - 3 + i, row, lane],
                        ),
                    )
                    for k in range(5)
                ]
            )
        cells += own
        for i in range(3):
            cells.append(
                [
                    jnp.where(
                        last,
                        own[depth - 1][k],
                        jnp.where(
                            even,
                            pair_ref[stride * k + i, row, lane],
                            far_ref[3 * k + i, row, lane],
                        ),
                    )
                    for k in range(5)
                ]
            )
        speeds, before = [], None
        for j, q in enumerate(cells):
            flux, pressure, thin, along = flux_of(q, 0)
            speeds.append(speed_of(pressure, thin, along))
            if j > 0:
                for k in range(5):
                    dq_s[number, k, j - 1] = q[k] - cells[j - 1][k]
                    df_s[number, k, j - 1] = flux[k] - before[k]
                    if 3 <= j < 3 + faces:
                        both_s[number, k, j - 3] = flux[k] + before[k]
            before = flux
        pairs = [jnp.maximum(speeds[i], speeds[i + 1]) for i in range(depth + 5)]
        for f in range(faces):
            alpha_s[number, f] = jnp.maximum(jnp.maximum(pairs[f], pairs[f + 2]), pairs[f + 4])
        return carry

    lax.fori_loop(0, tiles, point, 0)

    def faces_of(number, carry):
        at, lane, there = place(number)
        row, mine = rows(at, 0), rows(at, start)
        border = jnp.where(
            even, pair_ref[stride * fields, row, lane], far_ref[3 * fields, row, lane]
        )
        border = jnp.where(last, 0.0, border)
        switches = [mask_ref[i, mine, there] > 0 for i in range(depth)] + [border > 0.0]
        results = []
        for k in range(5):
            dq = [dq_s[number, k, j] for j in range(depth + 5)]
            df = [df_s[number, k, j] for j in range(depth + 5)]
            hats = [
                face_value(
                    dq[f : f + 5], df[f : f + 5], both_s[number, k, f], alpha_s[number, f], switches[f]
                )
                for f in range(faces)
            ]
            for i in range(depth):
                value = base_ref[k, i, mine, there] + FACE_SCALE * (hats[i + 1] - hats[i])
                if others is not None:
                    value = value - TIME_STEP * sum_ref[k, i, mine, there]
                results.append(value)
        for k in range(5):
            for i in range(depth):
                result[k, i, row, lane] = results[k * depth + i]
        if others is not None:
            hand_out(number).start()
        return carry

    def hand_out(number):
        at, lane, there = place(number)
        return pltpu.make_async_copy(
            result.at[:, :, rows(at, 0), lane],
            out_ref.at[:, :, rows(at, start), there],
            sem.at[number],
        )

    def settle(number, carry):
        hand_out(number).wait()
        return carry

    copies = []
    for number, other in enumerate(others or []):
        top, tall, left, wide = other

        def line(index, carry, number=number, top=top, tall=tall, left=left, wide=wide):
            k, i = index // depth, index % depth
            staged[number][k, i] = other_refs[number][k, i] - TIME_STEP * (
                sum_ref[k, i, top : top + tall, left : left + wide]
            )
            return carry

        lax.fori_loop(0, fields * depth, line, 0)
        copy = pltpu.make_async_copy(
            staged[number],
            out_ref.at[:, :, pl.ds(top, tall), pl.ds(left, wide)],
            other_sem.at[number],
        )
        copy.start()
        copies.append(copy)
    lax.fori_loop(0, tiles, faces_of, 0)
    if others is not None:
        lax.fori_loop(0, tiles, settle, 0)
    for copy in copies:
        copy.wait()


def stream_part(state, pair, far, mask_x, part, base, after=None, arrived=None, others=None):
    fields, depth, _, _ = state.shape
    _, rows_y, _, width = part
    tiles = rows_y * width // (ROWS * LANES)

    def vregs(*dims):
        return pltpu.VMEM(dims + (ROWS, LANES), jnp.float32)

    def cells(part):
        return (fields, depth, part[1], part[3])

    scratch = [
        vregs(tiles, fields, depth + 5),
        vregs(tiles, fields, depth + 5),
        vregs(tiles, fields, depth + 1),
        vregs(tiles, depth + 1),
    ]
    inputs = [state, pair, far, mask_x, base]
    places_in = [PLACE] * len(inputs)
    if others is None:
        inputs.append(after)
        places_in.append(ANYWHERE)
        places = None
        target, target_shape = PLACE, shape_of(*cells(part))
    else:
        places = [place for place, _ in others]
        inputs += [arrived] + [array for _, array in others]
        places_in = [PLACE] * len(inputs)
        target, target_shape = HBM, shape_of(*state.shape)
        scratch += [
            pltpu.VMEM(cells(part), jnp.float32),
            pltpu.SemaphoreType.DMA((tiles,)),
            pltpu.SemaphoreType.DMA((len(others),)),
        ] + [pltpu.VMEM(cells(place), jnp.float32) for place in places]
    return call(
        functools.partial(stream_kernel, part, places),
        "stream_faces",
        0.3 * tiles,
        places_in,
        target,
        target_shape,
        scratch,
    )(*inputs)


def circulant_tables(span):
    half = span // 2
    step = 1
    while step * step < half:
        step *= 2
    count = half // step
    places = np.arange(span)
    period = max(2 * count, LANES)
    high = 2.0 * np.pi / span * ((np.arange(count)[:, None] * step * places[None, :period]) % span)
    low = 2.0 * np.pi / span * ((np.arange(step)[:, None] * places[None]) % span)
    tables = [np.concatenate([np.cos(a), np.sin(a)]) for a in (high, low)]
    return step, count, [jnp.asarray(t.astype(np.float32)) for t in tables]


def circulant_kernel(
    count, step, filter_ref, inner_ref, outer_ref, after_ref, high_ref, low_ref, band
):
    period = inner_ref.shape[1]
    span = outer_ref.shape[1]
    tall, wide = high_ref.shape
    order = step * lax.broadcasted_iota(
        jnp.int32, (count, step), 0
    ) + lax.broadcasted_iota(jnp.int32, (count, step), 1)
    scale = 2.0 / span * (2.0 * np.pi / span) * order.astype(jnp.float32) * filter_ref[...]

    def dot(table):
        return lax.dot_general(
            scale,
            table,
            (((0,), (0,)), ((), ())),
            precision=lax.Precision.HIGHEST,
            preferred_element_type=jnp.float32,
        )

    repeat = span // period
    inner_cos = jnp.concatenate([dot(inner_ref[:count])] * repeat, 1)
    inner_sin = jnp.concatenate([dot(inner_ref[count:])] * repeat, 1)
    line = jnp.sum(
        outer_ref[step:] * inner_cos + outer_ref[:step] * inner_sin, axis=0, keepdims=True
    )
    base = jnp.broadcast_to(-line, (ROWS, span))
    place = lax.broadcasted_iota(jnp.int32, (ROWS, span), 0)
    skew = base
    for i in range(1, ROWS):
        skew = jnp.where(place == i, pltpu.roll(base, i, 1), skew)
    for b in range(LANES // ROWS):
        rows = skew if b == 0 else pltpu.roll(skew, b * ROWS, 1)
        for q in range(tall // LANES):
            at = q * LANES + b * ROWS
            first = q * LANES
            if first:
                band[at : at + ROWS, :first] = rows[:, span - first :]
            band[at : at + ROWS, first:span] = rows[:, : span - first]
    full = band[...]
    high = full.astype(jnp.bfloat16)
    low = (full - high.astype(jnp.float32)).astype(jnp.bfloat16)
    high_ref[:, :span] = high
    low_ref[:, :span] = low
    high_ref[:, span:] = high[:, : wide - span]
    low_ref[:, span:] = low[:, : wide - span]


def circulant(span_filter, span, width, after):
    tall = min(256, width)
    step, count, tables = circulant_tables(span)
    band = shape_of(tall, span + width, dtype=jnp.bfloat16)
    return call(
        functools.partial(circulant_kernel, count, step),
        "circulant_band",
        1.0,
        [PLACE, PLACE, PLACE, ANYWHERE],
        [PLACE, PLACE],
        [band, band],
        [pltpu.VMEM((tall, span), jnp.float32)],
    )(span_filter.reshape(count, step), *tables, after)


def fill_lines(shards, x_refs):
    _, depth, rows_y, width = shards[0].shape
    xh, xl = x_refs
    for number, shard in enumerate(shards):

        def plane(index, carry):
            i = index // (width // LANES)
            t = index % (width // LANES)
            flux, _, _, _ = flux_of([shard[k, i, :, lanes(t)] for k in range(5)], 2)
            to = lanes(t + number * (width // LANES))
            for k in range(5):
                high = flux[k].astype(jnp.bfloat16)
                line = pl.ds(pl.multiple_of((k * depth + i) * rows_y, rows_y), rows_y)
                xh[line, to] = high
                xl[line, to] = (flux[k] - high.astype(jnp.float32)).astype(jnp.bfloat16)
            return carry

        lax.fori_loop(0, depth * (width // LANES), plane, 0)


def product(target, sources, high_ref, low_ref, xh, xl, w_s):
    tall, wide = high_ref.shape
    width = xh.shape[1] // len(sources)
    span = wide - width
    deep = xh.shape[1]
    for number, source in enumerate(sources):
        for q in range(width // tall):
            start = lax.rem((target - source) * width - q * tall + 2 * span, span)
            start = pl.multiple_of(start, LANES)
            at = number * width + q * tall
            w_s[at : at + tall, :] = high_ref[:, pl.ds(start, width)]
            w_s[deep + at : deep + at + tall, :] = low_ref[:, pl.ds(start, width)]
    dot = functools.partial(jnp.dot, preferred_element_type=jnp.float32)
    high = w_s[:deep, :]
    return dot(xh[...], high) + dot(xl[...], high) + dot(xh[...], w_s[deep:, :])


def away_kernel(masks, high_ref, low_ref, own_ref, core_ref, *refs):
    sums = refs[: len(masks)]
    xh, xl, w_s = refs[len(masks) :]
    me = lax.axis_index("gz")
    fill_lines([own_ref, core_ref], [xh, xl])
    for mask, sum_ref in zip(masks, sums):
        total = product(me ^ mask, [me, me ^ 1], high_ref, low_ref, xh, xl, w_s)
        sum_ref[...] = total.reshape(own_ref.shape)


def away_part(band, state, core, masks):
    fields, depth, rows_all, width = state.shape
    line = shape_of(fields * depth * rows_all, 2 * width, dtype=jnp.bfloat16)
    outs = call(
        functools.partial(away_kernel, masks),
        "span_away",
        3.0,
        [PLACE] * 4,
        [PLACE] * (len(masks) + 2),
        [shape_of(*state.shape)] * len(masks) + [line, line],
        [pltpu.VMEM((4 * width, width), jnp.bfloat16)],
    )(*band, state, core)
    return outs[: len(masks)], outs[len(masks) :]


def home_kernel(high_ref, low_ref, xh, xl, first_ref, second_ref, out_ref, w_s):
    me = lax.axis_index("gz")
    half = first_ref.shape[1]
    total = product(me, [me, me ^ 1], high_ref, low_ref, xh, xl, w_s).reshape(out_ref.shape)
    out_ref[:, :half] = first_ref[...] - TIME_STEP * total[:, :half]
    out_ref[:, half:] = second_ref[...] - TIME_STEP * total[:, half:]


def home_part(band, lines, first, second):
    fields, half, rows_all, width = first.shape
    return call(
        home_kernel,
        "span_home",
        2.0,
        [PLACE] * 6,
        PLACE,
        shape_of(fields, half + second.shape[1], rows_all, width),
        [pltpu.VMEM((4 * width, width), jnp.bfloat16)],
    )(*band, *lines, first, second)


def per_device(state, mask_x, mask_y, span_filter):
    fields, depth, rows_all, width = state.shape
    groups = lax.axis_size("gz")
    slabs = lax.axis_size("gx")
    span = width * groups

    def flip(array, bit):
        return lax.ppermute(array, "gz", [(g, g ^ bit) for g in range(groups)])

    swap = [(i, i ^ 1) for i in range(slabs)]
    carry = [(i, i + 2) for i in range(0, slabs - 2, 2)] + [
        (i, i - 2) for i in range(3, slabs, 2)
    ]
    core = flip(state, 1)
    if width % (4 * LANES) == 0:
        narrow = width // 4
        parts = [
            (0, rows_all // 2, 0, width - narrow),
            (rows_all // 2, rows_all // 2, 0, width - narrow),
            (0, rows_all, width - narrow, narrow),
        ]
    else:
        part = rows_all // 4
        parts = [(0, 2 * part, 0, width), (2 * part, part, 0, width), (3 * part, part, 0, width)]
    (brick,) = pack_part(state, mask_x, parts[:1])
    pairs = [lax.ppermute(brick, "gx", swap)]
    band = circulant(span_filter, span, width, core)

    masks = list(range(2, groups, 2))
    sums, lines = away_part(band, state, core, masks)
    arrived = sum(flip(part_sum, mask) for part_sum, mask in zip(sums, masks))
    half = depth // 2
    acc_low = wall_part(state, mask_y, 0, half, lines[0])
    brick = bring_part(state, mask_x, parts[1], acc_low)
    pairs.append(lax.ppermute(brick, "gx", swap))
    planes = pass_part(pairs[0], depth, brick)
    fars = [lax.ppermute(planes, "gx", carry)]
    acc_high = wall_part(state, mask_y, half, depth - half, planes)
    base = home_part(band, lines, acc_low, acc_high)
    brick = bring_part(state, mask_x, parts[2], base)
    pairs.append(lax.ppermute(brick, "gx", swap))

    planes = pass_part(pairs[1], depth, brick)
    fars.append(lax.ppermute(planes, "gx", carry))
    ready = stream_part(state, pairs[0], fars[0], mask_x, parts[0], base, planes)
    others = [(parts[0], ready)]
    planes = pass_part(pairs[2], depth, ready)
    fars.append(lax.ppermute(planes, "gx", carry))
    ready = stream_part(state, pairs[1], fars[1], mask_x, parts[1], base, planes)
    others.append((parts[1], ready))
    return stream_part(
        state, pairs[2], fars[2], mask_x, parts[2], base, arrived=arrived, others=others
    )


def solution(mesh):
    return jax.shard_map(
        per_device,
        mesh=mesh,
        in_specs=(P(None, "gx", None, "gz"), P("gx", None, "gz"), P("gx", None, "gz"), P()),
        out_specs=P(None, "gx", None, "gz"),
        check_vma=False,
    )
```

```python
import functools

import jax
import jax.numpy as jnp
import numpy as np
from jax import lax
from jax.experimental import pallas as pl
from jax.experimental.pallas import tpu as pltpu
from jax.sharding import PartitionSpec as P

GAMMA_GAS = 1.4
SMALL_EPS = 1e-06
TIME_STEP = 0.1
ROWS = 8
LANES = 128
VMEM_BYTES = 24 * 1024 * 1024
PACK_BYTES = 60 * 1024 * 1024
FACE_SCALE = -TIME_STEP / 60.0
PLACE = pl.BlockSpec(memory_space=pltpu.VMEM)
ANYWHERE = pl.BlockSpec(memory_space=pl.ANY)
HBM = pl.BlockSpec(memory_space=pltpu.HBM)


def call(kernel, name, weight, ins, outs, out_shape, scratch=(), aliases=None, vmem=VMEM_BYTES):
    return pl.pallas_call(
        kernel,
        out_shape=out_shape,
        in_specs=ins,
        out_specs=outs,
        scratch_shapes=list(scratch),
        input_output_aliases=aliases or {},
        compiler_params=pltpu.CompilerParams(vmem_limit_bytes=vmem),
        cost_estimate=pl.CostEstimate(
            flops=int(weight * 1e9), bytes_accessed=int(weight * 3e6), transcendentals=0
        ),
        name=name,
    )


def shape_of(*dims, dtype=jnp.float32):
    return jax.ShapeDtypeStruct(dims, dtype)


def flux_of(q, normal):
    thin = pl.reciprocal(q[0], approx=True)
    velocity = [q[1] * thin, q[2] * thin, q[3] * thin]
    pressure = (GAMMA_GAS - 1.0) * (
        q[4] - 0.5 * (q[1] * velocity[0] + q[2] * velocity[1] + q[3] * velocity[2])
    )
    along = velocity[normal]
    flux = [q[normal + 1], q[1] * along, q[2] * along, q[3] * along, (q[4] + pressure) * along]
    flux[normal + 1] = flux[normal + 1] + pressure
    return flux, pressure, thin, along


def speed_of(pressure, thin, along):
    return jnp.abs(along) + jnp.sqrt(GAMMA_GAS * pressure * thin)


def weno_rest(d1, d2, d3, d4):
    low = d2 * d2 * 0.609375 + 3.0 * SMALL_EPS
    high = d3 * d3 * 0.609375 + 3.0 * SMALL_EPS
    x0 = d1 - 1.375 * d2
    x1 = d2 - 0.625 * d3
    x2 = d4 - 1.375 * d3
    t0 = low + x0 * x0
    t1 = high + x1 * x1
    t2 = high + x2 * x2
    w0 = t1 * t2
    w1 = t0 * t2
    w2 = t0 * t1
    w0 = w0 * w0
    w1 = w1 * w1
    w2 = w2 * w2 * 1.5
    top = w0 * (x0 + (d3 - 0.625 * d2)) + w2 * (x1 + x2)
    bottom = 0.5 * w0 + 3.0 * w1 + w2
    return top * pl.reciprocal(bottom, approx=True)


def face_value(dq, df, both, alpha, upwind):
    aq = [alpha * value for value in dq]
    plus = [df[k] + aq[k] for k in range(4)]
    minus = [df[k] - aq[k] for k in range(1, 5)]
    bend = df[1] - df[3]
    central = 7.0 * bend + (df[4] - df[0])
    rest = weno_rest(minus[3], minus[2], minus[1], minus[0]) - weno_rest(*plus)
    biased = 5.0 * (bend + (aq[1] + aq[3]) - (aq[2] + aq[2]) + rest)
    return 30.0 * both + jnp.where(upwind, biased, central)


def lanes(number):
    return pl.ds(pl.multiple_of(number * LANES, LANES), LANES)


def wall_kernel(low, state_ref, mask_ref, out_ref, q_s, f_s, speed_s, dq_s, df_s):
    rows_y = state_ref.shape[2]
    width = state_ref.shape[3]
    tiles = rows_y // ROWS
    end = ROWS + rows_y
    zero = jnp.zeros((5, ROWS, LANES), jnp.float32)
    for side in (dq_s, df_s):
        side[:, 0:ROWS, :] = zero
        side[:, end : end + ROWS, :] = zero
    row = lax.broadcasted_iota(jnp.int32, (ROWS, LANES), 0)

    def column(number, carry):
        plane = number // (width // LANES)
        lane = lanes(number % (width // LANES))
        zero_row = jnp.minimum(number, 0)

        def at(r, shift):
            return pl.ds(zero_row + (r * ROWS + ROWS + shift), ROWS)

        def still(r):
            return slice(r * ROWS + ROWS, r * ROWS + 2 * ROWS)

        qs = []
        for r in range(tiles):
            mine = slice(r * ROWS, r * ROWS + ROWS)
            q = [state_ref[k, low + plane, mine, lane] for k in range(5)]
            flux, pressure, thin, along = flux_of(q, 1)
            speed = speed_of(pressure, thin, along)
            for k in range(5):
                q_s[k, still(r), :] = q[k]
                f_s[k, still(r), :] = flux[k]
            speed_s[still(r), :] = speed
            if r == 0:
                for k in range(5):
                    q_s[k, 0:ROWS, :] = jnp.broadcast_to(q[k][0:1], (ROWS, LANES))
                    f_s[k, 0:ROWS, :] = jnp.broadcast_to(flux[k][0:1], (ROWS, LANES))
                speed_s[0:ROWS, :] = jnp.broadcast_to(speed[0:1], (ROWS, LANES))
            if r == tiles - 1:
                speed_s[end : end + ROWS, :] = jnp.broadcast_to(
                    speed[ROWS - 1 : ROWS], (ROWS, LANES)
                )
        for k in range(5):
            changes = [
                (
                    q_s[k, still(r), :] - q_s[k, at(r, -1), :],
                    f_s[k, still(r), :] - f_s[k, at(r, -1), :],
                )
                for r in range(tiles)
            ]
            for r in range(tiles):
                dq_s[k, still(r), :] = changes[r][0]
                df_s[k, still(r), :] = changes[r][1]
        alphas, switches = [], []
        for r in range(tiles):
            alpha = speed_s[still(r), :]
            for shift in (-3, -2, -1, 1, 2):
                alpha = jnp.maximum(alpha, speed_s[at(r, shift), :])
            alphas.append(alpha)
            switches.append(mask_ref[low + plane, r * ROWS : r * ROWS + ROWS, lane] > 0)
        for k in range(5):
            hats = []
            for r in range(tiles):
                dq = [dq_s[k, at(r, s), :] for s in (-2, -1)]
                df = [df_s[k, at(r, s), :] for s in (-2, -1)]
                dq += [dq_s[k, still(r), :]]
                df += [df_s[k, still(r), :]]
                dq += [dq_s[k, at(r, s), :] for s in (1, 2)]
                df += [df_s[k, at(r, s), :] for s in (1, 2)]
                here = f_s[k, still(r), :]
                both = here + here - df[2]
                hats.append(face_value(dq, df, both, alphas[r], switches[r]))
            top = (
                60.0 * f_s[k, end - 1 : end, :]
                + 7.0 * df_s[k, end - 1 : end, :]
                - df_s[k, end - 2 : end - 1, :]
            )
            turned = [pltpu.roll(hat, ROWS - 1, 0) for hat in hats]
            turned.append(jnp.broadcast_to(top, (ROWS, LANES)))
            for r in range(tiles):
                after = jnp.where(row == ROWS - 1, turned[r + 1], turned[r])
                mine = slice(r * ROWS, r * ROWS + ROWS)
                out_ref[k, plane, mine, lane] = q_s[k, still(r), :] + FACE_SCALE * (after - hats[r])
        return carry

    lax.fori_loop(0, out_ref.shape[1] * (width // LANES), column, 0)


def wall_part(state, mask_y, low, count, after):
    fields, depth, rows_y, width = state.shape
    tall = rows_y + 2 * ROWS
    padded = pltpu.VMEM((fields, tall, LANES), jnp.float32)

    def kernel(state_ref, mask_ref, after_ref, out_ref, *scratch):
        wall_kernel(low, state_ref, mask_ref, out_ref, *scratch)

    return call(
        kernel,
        "wall_faces",
        5.0 * count / depth,
        [PLACE, PLACE, ANYWHERE],
        PLACE,
        shape_of(fields, count, rows_y, width),
        [padded, padded, pltpu.VMEM((tall, LANES), jnp.float32), padded, padded],
    )(state, mask_y, after)


def pack_kernel(parts, state_ref, mask_ref, *refs):
    outs = refs[: len(parts)]
    mask_s, sems = refs[len(parts) :]
    planes = state_ref.shape[0]
    mask_copy = pltpu.make_async_copy(mask_ref.at[0], mask_s, sems.at[len(parts)])
    mask_copy.start()
    copies = [
        pltpu.make_async_copy(
            state_ref.at[:, pl.ds(row, rows), pl.ds(lane, width)],
            out.at[pl.ds(0, planes)],
            sems.at[c],
        )
        for c, ((row, rows, lane, width), out) in enumerate(zip(parts, outs))
    ]
    for copy in copies:
        copy.start()
    mask_copy.wait()
    for (row, rows, lane, width), out in zip(parts, outs):
        out[planes] = mask_s[row : row + rows, lane : lane + width].astype(jnp.float32)
    for copy in copies:
        copy.wait()


def pack_part(state, mask_x, parts):
    fields, depth, rows_all, width = state.shape
    planes = fields * depth
    return call(
        functools.partial(pack_kernel, parts),
        "pack_bricks",
        1.0,
        [HBM, HBM],
        [PLACE] * len(parts),
        [shape_of(planes + 1, rows, lane_count) for _, rows, _, lane_count in parts],
        [
            pltpu.VMEM((rows_all, width), jnp.int32),
            pltpu.SemaphoreType.DMA((len(parts) + 1,)),
        ],
        vmem=PACK_BYTES,
    )(state.reshape(planes, rows_all, width), mask_x)


def bring_kernel(part, state_ref, mask_ref, after_ref, out):
    row, rows, lane, width = part
    fields, depth, _, _ = state_ref.shape
    for k in range(fields):
        for i in range(depth):
            out[depth * k + i] = state_ref[k, i, row : row + rows, lane : lane + width]
    switches = mask_ref[0, row : row + rows, lane : lane + width]
    out[depth * fields] = switches.astype(jnp.float32)


def bring_part(state, mask_x, part, after):
    fields, depth, _, _ = state.shape
    _, rows, _, width = part
    return call(
        functools.partial(bring_kernel, part),
        "bring_planes",
        0.5,
        [PLACE, PLACE, ANYWHERE],
        PLACE,
        shape_of(depth * fields + 1, rows, width),
    )(state, mask_x, after)


def pass_kernel(depth, pair_ref, after_ref, out_ref):
    planes = pair_ref.shape[0] - 1
    skip = 1 - lax.rem(lax.axis_index("gx"), 2)
    for k in range(planes // depth):
        for i in range(3):
            out_ref[3 * k + i] = pair_ref[depth * k + i + skip * (depth - 3)]
    out_ref[3 * (planes // depth)] = pair_ref[planes]


def pass_part(pair, depth, after):
    planes, rows_y, width = pair.shape
    return call(
        functools.partial(pass_kernel, depth),
        "pass_planes",
        0.5,
        [PLACE, ANYWHERE],
        PLACE,
        shape_of(3 * (planes - 1) // depth + 1, rows_y, width),
    )(pair, after)


def stream_kernel(part, others, *refs):
    (state_ref, pair_ref, far_ref, mask_ref, base_ref), refs = refs[:5], refs[5:]
    if others is None:
        _, out_ref, dq_s, df_s, both_s, alpha_s = refs
        result = out_ref
    else:
        sum_ref, other_refs, refs = refs[0], refs[1 : 1 + len(others)], refs[1 + len(others) :]
        out_ref, dq_s, df_s, both_s, alpha_s, result, sem, other_sem = refs[:8]
        staged = refs[8:]
    fields, depth, _, _ = state_ref.shape
    start, rows_y, start_lane, width = part
    stride = depth
    rank = lax.axis_index("gx")
    even = lax.rem(rank, 2) == 0
    first = rank == 0
    last = rank == lax.axis_size("gx") - 1
    lane_tiles = width // LANES
    faces = depth + 1
    tiles = (rows_y // ROWS) * lane_tiles

    def rows(row, shift):
        return pl.ds(pl.multiple_of(row + shift, ROWS), ROWS)

    def place(number):
        lane = (number % lane_tiles) * LANES
        return (
            (number // lane_tiles) * ROWS,
            pl.ds(pl.multiple_of(lane, LANES), LANES),
            pl.ds(pl.multiple_of(lane + start_lane, LANES), LANES),
        )

    def point(number, carry):
        at, lane, there = place(number)
        row, mine = rows(at, 0), rows(at, start)
        own = [[state_ref[k, i, mine, there] for k in range(5)] for i in range(depth)]
        cells = []
        for i in range(3):
            cells.append(
                [
                    jnp.where(
                        first,
                        own[0][k],
                        jnp.where(
                            even,
                            far_ref[3 * k + i, row, lane],
                            pair_ref[stride * k + stride - 3 + i, row, lane],
                        ),
                    )
                    for k in range(5)
                ]
            )
        cells += own
        for i in range(3):
            cells.append(
                [
                    jnp.where(
                        last,
                        own[depth - 1][k],
                        jnp.where(
                            even,
                            pair_ref[stride * k + i, row, lane],
                            far_ref[3 * k + i, row, lane],
                        ),
                    )
                    for k in range(5)
                ]
            )
        speeds, before = [], None
        for j, q in enumerate(cells):
            flux, pressure, thin, along = flux_of(q, 0)
            speeds.append(speed_of(pressure, thin, along))
            if j > 0:
                for k in range(5):
                    dq_s[number, k, j - 1] = q[k] - cells[j - 1][k]
                    df_s[number, k, j - 1] = flux[k] - before[k]
                    if 3 <= j < 3 + faces:
                        both_s[number, k, j - 3] = flux[k] + before[k]
            before = flux
        pairs = [jnp.maximum(speeds[i], speeds[i + 1]) for i in range(depth + 5)]
        for f in range(faces):
            alpha_s[number, f] = jnp.maximum(jnp.maximum(pairs[f], pairs[f + 2]), pairs[f + 4])
        return carry

    lax.fori_loop(0, tiles, point, 0)

    def faces_of(number, carry):
        at, lane, there = place(number)
        row, mine = rows(at, 0), rows(at, start)
        border = jnp.where(
            even, pair_ref[stride * fields, row, lane], far_ref[3 * fields, row, lane]
        )
        border = jnp.where(last, 0.0, border)
        switches = [mask_ref[i, mine, there] > 0 for i in range(depth)] + [border > 0.0]
        results = []
        for k in range(5):
            dq = [dq_s[number, k, j] for j in range(depth + 5)]
            df = [df_s[number, k, j] for j in range(depth + 5)]
            hats = [
                face_value(
                    dq[f : f + 5], df[f : f + 5], both_s[number, k, f], alpha_s[number, f], switches[f]
                )
                for f in range(faces)
            ]
            for i in range(depth):
                value = base_ref[k, i, mine, there] + FACE_SCALE * (hats[i + 1] - hats[i])
                if others is not None:
                    value = value - TIME_STEP * sum_ref[k, i, mine, there]
                results.append(value)
        for k in range(5):
            for i in range(depth):
                result[k, i, row, lane] = results[k * depth + i]
        if others is not None:
            hand_out(number).start()
        return carry

    def hand_out(number):
        at, lane, there = place(number)
        return pltpu.make_async_copy(
            result.at[:, :, rows(at, 0), lane],
            out_ref.at[:, :, rows(at, start), there],
            sem.at[number],
        )

    def settle(number, carry):
        hand_out(number).wait()
        return carry

    copies = []
    for number, other in enumerate(others or []):
        top, tall, left, wide = other

        def line(index, carry, number=number, top=top, tall=tall, left=left, wide=wide):
            k, i = index // depth, index % depth
            staged[number][k, i] = other_refs[number][k, i] - TIME_STEP * (
                sum_ref[k, i, top : top + tall, left : left + wide]
            )
            return carry

        lax.fori_loop(0, fields * depth, line, 0)
        copy = pltpu.make_async_copy(
            staged[number],
            out_ref.at[:, :, pl.ds(top, tall), pl.ds(left, wide)],
            other_sem.at[number],
        )
        copy.start()
        copies.append(copy)
    lax.fori_loop(0, tiles, faces_of, 0)
    if others is not None:
        lax.fori_loop(0, tiles, settle, 0)
    for copy in copies:
        copy.wait()


def stream_part(state, pair, far, mask_x, part, base, after=None, arrived=None, others=None):
    fields, depth, _, _ = state.shape
    _, rows_y, _, width = part
    tiles = rows_y * width // (ROWS * LANES)

    def vregs(*dims):
        return pltpu.VMEM(dims + (ROWS, LANES), jnp.float32)

    def cells(part):
        return (fields, depth, part[1], part[3])

    scratch = [
        vregs(tiles, fields, depth + 5),
        vregs(tiles, fields, depth + 5),
        vregs(tiles, fields, depth + 1),
        vregs(tiles, depth + 1),
    ]
    inputs = [state, pair, far, mask_x, base]
    places_in = [PLACE] * len(inputs)
    if others is None:
        inputs.append(after)
        places_in.append(ANYWHERE)
        places = None
        target, target_shape = PLACE, shape_of(*cells(part))
    else:
        places = [place for place, _ in others]
        inputs += [arrived] + [array for _, array in others]
        places_in = [PLACE] * len(inputs)
        target, target_shape = HBM, shape_of(*state.shape)
        scratch += [
            pltpu.VMEM(cells(part), jnp.float32),
            pltpu.SemaphoreType.DMA((tiles,)),
            pltpu.SemaphoreType.DMA((len(others),)),
        ] + [pltpu.VMEM(cells(place), jnp.float32) for place in places]
    return call(
        functools.partial(stream_kernel, part, places),
        "stream_faces",
        0.3 * tiles,
        places_in,
        target,
        target_shape,
        scratch,
    )(*inputs)


def circulant_tables(span):
    half = span // 2
    step = 1
    while step * step < half:
        step *= 2
    count = half // step
    places = np.arange(span)
    period = max(2 * count, LANES)
    high = 2.0 * np.pi / span * ((np.arange(count)[:, None] * step * places[None, :period]) % span)
    low = 2.0 * np.pi / span * ((np.arange(step)[:, None] * places[None]) % span)
    tables = [np.concatenate([np.cos(a), np.sin(a)]) for a in (high, low)]
    return step, count, [jnp.asarray(t.astype(np.float32)) for t in tables]


def circulant_kernel(
    count, step, filter_ref, inner_ref, outer_ref, after_ref, high_ref, low_ref, band
):
    period = inner_ref.shape[1]
    span = outer_ref.shape[1]
    tall, wide = high_ref.shape
    order = step * lax.broadcasted_iota(
        jnp.int32, (count, step), 0
    ) + lax.broadcasted_iota(jnp.int32, (count, step), 1)
    scale = 2.0 / span * (2.0 * np.pi / span) * order.astype(jnp.float32) * filter_ref[...]

    def dot(table):
        return lax.dot_general(
            scale,
            table,
            (((0,), (0,)), ((), ())),
            precision=lax.Precision.HIGHEST,
            preferred_element_type=jnp.float32,
        )

    repeat = span // period
    inner_cos = jnp.concatenate([dot(inner_ref[:count])] * repeat, 1)
    inner_sin = jnp.concatenate([dot(inner_ref[count:])] * repeat, 1)
    line = jnp.sum(
        outer_ref[step:] * inner_cos + outer_ref[:step] * inner_sin, axis=0, keepdims=True
    )
    base = jnp.broadcast_to(-line, (ROWS, span))
    place = lax.broadcasted_iota(jnp.int32, (ROWS, span), 0)
    skew = base
    for i in range(1, ROWS):
        skew = jnp.where(place == i, pltpu.roll(base, i, 1), skew)
    for b in range(LANES // ROWS):
        rows = skew if b == 0 else pltpu.roll(skew, b * ROWS, 1)
        for q in range(tall // LANES):
            at = q * LANES + b * ROWS
            first = q * LANES
            if first:
                band[at : at + ROWS, :first] = rows[:, span - first :]
            band[at : at + ROWS, first:span] = rows[:, : span - first]
    full = band[...]
    high = full.astype(jnp.bfloat16)
    low = (full - high.astype(jnp.float32)).astype(jnp.bfloat16)
    high_ref[:, :span] = high
    low_ref[:, :span] = low
    high_ref[:, span:] = high[:, : wide - span]
    low_ref[:, span:] = low[:, : wide - span]


def circulant(span_filter, span, width, after):
    tall = min(256, width)
    step, count, tables = circulant_tables(span)
    band = shape_of(tall, span + width, dtype=jnp.bfloat16)
    return call(
        functools.partial(circulant_kernel, count, step),
        "circulant_band",
        1.0,
        [PLACE, PLACE, PLACE, ANYWHERE],
        [PLACE, PLACE],
        [band, band],
        [pltpu.VMEM((tall, span), jnp.float32)],
    )(span_filter.reshape(count, step), *tables, after)


def fill_lines(shards, x_refs):
    _, depth, rows_y, width = shards[0].shape
    xh, xl = x_refs
    for number, shard in enumerate(shards):

        def plane(index, carry):
            i = index // (width // LANES)
            t = index % (width // LANES)
            flux, _, _, _ = flux_of([shard[k, i, :, lanes(t)] for k in range(5)], 2)
            to = lanes(t + number * (width // LANES))
            for k in range(5):
                high = flux[k].astype(jnp.bfloat16)
                line = pl.ds(pl.multiple_of((k * depth + i) * rows_y, rows_y), rows_y)
                xh[line, to] = high
                xl[line, to] = (flux[k] - high.astype(jnp.float32)).astype(jnp.bfloat16)
            return carry

        lax.fori_loop(0, depth * (width // LANES), plane, 0)


def product(target, sources, high_ref, low_ref, xh, xl, w_s):
    tall, wide = high_ref.shape
    width = xh.shape[1] // len(sources)
    span = wide - width
    deep = xh.shape[1]
    for number, source in enumerate(sources):
        for q in range(width // tall):
            start = lax.rem((target - source) * width - q * tall + 2 * span, span)
            start = pl.multiple_of(start, LANES)
            at = number * width + q * tall
            w_s[at : at + tall, :] = high_ref[:, pl.ds(start, width)]
            w_s[deep + at : deep + at + tall, :] = low_ref[:, pl.ds(start, width)]
    dot = functools.partial(jnp.dot, preferred_element_type=jnp.float32)
    high = w_s[:deep, :]
    return dot(xh[...], high) + dot(xl[...], high) + dot(xh[...], w_s[deep:, :])


def away_kernel(masks, high_ref, low_ref, own_ref, core_ref, *refs):
    sums = refs[: len(masks)]
    xh, xl, w_s = refs[len(masks) :]
    me = lax.axis_index("gz")
    fill_lines([own_ref, core_ref], [xh, xl])
    for mask, sum_ref in zip(masks, sums):
        total = product(me ^ mask, [me, me ^ 1], high_ref, low_ref, xh, xl, w_s)
        sum_ref[...] = total.reshape(own_ref.shape)


def away_part(band, state, core, masks):
    fields, depth, rows_all, width = state.shape
    line = shape_of(fields * depth * rows_all, 2 * width, dtype=jnp.bfloat16)
    outs = call(
        functools.partial(away_kernel, masks),
        "span_away",
        3.0,
        [PLACE] * 4,
        [PLACE] * (len(masks) + 2),
        [shape_of(*state.shape)] * len(masks) + [line, line],
        [pltpu.VMEM((4 * width, width), jnp.bfloat16)],
    )(*band, state, core)
    return outs[: len(masks)], outs[len(masks) :]


def home_kernel(high_ref, low_ref, xh, xl, first_ref, second_ref, after_ref, out_ref, w_s):
    me = lax.axis_index("gz")
    half = first_ref.shape[1]
    total = product(me, [me, me ^ 1], high_ref, low_ref, xh, xl, w_s).reshape(out_ref.shape)
    out_ref[:, :half] = first_ref[...] - TIME_STEP * total[:, :half]
    out_ref[:, half:] = second_ref[...] - TIME_STEP * total[:, half:]


def home_part(band, lines, first, second, after):
    fields, half, rows_all, width = first.shape
    return call(
        home_kernel,
        "span_home",
        2.0,
        [PLACE] * 6 + [ANYWHERE],
        PLACE,
        shape_of(fields, half + second.shape[1], rows_all, width),
        [pltpu.VMEM((4 * width, width), jnp.bfloat16)],
    )(*band, *lines, first, second, after)


def per_device(state, mask_x, mask_y, span_filter):
    fields, depth, rows_all, width = state.shape
    groups = lax.axis_size("gz")
    slabs = lax.axis_size("gx")
    span = width * groups

    def flip(array, bit):
        return lax.ppermute(array, "gz", [(g, g ^ bit) for g in range(groups)])

    swap = [(i, i ^ 1) for i in range(slabs)]
    carry = [(i, i + 2) for i in range(0, slabs - 2, 2)] + [
        (i, i - 2) for i in range(3, slabs, 2)
    ]
    core = flip(state, 1)
    low = rows_all // 2
    if width % (4 * LANES) == 0:
        lane = width // 4
        parts = [
            (0, low, 0, 3 * lane),
            (low, low, 0, 2 * lane),
            (0, rows_all, 3 * lane, lane),
            (low, low, 2 * lane, lane),
        ]
    else:
        parts = [(row, rows_all // 4, 0, width) for row in range(0, rows_all, rows_all // 4)]
    (brick,) = pack_part(state, mask_x, parts[:1])
    pairs = [lax.ppermute(brick, "gx", swap)]
    band = circulant(span_filter, span, width, core)

    masks = list(range(2, groups, 2))
    sums, lines = away_part(band, state, core, masks)
    arrived = sum(flip(part_sum, mask) for part_sum, mask in zip(sums, masks))
    half = depth // 2
    fars, others = [], []

    def exchange(c, after):
        brick = bring_part(state, mask_x, parts[c], after)
        pairs.append(lax.ppermute(brick, "gx", swap))
        return brick

    def hand_on(c, after):
        planes = pass_part(pairs[c], depth, after)
        fars.append(lax.ppermute(planes, "gx", carry))
        return planes

    def stream(c, after):
        done = stream_part(state, pairs[c], fars[c], mask_x, parts[c], base, after)
        others.append((parts[c], done))
        return done

    acc_low = wall_part(state, mask_y, 0, half, lines[0])
    after = hand_on(0, exchange(1, acc_low))
    acc_high = wall_part(state, mask_y, half, depth - half, after)
    after = hand_on(1, exchange(2, acc_high))
    base = home_part(band, lines, acc_low, acc_high, after)
    after = hand_on(2, exchange(3, base))
    after = hand_on(3, stream(0, after))
    stream(2, stream(1, after))
    return stream_part(
        state, pairs[3], fars[3], mask_x, parts[3], base, arrived=arrived, others=others
    )


def solution(mesh):
    return jax.shard_map(
        per_device,
        mesh=mesh,
        in_specs=(P(None, "gx", None, "gz"), P("gx", None, "gz"), P("gx", None, "gz"), P()),
        out_specs=P(None, "gx", None, "gz"),
        check_vma=False,
    )
```

```python
import functools

import jax
import jax.numpy as jnp
import numpy as np
from jax import lax
from jax.experimental import pallas as pl
from jax.experimental.pallas import tpu as pltpu
from jax.sharding import PartitionSpec as P

GAMMA_GAS = 1.4
SMALL_EPS = 1e-06
TIME_STEP = 0.1
ROWS = 8
LANES = 128
VMEM_BYTES = 24 * 1024 * 1024
PACK_BYTES = 60 * 1024 * 1024
FACE_SCALE = -TIME_STEP / 60.0
PLACE = pl.BlockSpec(memory_space=pltpu.VMEM)
ANYWHERE = pl.BlockSpec(memory_space=pl.ANY)
HBM = pl.BlockSpec(memory_space=pltpu.HBM)


def call(kernel, name, weight, ins, outs, out_shape, scratch=(), aliases=None, vmem=VMEM_BYTES):
    return pl.pallas_call(
        kernel,
        out_shape=out_shape,
        in_specs=ins,
        out_specs=outs,
        scratch_shapes=list(scratch),
        input_output_aliases=aliases or {},
        compiler_params=pltpu.CompilerParams(vmem_limit_bytes=vmem),
        cost_estimate=pl.CostEstimate(
            flops=int(weight * 1e9), bytes_accessed=int(weight * 3e6), transcendentals=0
        ),
        name=name,
    )


def shape_of(*dims, dtype=jnp.float32):
    return jax.ShapeDtypeStruct(dims, dtype)


def flux_of(q, normal):
    thin = pl.reciprocal(q[0], approx=True)
    velocity = [q[1] * thin, q[2] * thin, q[3] * thin]
    pressure = (GAMMA_GAS - 1.0) * (
        q[4] - 0.5 * (q[1] * velocity[0] + q[2] * velocity[1] + q[3] * velocity[2])
    )
    along = velocity[normal]
    flux = [q[normal + 1], q[1] * along, q[2] * along, q[3] * along, (q[4] + pressure) * along]
    flux[normal + 1] = flux[normal + 1] + pressure
    return flux, pressure, thin, along


def speed_of(pressure, thin, along):
    return jnp.abs(along) + jnp.sqrt(GAMMA_GAS * pressure * thin)


def weno_rest(d1, d2, d3, d4):
    low = d2 * d2 * 0.609375 + 3.0 * SMALL_EPS
    high = d3 * d3 * 0.609375 + 3.0 * SMALL_EPS
    x0 = d1 - 1.375 * d2
    x1 = d2 - 0.625 * d3
    x2 = d4 - 1.375 * d3
    t0 = low + x0 * x0
    t1 = high + x1 * x1
    t2 = high + x2 * x2
    w0 = t1 * t2
    w1 = t0 * t2
    w2 = t0 * t1
    w0 = w0 * w0
    w1 = w1 * w1
    w2 = w2 * w2 * 1.5
    top = w0 * (x0 + (d3 - 0.625 * d2)) + w2 * (x1 + x2)
    bottom = 0.5 * w0 + 3.0 * w1 + w2
    return top * pl.reciprocal(bottom, approx=True)


def face_value(dq, df, both, alpha, upwind):
    aq = [alpha * value for value in dq]
    plus = [df[k] + aq[k] for k in range(4)]
    minus = [df[k] - aq[k] for k in range(1, 5)]
    bend = df[1] - df[3]
    central = 7.0 * bend + (df[4] - df[0])
    rest = weno_rest(minus[3], minus[2], minus[1], minus[0]) - weno_rest(*plus)
    biased = 5.0 * (bend + (aq[1] + aq[3]) - (aq[2] + aq[2]) + rest)
    return 30.0 * both + jnp.where(upwind, biased, central)


def lanes(number):
    return pl.ds(pl.multiple_of(number * LANES, LANES), LANES)


def wall_kernel(low, state_ref, mask_ref, out_ref, q_s, f_s, speed_s, dq_s, df_s):
    rows_y = state_ref.shape[2]
    width = state_ref.shape[3]
    tiles = rows_y // ROWS
    end = ROWS + rows_y
    zero = jnp.zeros((5, ROWS, LANES), jnp.float32)
    for side in (dq_s, df_s):
        side[:, 0:ROWS, :] = zero
        side[:, end : end + ROWS, :] = zero
    row = lax.broadcasted_iota(jnp.int32, (ROWS, LANES), 0)

    def column(number, carry):
        plane = number // (width // LANES)
        lane = lanes(number % (width // LANES))
        zero_row = jnp.minimum(number, 0)

        def at(r, shift):
            return pl.ds(zero_row + (r * ROWS + ROWS + shift), ROWS)

        def still(r):
            return slice(r * ROWS + ROWS, r * ROWS + 2 * ROWS)

        qs = []
        for r in range(tiles):
            mine = slice(r * ROWS, r * ROWS + ROWS)
            q = [state_ref[k, low + plane, mine, lane] for k in range(5)]
            flux, pressure, thin, along = flux_of(q, 1)
            speed = speed_of(pressure, thin, along)
            for k in range(5):
                q_s[k, still(r), :] = q[k]
                f_s[k, still(r), :] = flux[k]
            speed_s[still(r), :] = speed
            if r == 0:
                for k in range(5):
                    q_s[k, 0:ROWS, :] = jnp.broadcast_to(q[k][0:1], (ROWS, LANES))
                    f_s[k, 0:ROWS, :] = jnp.broadcast_to(flux[k][0:1], (ROWS, LANES))
                speed_s[0:ROWS, :] = jnp.broadcast_to(speed[0:1], (ROWS, LANES))
            if r == tiles - 1:
                speed_s[end : end + ROWS, :] = jnp.broadcast_to(
                    speed[ROWS - 1 : ROWS], (ROWS, LANES)
                )
        for k in range(5):
            changes = [
                (
                    q_s[k, still(r), :] - q_s[k, at(r, -1), :],
                    f_s[k, still(r), :] - f_s[k, at(r, -1), :],
                )
                for r in range(tiles)
            ]
            for r in range(tiles):
                dq_s[k, still(r), :] = changes[r][0]
                df_s[k, still(r), :] = changes[r][1]
        alphas, switches = [], []
        for r in range(tiles):
            alpha = speed_s[still(r), :]
            for shift in (-3, -2, -1, 1, 2):
                alpha = jnp.maximum(alpha, speed_s[at(r, shift), :])
            alphas.append(alpha)
            switches.append(mask_ref[low + plane, r * ROWS : r * ROWS + ROWS, lane] > 0)
        for k in range(5):
            hats = []
            for r in range(tiles):
                dq = [dq_s[k, at(r, s), :] for s in (-2, -1)]
                df = [df_s[k, at(r, s), :] for s in (-2, -1)]
                dq += [dq_s[k, still(r), :]]
                df += [df_s[k, still(r), :]]
                dq += [dq_s[k, at(r, s), :] for s in (1, 2)]
                df += [df_s[k, at(r, s), :] for s in (1, 2)]
                here = f_s[k, still(r), :]
                both = here + here - df[2]
                hats.append(face_value(dq, df, both, alphas[r], switches[r]))
            top = (
                60.0 * f_s[k, end - 1 : end, :]
                + 7.0 * df_s[k, end - 1 : end, :]
                - df_s[k, end - 2 : end - 1, :]
            )
            turned = [pltpu.roll(hat, ROWS - 1, 0) for hat in hats]
            turned.append(jnp.broadcast_to(top, (ROWS, LANES)))
            for r in range(tiles):
                after = jnp.where(row == ROWS - 1, turned[r + 1], turned[r])
                mine = slice(r * ROWS, r * ROWS + ROWS)
                out_ref[k, plane, mine, lane] = q_s[k, still(r), :] + FACE_SCALE * (after - hats[r])
        return carry

    lax.fori_loop(0, out_ref.shape[1] * (width // LANES), column, 0)


def wall_part(state, mask_y, low, count, after):
    fields, depth, rows_y, width = state.shape
    tall = rows_y + 2 * ROWS
    padded = pltpu.VMEM((fields, tall, LANES), jnp.float32)

    def kernel(state_ref, mask_ref, after_ref, out_ref, *scratch):
        wall_kernel(low, state_ref, mask_ref, out_ref, *scratch)

    return call(
        kernel,
        "wall_faces",
        5.0 * count / depth,
        [PLACE, PLACE, ANYWHERE],
        PLACE,
        shape_of(fields, count, rows_y, width),
        [padded, padded, pltpu.VMEM((tall, LANES), jnp.float32), padded, padded],
    )(state, mask_y, after)


def pack_kernel(parts, state_ref, mask_ref, *refs):
    outs = refs[: len(parts)]
    mask_s, sems = refs[len(parts) :]
    planes = state_ref.shape[0]
    mask_copy = pltpu.make_async_copy(mask_ref.at[0], mask_s, sems.at[len(parts)])
    mask_copy.start()
    copies = [
        pltpu.make_async_copy(
            state_ref.at[:, pl.ds(row, rows), pl.ds(lane, width)],
            out.at[pl.ds(0, planes)],
            sems.at[c],
        )
        for c, ((row, rows, lane, width), out) in enumerate(zip(parts, outs))
    ]
    for copy in copies:
        copy.start()
    mask_copy.wait()
    for (row, rows, lane, width), out in zip(parts, outs):
        out[planes] = mask_s[row : row + rows, lane : lane + width].astype(jnp.float32)
    for copy in copies:
        copy.wait()


def pack_part(state, mask_x, parts):
    fields, depth, rows_all, width = state.shape
    planes = fields * depth
    return call(
        functools.partial(pack_kernel, parts),
        "pack_bricks",
        1.0,
        [HBM, HBM],
        [PLACE] * len(parts),
        [shape_of(planes + 1, rows, lane_count) for _, rows, _, lane_count in parts],
        [
            pltpu.VMEM((rows_all, width), jnp.int32),
            pltpu.SemaphoreType.DMA((len(parts) + 1,)),
        ],
        vmem=PACK_BYTES,
    )(state.reshape(planes, rows_all, width), mask_x)


def bring_kernel(part, state_ref, mask_ref, after_ref, out):
    row, rows, lane, width = part
    fields, depth, _, _ = state_ref.shape
    for k in range(fields):
        for i in range(depth):
            out[depth * k + i] = state_ref[k, i, row : row + rows, lane : lane + width]
    switches = mask_ref[0, row : row + rows, lane : lane + width]
    out[depth * fields] = switches.astype(jnp.float32)


def bring_part(state, mask_x, part, after):
    fields, depth, _, _ = state.shape
    _, rows, _, width = part
    return call(
        functools.partial(bring_kernel, part),
        "bring_planes",
        0.5,
        [PLACE, PLACE, ANYWHERE],
        PLACE,
        shape_of(depth * fields + 1, rows, width),
    )(state, mask_x, after)


def pass_kernel(depth, pair_ref, after_ref, out_ref):
    planes = pair_ref.shape[0] - 1
    skip = 1 - lax.rem(lax.axis_index("gx"), 2)
    for k in range(planes // depth):
        for i in range(3):
            out_ref[3 * k + i] = pair_ref[depth * k + i + skip * (depth - 3)]
    out_ref[3 * (planes // depth)] = pair_ref[planes]


def pass_part(pair, depth, after):
    planes, rows_y, width = pair.shape
    return call(
        functools.partial(pass_kernel, depth),
        "pass_planes",
        0.5,
        [PLACE, ANYWHERE],
        PLACE,
        shape_of(3 * (planes - 1) // depth + 1, rows_y, width),
    )(pair, after)


def stream_kernel(part, others, *refs):
    (state_ref, pair_ref, far_ref, mask_ref, base_ref), refs = refs[:5], refs[5:]
    if others is None:
        _, out_ref, dq_s, df_s, both_s, alpha_s = refs
        result = out_ref
    else:
        sum_ref, other_refs, refs = refs[0], refs[1 : 1 + len(others)], refs[1 + len(others) :]
        out_ref, dq_s, df_s, both_s, alpha_s, result, sem, other_sem = refs[:8]
        staged = refs[8:]
    fields, depth, _, _ = state_ref.shape
    start, rows_y, start_lane, width = part
    stride = depth
    rank = lax.axis_index("gx")
    even = lax.rem(rank, 2) == 0
    first = rank == 0
    last = rank == lax.axis_size("gx") - 1
    lane_tiles = width // LANES
    faces = depth + 1
    tiles = (rows_y // ROWS) * lane_tiles

    def rows(row, shift):
        return pl.ds(pl.multiple_of(row + shift, ROWS), ROWS)

    def place(number):
        lane = (number % lane_tiles) * LANES
        return (
            (number // lane_tiles) * ROWS,
            pl.ds(pl.multiple_of(lane, LANES), LANES),
            pl.ds(pl.multiple_of(lane + start_lane, LANES), LANES),
        )

    def point(number, carry):
        at, lane, there = place(number)
        row, mine = rows(at, 0), rows(at, start)
        own = [[state_ref[k, i, mine, there] for k in range(5)] for i in range(depth)]
        cells = []
        for i in range(3):
            cells.append(
                [
                    jnp.where(
                        first,
                        own[0][k],
                        jnp.where(
                            even,
                            far_ref[3 * k + i, row, lane],
                            pair_ref[stride * k + stride - 3 + i, row, lane],
                        ),
                    )
                    for k in range(5)
                ]
            )
        cells += own
        for i in range(3):
            cells.append(
                [
                    jnp.where(
                        last,
                        own[depth - 1][k],
                        jnp.where(
                            even,
                            pair_ref[stride * k + i, row, lane],
                            far_ref[3 * k + i, row, lane],
                        ),
                    )
                    for k in range(5)
                ]
            )
        speeds, before = [], None
        for j, q in enumerate(cells):
            flux, pressure, thin, along = flux_of(q, 0)
            speeds.append(speed_of(pressure, thin, along))
            if j > 0:
                for k in range(5):
                    dq_s[number, k, j - 1] = q[k] - cells[j - 1][k]
                    df_s[number, k, j - 1] = flux[k] - before[k]
                    if 3 <= j < 3 + faces:
                        both_s[number, k, j - 3] = flux[k] + before[k]
            before = flux
        pairs = [jnp.maximum(speeds[i], speeds[i + 1]) for i in range(depth + 5)]
        for f in range(faces):
            alpha_s[number, f] = jnp.maximum(jnp.maximum(pairs[f], pairs[f + 2]), pairs[f + 4])
        return carry

    lax.fori_loop(0, tiles, point, 0)

    def faces_of(number, carry):
        at, lane, there = place(number)
        row, mine = rows(at, 0), rows(at, start)
        border = jnp.where(
            even, pair_ref[stride * fields, row, lane], far_ref[3 * fields, row, lane]
        )
        border = jnp.where(last, 0.0, border)
        switches = [mask_ref[i, mine, there] > 0 for i in range(depth)] + [border > 0.0]
        results = []
        for k in range(5):
            dq = [dq_s[number, k, j] for j in range(depth + 5)]
            df = [df_s[number, k, j] for j in range(depth + 5)]
            hats = [
                face_value(
                    dq[f : f + 5], df[f : f + 5], both_s[number, k, f], alpha_s[number, f], switches[f]
                )
                for f in range(faces)
            ]
            for i in range(depth):
                value = base_ref[k, i, mine, there] + FACE_SCALE * (hats[i + 1] - hats[i])
                if others is not None:
                    value = value - TIME_STEP * sum_ref[k, i, mine, there]
                results.append(value)
        for k in range(5):
            for i in range(depth):
                result[k, i, row, lane] = results[k * depth + i]
        if others is not None:
            hand_out(number).start()
        return carry

    def hand_out(number):
        at, lane, there = place(number)
        return pltpu.make_async_copy(
            result.at[:, :, rows(at, 0), lane],
            out_ref.at[:, :, rows(at, start), there],
            sem.at[number],
        )

    def settle(number, carry):
        hand_out(number).wait()
        return carry

    copies = []
    for number, other in enumerate(others or []):
        top, tall, left, wide = other

        def line(index, carry, number=number, top=top, tall=tall, left=left, wide=wide):
            k, i = index // depth, index % depth
            staged[number][k, i] = other_refs[number][k, i] - TIME_STEP * (
                sum_ref[k, i, top : top + tall, left : left + wide]
            )
            return carry

        lax.fori_loop(0, fields * depth, line, 0)
        copy = pltpu.make_async_copy(
            staged[number],
            out_ref.at[:, :, pl.ds(top, tall), pl.ds(left, wide)],
            other_sem.at[number],
        )
        copy.start()
        copies.append(copy)
    lax.fori_loop(0, tiles, faces_of, 0)
    if others is not None:
        lax.fori_loop(0, tiles, settle, 0)
    for copy in copies:
        copy.wait()


def stream_part(state, pair, far, mask_x, part, base, after=None, arrived=None, others=None):
    fields, depth, _, _ = state.shape
    _, rows_y, _, width = part
    tiles = rows_y * width // (ROWS * LANES)

    def vregs(*dims):
        return pltpu.VMEM(dims + (ROWS, LANES), jnp.float32)

    def cells(part):
        return (fields, depth, part[1], part[3])

    scratch = [
        vregs(tiles, fields, depth + 5),
        vregs(tiles, fields, depth + 5),
        vregs(tiles, fields, depth + 1),
        vregs(tiles, depth + 1),
    ]
    inputs = [state, pair, far, mask_x, base]
    places_in = [PLACE] * len(inputs)
    if others is None:
        inputs.append(after)
        places_in.append(ANYWHERE)
        places = None
        target, target_shape = PLACE, shape_of(*cells(part))
    else:
        places = [place for place, _ in others]
        inputs += [arrived] + [array for _, array in others]
        places_in = [PLACE] * len(inputs)
        target, target_shape = HBM, shape_of(*state.shape)
        scratch += [
            pltpu.VMEM(cells(part), jnp.float32),
            pltpu.SemaphoreType.DMA((tiles,)),
            pltpu.SemaphoreType.DMA((len(others),)),
        ] + [pltpu.VMEM(cells(place), jnp.float32) for place in places]
    return call(
        functools.partial(stream_kernel, part, places),
        "stream_faces",
        0.3 * tiles,
        places_in,
        target,
        target_shape,
        scratch,
    )(*inputs)


def circulant_tables(span):
    half = span // 2
    step = 1
    while step * step < half:
        step *= 2
    count = half // step
    places = np.arange(span)
    period = max(2 * count, LANES)
    high = 2.0 * np.pi / span * ((np.arange(count)[:, None] * step * places[None, :period]) % span)
    low = 2.0 * np.pi / span * ((np.arange(step)[:, None] * places[None]) % span)
    tables = [np.concatenate([np.cos(a), np.sin(a)]) for a in (high, low)]
    return step, count, [jnp.asarray(t.astype(np.float32)) for t in tables]


def circulant_kernel(
    count, step, filter_ref, inner_ref, outer_ref, after_ref, high_ref, low_ref, band
):
    period = inner_ref.shape[1]
    span = outer_ref.shape[1]
    tall, wide = high_ref.shape
    order = step * lax.broadcasted_iota(
        jnp.int32, (count, step), 0
    ) + lax.broadcasted_iota(jnp.int32, (count, step), 1)
    scale = 2.0 / span * (2.0 * np.pi / span) * order.astype(jnp.float32) * filter_ref[...]

    def dot(table):
        return lax.dot_general(
            scale,
            table,
            (((0,), (0,)), ((), ())),
            precision=lax.Precision.HIGHEST,
            preferred_element_type=jnp.float32,
        )

    repeat = span // period
    inner_cos = jnp.concatenate([dot(inner_ref[:count])] * repeat, 1)
    inner_sin = jnp.concatenate([dot(inner_ref[count:])] * repeat, 1)
    line = jnp.sum(
        outer_ref[step:] * inner_cos + outer_ref[:step] * inner_sin, axis=0, keepdims=True
    )
    base = jnp.broadcast_to(-line, (ROWS, span))
    place = lax.broadcasted_iota(jnp.int32, (ROWS, span), 0)
    skew = base
    for i in range(1, ROWS):
        skew = jnp.where(place == i, pltpu.roll(base, i, 1), skew)
    for b in range(LANES // ROWS):
        rows = skew if b == 0 else pltpu.roll(skew, b * ROWS, 1)
        for q in range(tall // LANES):
            at = q * LANES + b * ROWS
            first = q * LANES
            if first:
                band[at : at + ROWS, :first] = rows[:, span - first :]
            band[at : at + ROWS, first:span] = rows[:, : span - first]
    full = band[...]
    high = full.astype(jnp.bfloat16)
    low = (full - high.astype(jnp.float32)).astype(jnp.bfloat16)
    high_ref[:, :span] = high
    low_ref[:, :span] = low
    high_ref[:, span:] = high[:, : wide - span]
    low_ref[:, span:] = low[:, : wide - span]


def circulant(span_filter, span, width, after):
    tall = min(256, width)
    step, count, tables = circulant_tables(span)
    band = shape_of(tall, span + width, dtype=jnp.bfloat16)
    return call(
        functools.partial(circulant_kernel, count, step),
        "circulant_band",
        1.0,
        [PLACE, PLACE, PLACE, ANYWHERE],
        [PLACE, PLACE],
        [band, band],
        [pltpu.VMEM((tall, span), jnp.float32)],
    )(span_filter.reshape(count, step), *tables, after)


def fill_lines(shards, x_refs):
    _, depth, rows_y, width = shards[0].shape
    xh, xl = x_refs
    for number, shard in enumerate(shards):

        def plane(index, carry):
            i = index // (width // LANES)
            t = index % (width // LANES)
            flux, _, _, _ = flux_of([shard[k, i, :, lanes(t)] for k in range(5)], 2)
            to = lanes(t + number * (width // LANES))
            for k in range(5):
                high = flux[k].astype(jnp.bfloat16)
                line = pl.ds(pl.multiple_of((k * depth + i) * rows_y, rows_y), rows_y)
                xh[line, to] = high
                xl[line, to] = (flux[k] - high.astype(jnp.float32)).astype(jnp.bfloat16)
            return carry

        lax.fori_loop(0, depth * (width // LANES), plane, 0)


def product(target, sources, high_ref, low_ref, xh, xl, w_s):
    tall, wide = high_ref.shape
    width = xh.shape[1] // len(sources)
    span = wide - width
    deep = xh.shape[1]
    for number, source in enumerate(sources):
        for q in range(width // tall):
            start = lax.rem((target - source) * width - q * tall + 2 * span, span)
            start = pl.multiple_of(start, LANES)
            at = number * width + q * tall
            w_s[at : at + tall, :] = high_ref[:, pl.ds(start, width)]
            w_s[deep + at : deep + at + tall, :] = low_ref[:, pl.ds(start, width)]
    dot = functools.partial(jnp.dot, preferred_element_type=jnp.float32)
    high = w_s[:deep, :]
    return dot(xh[...], high) + dot(xl[...], high) + dot(xh[...], w_s[deep:, :])


def away_kernel(masks, high_ref, low_ref, own_ref, core_ref, *refs):
    sums = refs[: len(masks)]
    xh, xl, w_s = refs[len(masks) :]
    me = lax.axis_index("gz")
    fill_lines([own_ref, core_ref], [xh, xl])
    for mask, sum_ref in zip(masks, sums):
        total = product(me ^ mask, [me, me ^ 1], high_ref, low_ref, xh, xl, w_s)
        sum_ref[...] = total.reshape(own_ref.shape)


def away_part(band, state, core, masks):
    fields, depth, rows_all, width = state.shape
    line = shape_of(fields * depth * rows_all, 2 * width, dtype=jnp.bfloat16)
    outs = call(
        functools.partial(away_kernel, masks),
        "span_away",
        3.0,
        [PLACE] * 4,
        [PLACE] * (len(masks) + 2),
        [shape_of(*state.shape)] * len(masks) + [line, line],
        [pltpu.VMEM((4 * width, width), jnp.bfloat16)],
    )(*band, state, core)
    return outs[: len(masks)], outs[len(masks) :]


def home_kernel(high_ref, low_ref, xh, xl, first_ref, second_ref, after_ref, out_ref, w_s):
    me = lax.axis_index("gz")
    half = first_ref.shape[1]
    total = product(me, [me, me ^ 1], high_ref, low_ref, xh, xl, w_s).reshape(out_ref.shape)
    out_ref[:, :half] = first_ref[...] - TIME_STEP * total[:, :half]
    out_ref[:, half:] = second_ref[...] - TIME_STEP * total[:, half:]


def home_part(band, lines, first, second, after):
    fields, half, rows_all, width = first.shape
    return call(
        home_kernel,
        "span_home",
        2.0,
        [PLACE] * 6 + [ANYWHERE],
        PLACE,
        shape_of(fields, half + second.shape[1], rows_all, width),
        [pltpu.VMEM((4 * width, width), jnp.bfloat16)],
    )(*band, *lines, first, second, after)


def per_device(state, mask_x, mask_y, span_filter):
    fields, depth, rows_all, width = state.shape
    groups = lax.axis_size("gz")
    slabs = lax.axis_size("gx")
    span = width * groups

    def flip(array, bit):
        return lax.ppermute(array, "gz", [(g, g ^ bit) for g in range(groups)])

    swap = [(i, i ^ 1) for i in range(slabs)]
    carry = [(i, i + 2) for i in range(0, slabs - 2, 2)] + [
        (i, i - 2) for i in range(3, slabs, 2)
    ]
    core = flip(state, 1)
    low = rows_all // 2
    if width % (4 * LANES) == 0:
        lane = width // 4
        parts = [
            (0, low, 0, 3 * lane),
            (low, low, 0, 2 * lane),
            (0, rows_all, 3 * lane, lane),
            (low, low, 2 * lane, lane),
        ]
    else:
        parts = [(row, rows_all // 4, 0, width) for row in range(0, rows_all, rows_all // 4)]
    (brick,) = pack_part(state, mask_x, parts[:1])
    pairs = [lax.ppermute(brick, "gx", swap)]
    band = circulant(span_filter, span, width, core)

    masks = list(range(2, groups, 2))
    sums, lines = away_part(band, state, core, masks)
    arrived = sum(flip(part_sum, mask) for part_sum, mask in zip(sums, masks))
    half = depth // 2
    fars, others = [], []

    def exchange(c, after):
        brick = bring_part(state, mask_x, parts[c], after)
        pairs.append(lax.ppermute(brick, "gx", swap))
        return brick

    def hand_on(c, after):
        planes = pass_part(pairs[c], depth, after)
        fars.append(lax.ppermute(planes, "gx", carry))
        return planes

    def stream(c, after):
        done = stream_part(state, pairs[c], fars[c], mask_x, parts[c], base, after)
        others.append((parts[c], done))
        return done

    acc_low = wall_part(state, mask_y, 0, half, lines[0])
    after = hand_on(0, exchange(1, acc_low))
    acc_high = wall_part(state, mask_y, half, depth - half, after)
    after = hand_on(1, exchange(2, acc_high))
    base = home_part(band, lines, acc_low, acc_high, after)
    after = exchange(3, base)
    after = hand_on(2, stream(0, after))
    after = hand_on(3, after)
    stream(2, stream(1, after))
    return stream_part(
        state, pairs[3], fars[3], mask_x, parts[3], base, arrived=arrived, others=others
    )


def solution(mesh):
    return jax.shard_map(
        per_device,
        mesh=mesh,
        in_specs=(P(None, "gx", None, "gz"), P("gx", None, "gz"), P("gx", None, "gz"), P()),
        out_specs=P(None, "gx", None, "gz"),
        check_vma=False,
    )
```

```python
import functools

import jax
import jax.numpy as jnp
import numpy as np
from jax import lax
from jax.experimental import pallas as pl
from jax.experimental.pallas import tpu as pltpu
from jax.sharding import PartitionSpec as P

GAMMA_GAS = 1.4
SMALL_EPS = 1e-06
TIME_STEP = 0.1
ROWS = 8
LANES = 128
VMEM_BYTES = 24 * 1024 * 1024
PACK_BYTES = 60 * 1024 * 1024
FACE_SCALE = -TIME_STEP / 60.0
PLACE = pl.BlockSpec(memory_space=pltpu.VMEM)
ANYWHERE = pl.BlockSpec(memory_space=pl.ANY)
HBM = pl.BlockSpec(memory_space=pltpu.HBM)


def call(kernel, name, weight, ins, outs, out_shape, scratch=(), aliases=None, vmem=VMEM_BYTES):
    return pl.pallas_call(
        kernel,
        out_shape=out_shape,
        in_specs=ins,
        out_specs=outs,
        scratch_shapes=list(scratch),
        input_output_aliases=aliases or {},
        compiler_params=pltpu.CompilerParams(vmem_limit_bytes=vmem),
        cost_estimate=pl.CostEstimate(
            flops=int(weight * 1e9), bytes_accessed=int(weight * 3e6), transcendentals=0
        ),
        name=name,
    )


def shape_of(*dims, dtype=jnp.float32):
    return jax.ShapeDtypeStruct(dims, dtype)


def flux_of(q, normal):
    thin = pl.reciprocal(q[0], approx=True)
    velocity = [q[1] * thin, q[2] * thin, q[3] * thin]
    pressure = (GAMMA_GAS - 1.0) * (
        q[4] - 0.5 * (q[1] * velocity[0] + q[2] * velocity[1] + q[3] * velocity[2])
    )
    along = velocity[normal]
    flux = [q[normal + 1], q[1] * along, q[2] * along, q[3] * along, (q[4] + pressure) * along]
    flux[normal + 1] = flux[normal + 1] + pressure
    return flux, pressure, thin, along


def speed_of(pressure, thin, along):
    return jnp.abs(along) + jnp.sqrt(GAMMA_GAS * pressure * thin)


def weno_rest(d1, d2, d3, d4):
    low = d2 * d2 * 0.609375 + 3.0 * SMALL_EPS
    high = d3 * d3 * 0.609375 + 3.0 * SMALL_EPS
    x0 = d1 - 1.375 * d2
    x1 = d2 - 0.625 * d3
    x2 = d4 - 1.375 * d3
    t0 = low + x0 * x0
    t1 = high + x1 * x1
    t2 = high + x2 * x2
    w0 = t1 * t2
    w1 = t0 * t2
    w2 = t0 * t1
    w0 = w0 * w0
    w1 = w1 * w1
    w2 = w2 * w2 * 1.5
    top = w0 * (x0 + (d3 - 0.625 * d2)) + w2 * (x1 + x2)
    bottom = 0.5 * w0 + 3.0 * w1 + w2
    return top * pl.reciprocal(bottom, approx=True)


def face_value(dq, df, both, alpha, upwind):
    aq = [alpha * value for value in dq]
    plus = [df[k] + aq[k] for k in range(4)]
    minus = [df[k] - aq[k] for k in range(1, 5)]
    bend = df[1] - df[3]
    central = 7.0 * bend + (df[4] - df[0])
    rest = weno_rest(minus[3], minus[2], minus[1], minus[0]) - weno_rest(*plus)
    biased = 5.0 * (bend + (aq[1] + aq[3]) - (aq[2] + aq[2]) + rest)
    return 30.0 * both + jnp.where(upwind, biased, central)


def lanes(number):
    return pl.ds(pl.multiple_of(number * LANES, LANES), LANES)


def wall_kernel(low, state_ref, mask_ref, out_ref, q_s, f_s, speed_s, dq_s, df_s):
    rows_y = state_ref.shape[2]
    width = state_ref.shape[3]
    tiles = rows_y // ROWS
    end = ROWS + rows_y
    zero = jnp.zeros((5, ROWS, LANES), jnp.float32)
    for side in (dq_s, df_s):
        side[:, 0:ROWS, :] = zero
        side[:, end : end + ROWS, :] = zero
    row = lax.broadcasted_iota(jnp.int32, (ROWS, LANES), 0)

    def column(number, carry):
        plane = number // (width // LANES)
        lane = lanes(number % (width // LANES))
        zero_row = jnp.minimum(number, 0)

        def at(r, shift):
            return pl.ds(zero_row + (r * ROWS + ROWS + shift), ROWS)

        def still(r):
            return slice(r * ROWS + ROWS, r * ROWS + 2 * ROWS)

        qs = []
        for r in range(tiles):
            mine = slice(r * ROWS, r * ROWS + ROWS)
            q = [state_ref[k, low + plane, mine, lane] for k in range(5)]
            flux, pressure, thin, along = flux_of(q, 1)
            speed = speed_of(pressure, thin, along)
            for k in range(5):
                q_s[k, still(r), :] = q[k]
                f_s[k, still(r), :] = flux[k]
            speed_s[still(r), :] = speed
            if r == 0:
                for k in range(5):
                    q_s[k, 0:ROWS, :] = jnp.broadcast_to(q[k][0:1], (ROWS, LANES))
                    f_s[k, 0:ROWS, :] = jnp.broadcast_to(flux[k][0:1], (ROWS, LANES))
                speed_s[0:ROWS, :] = jnp.broadcast_to(speed[0:1], (ROWS, LANES))
            if r == tiles - 1:
                speed_s[end : end + ROWS, :] = jnp.broadcast_to(
                    speed[ROWS - 1 : ROWS], (ROWS, LANES)
                )
        for k in range(5):
            changes = [
                (
                    q_s[k, still(r), :] - q_s[k, at(r, -1), :],
                    f_s[k, still(r), :] - f_s[k, at(r, -1), :],
                )
                for r in range(tiles)
            ]
            for r in range(tiles):
                dq_s[k, still(r), :] = changes[r][0]
                df_s[k, still(r), :] = changes[r][1]
        alphas, switches = [], []
        for r in range(tiles):
            alpha = speed_s[still(r), :]
            for shift in (-3, -2, -1, 1, 2):
                alpha = jnp.maximum(alpha, speed_s[at(r, shift), :])
            alphas.append(alpha)
            switches.append(mask_ref[low + plane, r * ROWS : r * ROWS + ROWS, lane] > 0)
        for k in range(5):
            hats = []
            for r in range(tiles):
                dq = [dq_s[k, at(r, s), :] for s in (-2, -1)]
                df = [df_s[k, at(r, s), :] for s in (-2, -1)]
                dq += [dq_s[k, still(r), :]]
                df += [df_s[k, still(r), :]]
                dq += [dq_s[k, at(r, s), :] for s in (1, 2)]
                df += [df_s[k, at(r, s), :] for s in (1, 2)]
                here = f_s[k, still(r), :]
                both = here + here - df[2]
                hats.append(face_value(dq, df, both, alphas[r], switches[r]))
            top = (
                60.0 * f_s[k, end - 1 : end, :]
                + 7.0 * df_s[k, end - 1 : end, :]
                - df_s[k, end - 2 : end - 1, :]
            )
            turned = [pltpu.roll(hat, ROWS - 1, 0) for hat in hats]
            turned.append(jnp.broadcast_to(top, (ROWS, LANES)))
            for r in range(tiles):
                after = jnp.where(row == ROWS - 1, turned[r + 1], turned[r])
                mine = slice(r * ROWS, r * ROWS + ROWS)
                out_ref[k, plane, mine, lane] = q_s[k, still(r), :] + FACE_SCALE * (after - hats[r])
        return carry

    lax.fori_loop(0, out_ref.shape[1] * (width // LANES), column, 0)


def wall_part(state, mask_y, low, count, after):
    fields, depth, rows_y, width = state.shape
    tall = rows_y + 2 * ROWS
    padded = pltpu.VMEM((fields, tall, LANES), jnp.float32)

    def kernel(state_ref, mask_ref, after_ref, out_ref, *scratch):
        wall_kernel(low, state_ref, mask_ref, out_ref, *scratch)

    return call(
        kernel,
        "wall_faces",
        5.0 * count / depth,
        [PLACE, PLACE, ANYWHERE],
        PLACE,
        shape_of(fields, count, rows_y, width),
        [padded, padded, pltpu.VMEM((tall, LANES), jnp.float32), padded, padded],
    )(state, mask_y, after)


def pack_kernel(parts, state_ref, mask_ref, *refs):
    outs = refs[: len(parts)]
    mask_s, sems = refs[len(parts) :]
    planes = state_ref.shape[0]
    mask_copy = pltpu.make_async_copy(mask_ref.at[0], mask_s, sems.at[len(parts)])
    mask_copy.start()
    copies = [
        pltpu.make_async_copy(
            state_ref.at[:, pl.ds(row, rows), pl.ds(lane, width)],
            out.at[pl.ds(0, planes)],
            sems.at[c],
        )
        for c, ((row, rows, lane, width), out) in enumerate(zip(parts, outs))
    ]
    for copy in copies:
        copy.start()
    mask_copy.wait()
    for (row, rows, lane, width), out in zip(parts, outs):
        out[planes] = mask_s[row : row + rows, lane : lane + width].astype(jnp.float32)
    for copy in copies:
        copy.wait()


def pack_part(state, mask_x, parts):
    fields, depth, rows_all, width = state.shape
    planes = fields * depth
    return call(
        functools.partial(pack_kernel, parts),
        "pack_bricks",
        1.0,
        [HBM, HBM],
        [PLACE] * len(parts),
        [shape_of(planes + 1, rows, lane_count) for _, rows, _, lane_count in parts],
        [
            pltpu.VMEM((rows_all, width), jnp.int32),
            pltpu.SemaphoreType.DMA((len(parts) + 1,)),
        ],
        vmem=PACK_BYTES,
    )(state.reshape(planes, rows_all, width), mask_x)


def bring_kernel(part, state_ref, mask_ref, after_ref, out):
    row, rows, lane, width = part
    fields, depth, _, _ = state_ref.shape
    for k in range(fields):
        for i in range(depth):
            out[depth * k + i] = state_ref[k, i, row : row + rows, lane : lane + width]
    switches = mask_ref[0, row : row + rows, lane : lane + width]
    out[depth * fields] = switches.astype(jnp.float32)


def bring_part(state, mask_x, part, after):
    fields, depth, _, _ = state.shape
    _, rows, _, width = part
    return call(
        functools.partial(bring_kernel, part),
        "bring_planes",
        0.5,
        [PLACE, PLACE, ANYWHERE],
        PLACE,
        shape_of(depth * fields + 1, rows, width),
    )(state, mask_x, after)


def pass_kernel(depth, pair_ref, after_ref, out_ref):
    planes = pair_ref.shape[0] - 1
    skip = 1 - lax.rem(lax.axis_index("gx"), 2)
    for k in range(planes // depth):
        for i in range(3):
            out_ref[3 * k + i] = pair_ref[depth * k + i + skip * (depth - 3)]
    out_ref[3 * (planes // depth)] = pair_ref[planes]


def pass_part(pair, depth, after):
    planes, rows_y, width = pair.shape
    return call(
        functools.partial(pass_kernel, depth),
        "pass_planes",
        0.5,
        [PLACE, ANYWHERE],
        PLACE,
        shape_of(3 * (planes - 1) // depth + 1, rows_y, width),
    )(pair, after)


def stream_kernel(part, others, *refs):
    (state_ref, pair_ref, far_ref, mask_ref, base_ref), refs = refs[:5], refs[5:]
    if others is None:
        _, out_ref, dq_s, df_s, both_s, alpha_s = refs
        result = out_ref
    else:
        sum_ref, other_refs, refs = refs[0], refs[1 : 1 + len(others)], refs[1 + len(others) :]
        out_ref, dq_s, df_s, both_s, alpha_s, result, sem, other_sem = refs[:8]
        staged = refs[8:]
    fields, depth, _, _ = state_ref.shape
    start, rows_y, start_lane, width = part
    stride = depth
    rank = lax.axis_index("gx")
    even = lax.rem(rank, 2) == 0
    first = rank == 0
    last = rank == lax.axis_size("gx") - 1
    lane_tiles = width // LANES
    faces = depth + 1
    tiles = (rows_y // ROWS) * lane_tiles

    def rows(row, shift):
        return pl.ds(pl.multiple_of(row + shift, ROWS), ROWS)

    def place(number):
        lane = (number % lane_tiles) * LANES
        return (
            (number // lane_tiles) * ROWS,
            pl.ds(pl.multiple_of(lane, LANES), LANES),
            pl.ds(pl.multiple_of(lane + start_lane, LANES), LANES),
        )

    def point(number, carry):
        at, lane, there = place(number)
        row, mine = rows(at, 0), rows(at, start)
        own = [[state_ref[k, i, mine, there] for k in range(5)] for i in range(depth)]
        cells = []
        for i in range(3):
            cells.append(
                [
                    jnp.where(
                        first,
                        own[0][k],
                        jnp.where(
                            even,
                            far_ref[3 * k + i, row, lane],
                            pair_ref[stride * k + stride - 3 + i, row, lane],
                        ),
                    )
                    for k in range(5)
                ]
            )
        cells += own
        for i in range(3):
            cells.append(
                [
                    jnp.where(
                        last,
                        own[depth - 1][k],
                        jnp.where(
                            even,
                            pair_ref[stride * k + i, row, lane],
                            far_ref[3 * k + i, row, lane],
                        ),
                    )
                    for k in range(5)
                ]
            )
        speeds, before = [], None
        for j, q in enumerate(cells):
            flux, pressure, thin, along = flux_of(q, 0)
            speeds.append(speed_of(pressure, thin, along))
            if j > 0:
                for k in range(5):
                    dq_s[number, k, j - 1] = q[k] - cells[j - 1][k]
                    df_s[number, k, j - 1] = flux[k] - before[k]
                    if 3 <= j < 3 + faces:
                        both_s[number, k, j - 3] = flux[k] + before[k]
            before = flux
        pairs = [jnp.maximum(speeds[i], speeds[i + 1]) for i in range(depth + 5)]
        for f in range(faces):
            alpha_s[number, f] = jnp.maximum(jnp.maximum(pairs[f], pairs[f + 2]), pairs[f + 4])
        return carry

    lax.fori_loop(0, tiles, point, 0)

    def faces_of(number, carry):
        at, lane, there = place(number)
        row, mine = rows(at, 0), rows(at, start)
        border = jnp.where(
            even, pair_ref[stride * fields, row, lane], far_ref[3 * fields, row, lane]
        )
        border = jnp.where(last, 0.0, border)
        switches = [mask_ref[i, mine, there] > 0 for i in range(depth)] + [border > 0.0]
        results = []
        for k in range(5):
            dq = [dq_s[number, k, j] for j in range(depth + 5)]
            df = [df_s[number, k, j] for j in range(depth + 5)]
            hats = [
                face_value(
                    dq[f : f + 5], df[f : f + 5], both_s[number, k, f], alpha_s[number, f], switches[f]
                )
                for f in range(faces)
            ]
            for i in range(depth):
                value = base_ref[k, i, mine, there] + FACE_SCALE * (hats[i + 1] - hats[i])
                if others is not None:
                    value = value - TIME_STEP * sum_ref[k, i, mine, there]
                results.append(value)
        for k in range(5):
            for i in range(depth):
                result[k, i, row, lane] = results[k * depth + i]
        if others is not None:
            hand_out(number).start()
        return carry

    def hand_out(number):
        at, lane, there = place(number)
        return pltpu.make_async_copy(
            result.at[:, :, rows(at, 0), lane],
            out_ref.at[:, :, rows(at, start), there],
            sem.at[number],
        )

    def settle(number, carry):
        hand_out(number).wait()
        return carry

    copies = []
    for number, other in enumerate(others or []):
        top, tall, left, wide = other

        def line(index, carry, number=number, top=top, tall=tall, left=left, wide=wide):
            k, i = index // depth, index % depth
            staged[number][k, i] = other_refs[number][k, i] - TIME_STEP * (
                sum_ref[k, i, top : top + tall, left : left + wide]
            )
            return carry

        lax.fori_loop(0, fields * depth, line, 0)
        copy = pltpu.make_async_copy(
            staged[number],
            out_ref.at[:, :, pl.ds(top, tall), pl.ds(left, wide)],
            other_sem.at[number],
        )
        copy.start()
        copies.append(copy)
    lax.fori_loop(0, tiles, faces_of, 0)
    if others is not None:
        lax.fori_loop(0, tiles, settle, 0)
    for copy in copies:
        copy.wait()


def stream_part(state, pair, far, mask_x, part, base, after=None, arrived=None, others=None):
    fields, depth, _, _ = state.shape
    _, rows_y, _, width = part
    tiles = rows_y * width // (ROWS * LANES)

    def vregs(*dims):
        return pltpu.VMEM(dims + (ROWS, LANES), jnp.float32)

    def cells(part):
        return (fields, depth, part[1], part[3])

    scratch = [
        vregs(tiles, fields, depth + 5),
        vregs(tiles, fields, depth + 5),
        vregs(tiles, fields, depth + 1),
        vregs(tiles, depth + 1),
    ]
    inputs = [state, pair, far, mask_x, base]
    places_in = [PLACE] * len(inputs)
    if others is None:
        inputs.append(after)
        places_in.append(ANYWHERE)
        places = None
        target, target_shape = PLACE, shape_of(*cells(part))
    else:
        places = [place for place, _ in others]
        inputs += [arrived] + [array for _, array in others]
        places_in = [PLACE] * len(inputs)
        target, target_shape = HBM, shape_of(*state.shape)
        scratch += [
            pltpu.VMEM(cells(part), jnp.float32),
            pltpu.SemaphoreType.DMA((tiles,)),
            pltpu.SemaphoreType.DMA((len(others),)),
        ] + [pltpu.VMEM(cells(place), jnp.float32) for place in places]
    return call(
        functools.partial(stream_kernel, part, places),
        "stream_faces",
        0.3 * tiles,
        places_in,
        target,
        target_shape,
        scratch,
    )(*inputs)


def circulant_tables(span):
    half = span // 2
    step = 1
    while step * step < half:
        step *= 2
    count = half // step
    places = np.arange(span)
    period = max(2 * count, LANES)
    high = 2.0 * np.pi / span * ((np.arange(count)[:, None] * step * places[None, :period]) % span)
    low = 2.0 * np.pi / span * ((np.arange(step)[:, None] * places[None]) % span)
    tables = [np.concatenate([np.cos(a), np.sin(a)]) for a in (high, low)]
    return step, count, [jnp.asarray(t.astype(np.float32)) for t in tables]


def circulant_kernel(
    count, step, filter_ref, inner_ref, outer_ref, after_ref, high_ref, low_ref, band
):
    period = inner_ref.shape[1]
    span = outer_ref.shape[1]
    tall, wide = high_ref.shape
    order = step * lax.broadcasted_iota(
        jnp.int32, (count, step), 0
    ) + lax.broadcasted_iota(jnp.int32, (count, step), 1)
    scale = 2.0 / span * (2.0 * np.pi / span) * order.astype(jnp.float32) * filter_ref[...]

    def dot(table):
        return lax.dot_general(
            scale,
            table,
            (((0,), (0,)), ((), ())),
            precision=lax.Precision.HIGHEST,
            preferred_element_type=jnp.float32,
        )

    repeat = span // period
    inner_cos = jnp.concatenate([dot(inner_ref[:count])] * repeat, 1)
    inner_sin = jnp.concatenate([dot(inner_ref[count:])] * repeat, 1)
    line = jnp.sum(
        outer_ref[step:] * inner_cos + outer_ref[:step] * inner_sin, axis=0, keepdims=True
    )
    base = jnp.broadcast_to(-line, (ROWS, span))
    place = lax.broadcasted_iota(jnp.int32, (ROWS, span), 0)
    skew = base
    for i in range(1, ROWS):
        skew = jnp.where(place == i, pltpu.roll(base, i, 1), skew)
    for b in range(LANES // ROWS):
        rows = skew if b == 0 else pltpu.roll(skew, b * ROWS, 1)
        for q in range(tall // LANES):
            at = q * LANES + b * ROWS
            first = q * LANES
            if first:
                band[at : at + ROWS, :first] = rows[:, span - first :]
            band[at : at + ROWS, first:span] = rows[:, : span - first]
    full = band[...]
    high = full.astype(jnp.bfloat16)
    low = (full - high.astype(jnp.float32)).astype(jnp.bfloat16)
    high_ref[:, :span] = high
    low_ref[:, :span] = low
    high_ref[:, span:] = high[:, : wide - span]
    low_ref[:, span:] = low[:, : wide - span]


def circulant(span_filter, span, width, after):
    tall = min(256, width)
    step, count, tables = circulant_tables(span)
    band = shape_of(tall, span + width, dtype=jnp.bfloat16)
    return call(
        functools.partial(circulant_kernel, count, step),
        "circulant_band",
        1.0,
        [PLACE, PLACE, PLACE, ANYWHERE],
        [PLACE, PLACE],
        [band, band],
        [pltpu.VMEM((tall, span), jnp.float32)],
    )(span_filter.reshape(count, step), *tables, after)


def fill_lines(shards, x_refs):
    _, depth, rows_y, width = shards[0].shape
    xh, xl = x_refs
    for number, shard in enumerate(shards):

        def plane(index, carry):
            i = index // (width // LANES)
            t = index % (width // LANES)
            flux, _, _, _ = flux_of([shard[k, i, :, lanes(t)] for k in range(5)], 2)
            to = lanes(t + number * (width // LANES))
            for k in range(5):
                high = flux[k].astype(jnp.bfloat16)
                line = pl.ds(pl.multiple_of((k * depth + i) * rows_y, rows_y), rows_y)
                xh[line, to] = high
                xl[line, to] = (flux[k] - high.astype(jnp.float32)).astype(jnp.bfloat16)
            return carry

        lax.fori_loop(0, depth * (width // LANES), plane, 0)


def product(target, sources, high_ref, low_ref, xh, xl, w_s):
    tall, wide = high_ref.shape
    width = xh.shape[1] // len(sources)
    span = wide - width
    deep = xh.shape[1]
    for number, source in enumerate(sources):
        for q in range(width // tall):
            start = lax.rem((target - source) * width - q * tall + 2 * span, span)
            start = pl.multiple_of(start, LANES)
            at = number * width + q * tall
            w_s[at : at + tall, :] = high_ref[:, pl.ds(start, width)]
            w_s[deep + at : deep + at + tall, :] = low_ref[:, pl.ds(start, width)]
    dot = functools.partial(jnp.dot, preferred_element_type=jnp.float32)
    high = w_s[:deep, :]
    return dot(xh[...], high) + dot(xl[...], high) + dot(xh[...], w_s[deep:, :])


def away_kernel(masks, high_ref, low_ref, own_ref, core_ref, *refs):
    sums = refs[: len(masks)]
    xh, xl, w_s = refs[len(masks) :]
    me = lax.axis_index("gz")
    fill_lines([own_ref, core_ref], [xh, xl])
    for mask, sum_ref in zip(masks, sums):
        total = product(me ^ mask, [me, me ^ 1], high_ref, low_ref, xh, xl, w_s)
        sum_ref[...] = total.reshape(own_ref.shape)


def away_part(band, state, core, masks):
    fields, depth, rows_all, width = state.shape
    line = shape_of(fields * depth * rows_all, 2 * width, dtype=jnp.bfloat16)
    outs = call(
        functools.partial(away_kernel, masks),
        "span_away",
        3.0,
        [PLACE] * 4,
        [PLACE] * (len(masks) + 2),
        [shape_of(*state.shape)] * len(masks) + [line, line],
        [pltpu.VMEM((4 * width, width), jnp.bfloat16)],
    )(*band, state, core)
    return outs[: len(masks)], outs[len(masks) :]


def home_kernel(high_ref, low_ref, xh, xl, first_ref, second_ref, after_ref, out_ref, w_s):
    me = lax.axis_index("gz")
    half = first_ref.shape[1]
    total = product(me, [me, me ^ 1], high_ref, low_ref, xh, xl, w_s).reshape(out_ref.shape)
    out_ref[:, :half] = first_ref[...] - TIME_STEP * total[:, :half]
    out_ref[:, half:] = second_ref[...] - TIME_STEP * total[:, half:]


def home_part(band, lines, first, second, after):
    fields, half, rows_all, width = first.shape
    return call(
        home_kernel,
        "span_home",
        2.0,
        [PLACE] * 6 + [ANYWHERE],
        PLACE,
        shape_of(fields, half + second.shape[1], rows_all, width),
        [pltpu.VMEM((4 * width, width), jnp.bfloat16)],
    )(*band, *lines, first, second, after)


def per_device(state, mask_x, mask_y, span_filter):
    fields, depth, rows_all, width = state.shape
    groups = lax.axis_size("gz")
    slabs = lax.axis_size("gx")
    span = width * groups

    def flip(array, bit):
        return lax.ppermute(array, "gz", [(g, g ^ bit) for g in range(groups)])

    swap = [(i, i ^ 1) for i in range(slabs)]
    carry = [(i, i + 2) for i in range(0, slabs - 2, 2)] + [
        (i, i - 2) for i in range(3, slabs, 2)
    ]
    core = flip(state, 1)
    low = rows_all // 2
    if width % (4 * LANES) == 0:
        lane = width // 4
        parts = [
            (0, low, 0, 3 * lane),
            (low, low, 0, 2 * lane),
            (0, rows_all, 3 * lane, lane),
            (low, low, 2 * lane, lane),
        ]
    else:
        parts = [(row, rows_all // 4, 0, width) for row in range(0, rows_all, rows_all // 4)]
    (brick,) = pack_part(state, mask_x, parts[:1])
    pairs = [lax.ppermute(brick, "gx", swap)]
    band = circulant(span_filter, span, width, core)

    masks = list(range(2, groups, 2))
    sums, lines = away_part(band, state, core, masks)
    arrived = sum(flip(part_sum, mask) for part_sum, mask in zip(sums, masks))
    half = depth // 2
    fars, others = [], []

    def exchange(c, after):
        brick = bring_part(state, mask_x, parts[c], after)
        pairs.append(lax.ppermute(brick, "gx", swap))
        return brick

    def hand_on(c, after):
        planes = pass_part(pairs[c], depth, after)
        fars.append(lax.ppermute(planes, "gx", carry))
        return planes

    def stream(c, after):
        done = stream_part(state, pairs[c], fars[c], mask_x, parts[c], base, after)
        others.append((parts[c], done))
        return done

    acc_low = wall_part(state, mask_y, 0, half, lines[0])
    after = exchange(1, acc_low)
    acc_high = wall_part(state, mask_y, half, depth - half, after)
    after = exchange(2, hand_on(0, acc_high))
    base = home_part(band, lines, acc_low, acc_high, after)
    after = exchange(3, hand_on(1, base))
    after = hand_on(2, stream(0, after))
    after = hand_on(3, after)
    stream(2, stream(1, after))
    return stream_part(
        state, pairs[3], fars[3], mask_x, parts[3], base, arrived=arrived, others=others
    )


def solution(mesh):
    return jax.shard_map(
        per_device,
        mesh=mesh,
        in_specs=(P(None, "gx", None, "gz"), P("gx", None, "gz"), P("gx", None, "gz"), P()),
        out_specs=P(None, "gx", None, "gz"),
        check_vma=False,
    )
```

```python
import functools

import jax
import jax.numpy as jnp
import numpy as np
from jax import lax
from jax.experimental import pallas as pl
from jax.experimental.pallas import tpu as pltpu
from jax.sharding import PartitionSpec as P

GAMMA_GAS = 1.4
SMALL_EPS = 1e-06
TIME_STEP = 0.1
ROWS = 8
LANES = 128
VMEM_BYTES = 24 * 1024 * 1024
FACE_SCALE = -TIME_STEP / 60.0
PLACE = pl.BlockSpec(memory_space=pltpu.VMEM)
ANYWHERE = pl.BlockSpec(memory_space=pl.ANY)
HBM = pl.BlockSpec(memory_space=pltpu.HBM)


def call(kernel, name, weight, ins, outs, out_shape, scratch=(), aliases=None):
    return pl.pallas_call(
        kernel,
        out_shape=out_shape,
        in_specs=ins,
        out_specs=outs,
        scratch_shapes=list(scratch),
        input_output_aliases=aliases or {},
        compiler_params=pltpu.CompilerParams(vmem_limit_bytes=VMEM_BYTES),
        cost_estimate=pl.CostEstimate(
            flops=int(weight * 1e9), bytes_accessed=int(weight * 3e6), transcendentals=0
        ),
        name=name,
    )


def shape_of(*dims, dtype=jnp.float32):
    return jax.ShapeDtypeStruct(dims, dtype)


def flux_of(q, normal):
    thin = pl.reciprocal(q[0], approx=True)
    velocity = [q[1] * thin, q[2] * thin, q[3] * thin]
    pressure = (GAMMA_GAS - 1.0) * (
        q[4] - 0.5 * (q[1] * velocity[0] + q[2] * velocity[1] + q[3] * velocity[2])
    )
    along = velocity[normal]
    flux = [q[normal + 1], q[1] * along, q[2] * along, q[3] * along, (q[4] + pressure) * along]
    flux[normal + 1] = flux[normal + 1] + pressure
    return flux, pressure, thin, along


def speed_of(pressure, thin, along):
    return jnp.abs(along) + jnp.sqrt(GAMMA_GAS * pressure * thin)


def weno_rest(d1, d2, d3, d4):
    low = d2 * d2 * 0.609375 + 3.0 * SMALL_EPS
    high = d3 * d3 * 0.609375 + 3.0 * SMALL_EPS
    x0 = d1 - 1.375 * d2
    x1 = d2 - 0.625 * d3
    x2 = d4 - 1.375 * d3
    t0 = low + x0 * x0
    t1 = high + x1 * x1
    t2 = high + x2 * x2
    w0 = t1 * t2
    w1 = t0 * t2
    w2 = t0 * t1
    w0 = w0 * w0
    w1 = w1 * w1
    w2 = w2 * w2 * 1.5
    top = w0 * (x0 + (d3 - 0.625 * d2)) + w2 * (x1 + x2)
    bottom = 0.5 * w0 + 3.0 * w1 + w2
    return top * pl.reciprocal(bottom, approx=True)


def face_value(dq, df, both, alpha, upwind):
    aq = [alpha * value for value in dq]
    plus = [df[k] + aq[k] for k in range(4)]
    minus = [df[k] - aq[k] for k in range(1, 5)]
    bend = df[1] - df[3]
    central = 7.0 * bend + (df[4] - df[0])
    rest = weno_rest(minus[3], minus[2], minus[1], minus[0]) - weno_rest(*plus)
    biased = 5.0 * (bend + (aq[1] + aq[3]) - (aq[2] + aq[2]) + rest)
    return 30.0 * both + jnp.where(upwind, biased, central)


def lanes(number):
    return pl.ds(pl.multiple_of(number * LANES, LANES), LANES)


def wall_kernel(low, state_ref, mask_ref, out_ref, q_s, f_s, speed_s, dq_s, df_s):
    rows_y = state_ref.shape[2]
    width = state_ref.shape[3]
    tiles = rows_y // ROWS
    end = ROWS + rows_y
    zero = jnp.zeros((5, ROWS, LANES), jnp.float32)
    for side in (dq_s, df_s):
        side[:, 0:ROWS, :] = zero
        side[:, end : end + ROWS, :] = zero
    row = lax.broadcasted_iota(jnp.int32, (ROWS, LANES), 0)

    def column(number, carry):
        plane = number // (width // LANES)
        lane = lanes(number % (width // LANES))
        zero_row = jnp.minimum(number, 0)

        def at(r, shift):
            return pl.ds(zero_row + (r * ROWS + ROWS + shift), ROWS)

        def still(r):
            return slice(r * ROWS + ROWS, r * ROWS + 2 * ROWS)

        qs = []
        for r in range(tiles):
            mine = slice(r * ROWS, r * ROWS + ROWS)
            q = [state_ref[k, low + plane, mine, lane] for k in range(5)]
            flux, pressure, thin, along = flux_of(q, 1)
            speed = speed_of(pressure, thin, along)
            for k in range(5):
                q_s[k, still(r), :] = q[k]
                f_s[k, still(r), :] = flux[k]
            speed_s[still(r), :] = speed
            if r == 0:
                for k in range(5):
                    q_s[k, 0:ROWS, :] = jnp.broadcast_to(q[k][0:1], (ROWS, LANES))
                    f_s[k, 0:ROWS, :] = jnp.broadcast_to(flux[k][0:1], (ROWS, LANES))
                speed_s[0:ROWS, :] = jnp.broadcast_to(speed[0:1], (ROWS, LANES))
            if r == tiles - 1:
                speed_s[end : end + ROWS, :] = jnp.broadcast_to(
                    speed[ROWS - 1 : ROWS], (ROWS, LANES)
                )
        for k in range(5):
            changes = [
                (
                    q_s[k, still(r), :] - q_s[k, at(r, -1), :],
                    f_s[k, still(r), :] - f_s[k, at(r, -1), :],
                )
                for r in range(tiles)
            ]
            for r in range(tiles):
                dq_s[k, still(r), :] = changes[r][0]
                df_s[k, still(r), :] = changes[r][1]
        alphas, switches = [], []
        for r in range(tiles):
            alpha = speed_s[still(r), :]
            for shift in (-3, -2, -1, 1, 2):
                alpha = jnp.maximum(alpha, speed_s[at(r, shift), :])
            alphas.append(alpha)
            switches.append(mask_ref[low + plane, r * ROWS : r * ROWS + ROWS, lane] > 0)
        for k in range(5):
            hats = []
            for r in range(tiles):
                dq = [dq_s[k, at(r, s), :] for s in (-2, -1)]
                df = [df_s[k, at(r, s), :] for s in (-2, -1)]
                dq += [dq_s[k, still(r), :]]
                df += [df_s[k, still(r), :]]
                dq += [dq_s[k, at(r, s), :] for s in (1, 2)]
                df += [df_s[k, at(r, s), :] for s in (1, 2)]
                here = f_s[k, still(r), :]
                both = here + here - df[2]
                hats.append(face_value(dq, df, both, alphas[r], switches[r]))
            top = (
                60.0 * f_s[k, end - 1 : end, :]
                + 7.0 * df_s[k, end - 1 : end, :]
                - df_s[k, end - 2 : end - 1, :]
            )
            turned = [pltpu.roll(hat, ROWS - 1, 0) for hat in hats]
            turned.append(jnp.broadcast_to(top, (ROWS, LANES)))
            for r in range(tiles):
                after = jnp.where(row == ROWS - 1, turned[r + 1], turned[r])
                mine = slice(r * ROWS, r * ROWS + ROWS)
                out_ref[k, plane, mine, lane] = q_s[k, still(r), :] + FACE_SCALE * (after - hats[r])
        return carry

    lax.fori_loop(0, out_ref.shape[1] * (width // LANES), column, 0)


def wall_part(state, mask_y, low, count, after):
    fields, depth, rows_y, width = state.shape
    tall = rows_y + 2 * ROWS
    padded = pltpu.VMEM((fields, tall, LANES), jnp.float32)

    def kernel(state_ref, mask_ref, after_ref, out_ref, *scratch):
        wall_kernel(low, state_ref, mask_ref, out_ref, *scratch)

    return call(
        kernel,
        "wall_faces",
        5.0 * count / depth,
        [PLACE, PLACE, ANYWHERE],
        PLACE,
        shape_of(fields, count, rows_y, width),
        [padded, padded, pltpu.VMEM((tall, LANES), jnp.float32), padded, padded],
    )(state, mask_y, after)


def bring_kernel(part, state_ref, mask_ref, after_ref, out):
    row, rows, lane, width = part
    fields, depth, _, _ = state_ref.shape
    for k in range(fields):
        for i in range(depth):
            out[depth * k + i] = state_ref[k, i, row : row + rows, lane : lane + width]
    switches = mask_ref[0, row : row + rows, lane : lane + width]
    out[depth * fields] = switches.astype(jnp.float32)


def bring_part(state, mask_x, part, after):
    fields, depth, _, _ = state.shape
    _, rows, _, width = part
    return call(
        functools.partial(bring_kernel, part),
        "bring_planes",
        0.5,
        [PLACE, PLACE, ANYWHERE],
        PLACE,
        shape_of(depth * fields + 1, rows, width),
    )(state, mask_x, after)


def pass_kernel(depth, pair_ref, after_ref, out_ref):
    planes = pair_ref.shape[0] - 1
    skip = 1 - lax.rem(lax.axis_index("gx"), 2)
    for k in range(planes // depth):
        for i in range(3):
            out_ref[3 * k + i] = pair_ref[depth * k + i + skip * (depth - 3)]
    out_ref[3 * (planes // depth)] = pair_ref[planes]


def pass_part(pair, depth, after):
    planes, rows_y, width = pair.shape
    return call(
        functools.partial(pass_kernel, depth),
        "pass_planes",
        0.5,
        [PLACE, ANYWHERE],
        PLACE,
        shape_of(3 * (planes - 1) // depth + 1, rows_y, width),
    )(pair, after)


def stream_kernel(part, others, *refs):
    (state_ref, pair_ref, far_ref, mask_ref, base_ref), refs = refs[:5], refs[5:]
    if others is None:
        _, out_ref, dq_s, df_s, both_s, alpha_s = refs
        result = out_ref
    else:
        sum_ref, other_refs, refs = refs[0], refs[1 : 1 + len(others)], refs[1 + len(others) :]
        out_ref, dq_s, df_s, both_s, alpha_s, result, sem, other_sem = refs[:8]
        staged = refs[8:]
    fields, depth, _, _ = state_ref.shape
    start, rows_y, start_lane, width = part
    stride = depth
    rank = lax.axis_index("gx")
    even = lax.rem(rank, 2) == 0
    first = rank == 0
    last = rank == lax.axis_size("gx") - 1
    lane_tiles = width // LANES
    faces = depth + 1
    tiles = (rows_y // ROWS) * lane_tiles

    def rows(row, shift):
        return pl.ds(pl.multiple_of(row + shift, ROWS), ROWS)

    def place(number):
        lane = (number % lane_tiles) * LANES
        return (
            (number // lane_tiles) * ROWS,
            pl.ds(pl.multiple_of(lane, LANES), LANES),
            pl.ds(pl.multiple_of(lane + start_lane, LANES), LANES),
        )

    def point(number, carry):
        at, lane, there = place(number)
        row, mine = rows(at, 0), rows(at, start)
        own = [[state_ref[k, i, mine, there] for k in range(5)] for i in range(depth)]
        cells = []
        for i in range(3):
            cells.append(
                [
                    jnp.where(
                        first,
                        own[0][k],
                        jnp.where(
                            even,
                            far_ref[3 * k + i, row, lane],
                            pair_ref[stride * k + stride - 3 + i, row, lane],
                        ),
                    )
                    for k in range(5)
                ]
            )
        cells += own
        for i in range(3):
            cells.append(
                [
                    jnp.where(
                        last,
                        own[depth - 1][k],
                        jnp.where(
                            even,
                            pair_ref[stride * k + i, row, lane],
                            far_ref[3 * k + i, row, lane],
                        ),
                    )
                    for k in range(5)
                ]
            )
        speeds, before = [], None
        for j, q in enumerate(cells):
            flux, pressure, thin, along = flux_of(q, 0)
            speeds.append(speed_of(pressure, thin, along))
            if j > 0:
                for k in range(5):
                    dq_s[number, k, j - 1] = q[k] - cells[j - 1][k]
                    df_s[number, k, j - 1] = flux[k] - before[k]
                    if 3 <= j < 3 + faces:
                        both_s[number, k, j - 3] = flux[k] + before[k]
            before = flux
        pairs = [jnp.maximum(speeds[i], speeds[i + 1]) for i in range(depth + 5)]
        for f in range(faces):
            alpha_s[number, f] = jnp.maximum(jnp.maximum(pairs[f], pairs[f + 2]), pairs[f + 4])
        return carry

    lax.fori_loop(0, tiles, point, 0)

    def faces_of(number, carry):
        at, lane, there = place(number)
        row, mine = rows(at, 0), rows(at, start)
        border = jnp.where(
            even, pair_ref[stride * fields, row, lane], far_ref[3 * fields, row, lane]
        )
        border = jnp.where(last, 0.0, border)
        switches = [mask_ref[i, mine, there] > 0 for i in range(depth)] + [border > 0.0]
        results = []
        for k in range(5):
            dq = [dq_s[number, k, j] for j in range(depth + 5)]
            df = [df_s[number, k, j] for j in range(depth + 5)]
            hats = [
                face_value(
                    dq[f : f + 5], df[f : f + 5], both_s[number, k, f], alpha_s[number, f], switches[f]
                )
                for f in range(faces)
            ]
            for i in range(depth):
                value = base_ref[k, i, mine, there] + FACE_SCALE * (hats[i + 1] - hats[i])
                if others is not None:
                    value = value - TIME_STEP * sum_ref[k, i, mine, there]
                results.append(value)
        for k in range(5):
            for i in range(depth):
                result[k, i, row, lane] = results[k * depth + i]
        if others is not None:
            hand_out(number).start()
        return carry

    def hand_out(number):
        at, lane, there = place(number)
        return pltpu.make_async_copy(
            result.at[:, :, rows(at, 0), lane],
            out_ref.at[:, :, rows(at, start), there],
            sem.at[number],
        )

    def settle(number, carry):
        hand_out(number).wait()
        return carry

    copies = []
    for number, other in enumerate(others or []):
        top, tall, left, wide = other

        def line(index, carry, number=number, top=top, tall=tall, left=left, wide=wide):
            k, i = index // depth, index % depth
            staged[number][k, i] = other_refs[number][k, i] - TIME_STEP * (
                sum_ref[k, i, top : top + tall, left : left + wide]
            )
            return carry

        lax.fori_loop(0, fields * depth, line, 0)
        copy = pltpu.make_async_copy(
            staged[number],
            out_ref.at[:, :, pl.ds(top, tall), pl.ds(left, wide)],
            other_sem.at[number],
        )
        copy.start()
        copies.append(copy)
    lax.fori_loop(0, tiles, faces_of, 0)
    if others is not None:
        lax.fori_loop(0, tiles, settle, 0)
    for copy in copies:
        copy.wait()


def stream_part(state, pair, far, mask_x, part, base, after=None, arrived=None, others=None):
    fields, depth, _, _ = state.shape
    _, rows_y, _, width = part
    tiles = rows_y * width // (ROWS * LANES)

    def vregs(*dims):
        return pltpu.VMEM(dims + (ROWS, LANES), jnp.float32)

    def cells(part):
        return (fields, depth, part[1], part[3])

    scratch = [
        vregs(tiles, fields, depth + 5),
        vregs(tiles, fields, depth + 5),
        vregs(tiles, fields, depth + 1),
        vregs(tiles, depth + 1),
    ]
    inputs = [state, pair, far, mask_x, base]
    places_in = [PLACE] * len(inputs)
    if others is None:
        inputs.append(after)
        places_in.append(ANYWHERE)
        places = None
        target, target_shape = PLACE, shape_of(*cells(part))
    else:
        places = [place for place, _ in others]
        inputs += [arrived] + [array for _, array in others]
        places_in = [PLACE] * len(inputs)
        target, target_shape = HBM, shape_of(*state.shape)
        scratch += [
            pltpu.VMEM(cells(part), jnp.float32),
            pltpu.SemaphoreType.DMA((tiles,)),
            pltpu.SemaphoreType.DMA((len(others),)),
        ] + [pltpu.VMEM(cells(place), jnp.float32) for place in places]
    return call(
        functools.partial(stream_kernel, part, places),
        "stream_faces",
        0.3 * tiles,
        places_in,
        target,
        target_shape,
        scratch,
    )(*inputs)


def circulant_tables(span):
    half = span // 2
    step = 1
    while step * step < half:
        step *= 2
    count = half // step
    places = np.arange(span)
    period = max(2 * count, LANES)
    high = 2.0 * np.pi / span * ((np.arange(count)[:, None] * step * places[None, :period]) % span)
    low = 2.0 * np.pi / span * ((np.arange(step)[:, None] * places[None]) % span)
    tables = [np.concatenate([np.cos(a), np.sin(a)]) for a in (high, low)]
    return step, count, [jnp.asarray(t.astype(np.float32)) for t in tables]


def circulant_kernel(
    count, step, filter_ref, inner_ref, outer_ref, after_ref, high_ref, low_ref, band
):
    period = inner_ref.shape[1]
    span = outer_ref.shape[1]
    tall, wide = high_ref.shape
    order = step * lax.broadcasted_iota(
        jnp.int32, (count, step), 0
    ) + lax.broadcasted_iota(jnp.int32, (count, step), 1)
    scale = 2.0 / span * (2.0 * np.pi / span) * order.astype(jnp.float32) * filter_ref[...]

    def dot(table):
        return lax.dot_general(
            scale,
            table,
            (((0,), (0,)), ((), ())),
            precision=lax.Precision.HIGHEST,
            preferred_element_type=jnp.float32,
        )

    repeat = span // period
    inner_cos = jnp.concatenate([dot(inner_ref[:count])] * repeat, 1)
    inner_sin = jnp.concatenate([dot(inner_ref[count:])] * repeat, 1)
    line = jnp.sum(
        outer_ref[step:] * inner_cos + outer_ref[:step] * inner_sin, axis=0, keepdims=True
    )
    base = jnp.broadcast_to(-line, (ROWS, span))
    place = lax.broadcasted_iota(jnp.int32, (ROWS, span), 0)
    skew = base
    for i in range(1, ROWS):
        skew = jnp.where(place == i, pltpu.roll(base, i, 1), skew)
    for b in range(LANES // ROWS):
        rows = skew if b == 0 else pltpu.roll(skew, b * ROWS, 1)
        for q in range(tall // LANES):
            at = q * LANES + b * ROWS
            first = q * LANES
            if first:
                band[at : at + ROWS, :first] = rows[:, span - first :]
            band[at : at + ROWS, first:span] = rows[:, : span - first]
    full = band[...]
    high = full.astype(jnp.bfloat16)
    low = (full - high.astype(jnp.float32)).astype(jnp.bfloat16)
    high_ref[:, :span] = high
    low_ref[:, :span] = low
    high_ref[:, span:] = high[:, : wide - span]
    low_ref[:, span:] = low[:, : wide - span]


def circulant(span_filter, span, width, after):
    tall = min(256, width)
    step, count, tables = circulant_tables(span)
    band = shape_of(tall, span + width, dtype=jnp.bfloat16)
    return call(
        functools.partial(circulant_kernel, count, step),
        "circulant_band",
        1.0,
        [PLACE, PLACE, PLACE, ANYWHERE],
        [PLACE, PLACE],
        [band, band],
        [pltpu.VMEM((tall, span), jnp.float32)],
    )(span_filter.reshape(count, step), *tables, after)


def fill_lines(shards, x_refs):
    _, depth, rows_y, width = shards[0].shape
    xh, xl = x_refs
    for number, shard in enumerate(shards):

        def plane(index, carry):
            i = index // (width // LANES)
            t = index % (width // LANES)
            flux, _, _, _ = flux_of([shard[k, i, :, lanes(t)] for k in range(5)], 2)
            to = lanes(t + number * (width // LANES))
            for k in range(5):
                high = flux[k].astype(jnp.bfloat16)
                line = pl.ds(pl.multiple_of((k * depth + i) * rows_y, rows_y), rows_y)
                xh[line, to] = high
                xl[line, to] = (flux[k] - high.astype(jnp.float32)).astype(jnp.bfloat16)
            return carry

        lax.fori_loop(0, depth * (width // LANES), plane, 0)


def product(target, sources, high_ref, low_ref, xh, xl, w_s):
    tall, wide = high_ref.shape
    width = xh.shape[1] // len(sources)
    span = wide - width
    deep = xh.shape[1]
    for number, source in enumerate(sources):
        for q in range(width // tall):
            start = lax.rem((target - source) * width - q * tall + 2 * span, span)
            start = pl.multiple_of(start, LANES)
            at = number * width + q * tall
            w_s[at : at + tall, :] = high_ref[:, pl.ds(start, width)]
            w_s[deep + at : deep + at + tall, :] = low_ref[:, pl.ds(start, width)]
    dot = functools.partial(jnp.dot, preferred_element_type=jnp.float32)
    high = w_s[:deep, :]
    return dot(xh[...], high) + dot(xl[...], high) + dot(xh[...], w_s[deep:, :])


def away_kernel(masks, high_ref, low_ref, own_ref, core_ref, *refs):
    sums = refs[: len(masks)]
    xh, xl, w_s = refs[len(masks) :]
    me = lax.axis_index("gz")
    fill_lines([own_ref, core_ref], [xh, xl])
    for mask, sum_ref in zip(masks, sums):
        total = product(me ^ mask, [me, me ^ 1], high_ref, low_ref, xh, xl, w_s)
        sum_ref[...] = total.reshape(own_ref.shape)


def away_part(band, state, core, masks):
    fields, depth, rows_all, width = state.shape
    line = shape_of(fields * depth * rows_all, 2 * width, dtype=jnp.bfloat16)
    outs = call(
        functools.partial(away_kernel, masks),
        "span_away",
        3.0,
        [PLACE] * 4,
        [PLACE] * (len(masks) + 2),
        [shape_of(*state.shape)] * len(masks) + [line, line],
        [pltpu.VMEM((4 * width, width), jnp.bfloat16)],
    )(*band, state, core)
    return outs[: len(masks)], outs[len(masks) :]


def home_kernel(high_ref, low_ref, xh, xl, first_ref, second_ref, after_ref, out_ref, w_s):
    me = lax.axis_index("gz")
    half = first_ref.shape[1]
    total = product(me, [me, me ^ 1], high_ref, low_ref, xh, xl, w_s).reshape(out_ref.shape)
    out_ref[:, :half] = first_ref[...] - TIME_STEP * total[:, :half]
    out_ref[:, half:] = second_ref[...] - TIME_STEP * total[:, half:]


def home_part(band, lines, first, second, after):
    fields, half, rows_all, width = first.shape
    return call(
        home_kernel,
        "span_home",
        2.0,
        [PLACE] * 6 + [ANYWHERE],
        PLACE,
        shape_of(fields, half + second.shape[1], rows_all, width),
        [pltpu.VMEM((4 * width, width), jnp.bfloat16)],
    )(*band, *lines, first, second, after)


def per_device(state, mask_x, mask_y, span_filter):
    fields, depth, rows_all, width = state.shape
    groups = lax.axis_size("gz")
    slabs = lax.axis_size("gx")
    span = width * groups

    def flip(array, bit):
        return lax.ppermute(array, "gz", [(g, g ^ bit) for g in range(groups)])

    swap = [(i, i ^ 1) for i in range(slabs)]
    carry = [(i, i + 2) for i in range(0, slabs - 2, 2)] + [
        (i, i - 2) for i in range(3, slabs, 2)
    ]
    core = flip(state, 1)
    low = rows_all // 2
    if width % (4 * LANES) == 0:
        lane = width // 4
        parts = [
            (0, low, 0, 3 * lane),
            (low, low, 0, 2 * lane),
            (0, rows_all, 3 * lane, lane),
            (low, low, 2 * lane, lane),
        ]
    else:
        parts = [(row, rows_all // 4, 0, width) for row in range(0, rows_all, rows_all // 4)]
    row, rows, lane, count = parts[0]
    cells = state[:, :, row : row + rows, lane : lane + count]
    switches = mask_x[:1, row : row + rows, lane : lane + count]
    brick = bring_part(cells, switches, (0, rows, 0, count), switches)
    pairs = [lax.ppermute(brick, "gx", swap)]
    band = circulant(span_filter, span, width, core)

    masks = list(range(2, groups, 2))
    sums, lines = away_part(band, state, core, masks)
    arrived = sum(flip(part_sum, mask) for part_sum, mask in zip(sums, masks))
    half = depth // 2
    fars, others = [], []

    def exchange(c, after):
        brick = bring_part(state, mask_x, parts[c], after)
        pairs.append(lax.ppermute(brick, "gx", swap))
        return brick

    def hand_on(c, after):
        planes = pass_part(pairs[c], depth, after)
        fars.append(lax.ppermute(planes, "gx", carry))
        return planes

    def stream(c, after):
        done = stream_part(state, pairs[c], fars[c], mask_x, parts[c], base, after)
        others.append((parts[c], done))
        return done

    acc_low = wall_part(state, mask_y, 0, half, lines[0])
    after = exchange(1, acc_low)
    acc_high = wall_part(state, mask_y, half, depth - half, after)
    after = exchange(2, hand_on(0, acc_high))
    base = home_part(band, lines, acc_low, acc_high, after)
    after = exchange(3, hand_on(1, base))
    after = hand_on(2, stream(0, after))
    after = hand_on(3, after)
    stream(2, stream(1, after))
    return stream_part(
        state, pairs[3], fars[3], mask_x, parts[3], base, arrived=arrived, others=others
    )


def solution(mesh):
    return jax.shard_map(
        per_device,
        mesh=mesh,
        in_specs=(P(None, "gx", None, "gz"), P("gx", None, "gz"), P("gx", None, "gz"), P()),
        out_specs=P(None, "gx", None, "gz"),
        check_vma=False,
    )
```

```python
import functools

import jax
import jax.numpy as jnp
import numpy as np
from jax import lax
from jax.experimental import pallas as pl
from jax.experimental.pallas import tpu as pltpu
from jax.sharding import PartitionSpec as P

GAMMA_GAS = 1.4
SMALL_EPS = 1e-06
TIME_STEP = 0.1
ROWS = 8
LANES = 128
VMEM_BYTES = 24 * 1024 * 1024
PACK_BYTES = 60 * 1024 * 1024
FACE_SCALE = -TIME_STEP / 60.0
PLACE = pl.BlockSpec(memory_space=pltpu.VMEM)
ANYWHERE = pl.BlockSpec(memory_space=pl.ANY)
HBM = pl.BlockSpec(memory_space=pltpu.HBM)


def call(kernel, name, weight, ins, outs, out_shape, scratch=(), aliases=None, vmem=VMEM_BYTES):
    return pl.pallas_call(
        kernel,
        out_shape=out_shape,
        in_specs=ins,
        out_specs=outs,
        scratch_shapes=list(scratch),
        input_output_aliases=aliases or {},
        compiler_params=pltpu.CompilerParams(vmem_limit_bytes=vmem),
        cost_estimate=pl.CostEstimate(
            flops=int(weight * 1e9), bytes_accessed=int(weight * 3e6), transcendentals=0
        ),
        name=name,
    )


def shape_of(*dims, dtype=jnp.float32):
    return jax.ShapeDtypeStruct(dims, dtype)


def flux_of(q, normal):
    thin = pl.reciprocal(q[0], approx=True)
    velocity = [q[1] * thin, q[2] * thin, q[3] * thin]
    pressure = (GAMMA_GAS - 1.0) * (
        q[4] - 0.5 * (q[1] * velocity[0] + q[2] * velocity[1] + q[3] * velocity[2])
    )
    along = velocity[normal]
    flux = [q[normal + 1], q[1] * along, q[2] * along, q[3] * along, (q[4] + pressure) * along]
    flux[normal + 1] = flux[normal + 1] + pressure
    return flux, pressure, thin, along


def speed_of(pressure, thin, along):
    return jnp.abs(along) + jnp.sqrt(GAMMA_GAS * pressure * thin)


def weno_rest(d1, d2, d3, d4):
    low = d2 * d2 * 0.609375 + 3.0 * SMALL_EPS
    high = d3 * d3 * 0.609375 + 3.0 * SMALL_EPS
    x0 = d1 - 1.375 * d2
    x1 = d2 - 0.625 * d3
    x2 = d4 - 1.375 * d3
    t0 = low + x0 * x0
    t1 = high + x1 * x1
    t2 = high + x2 * x2
    w0 = t1 * t2
    w1 = t0 * t2
    w2 = t0 * t1
    w0 = w0 * w0
    w1 = w1 * w1
    w2 = w2 * w2 * 1.5
    top = w0 * (x0 + (d3 - 0.625 * d2)) + w2 * (x1 + x2)
    bottom = 0.5 * w0 + 3.0 * w1 + w2
    return top * pl.reciprocal(bottom, approx=True)


def face_value(dq, df, both, alpha, upwind):
    aq = [alpha * value for value in dq]
    plus = [df[k] + aq[k] for k in range(4)]
    minus = [df[k] - aq[k] for k in range(1, 5)]
    bend = df[1] - df[3]
    central = 7.0 * bend + (df[4] - df[0])
    rest = weno_rest(minus[3], minus[2], minus[1], minus[0]) - weno_rest(*plus)
    biased = 5.0 * (bend + (aq[1] + aq[3]) - (aq[2] + aq[2]) + rest)
    return 30.0 * both + jnp.where(upwind, biased, central)


def lanes(number):
    return pl.ds(pl.multiple_of(number * LANES, LANES), LANES)


def wall_kernel(low, state_ref, mask_ref, out_ref, q_s, f_s, speed_s, dq_s, df_s):
    rows_y = state_ref.shape[2]
    width = state_ref.shape[3]
    tiles = rows_y // ROWS
    end = ROWS + rows_y
    zero = jnp.zeros((5, ROWS, LANES), jnp.float32)
    for side in (dq_s, df_s):
        side[:, 0:ROWS, :] = zero
        side[:, end : end + ROWS, :] = zero
    row = lax.broadcasted_iota(jnp.int32, (ROWS, LANES), 0)

    def column(number, carry):
        plane = number // (width // LANES)
        lane = lanes(number % (width // LANES))
        zero_row = jnp.minimum(number, 0)

        def at(r, shift):
            return pl.ds(zero_row + (r * ROWS + ROWS + shift), ROWS)

        def still(r):
            return slice(r * ROWS + ROWS, r * ROWS + 2 * ROWS)

        qs = []
        for r in range(tiles):
            mine = slice(r * ROWS, r * ROWS + ROWS)
            q = [state_ref[k, low + plane, mine, lane] for k in range(5)]
            flux, pressure, thin, along = flux_of(q, 1)
            speed = speed_of(pressure, thin, along)
            for k in range(5):
                q_s[k, still(r), :] = q[k]
                f_s[k, still(r), :] = flux[k]
            speed_s[still(r), :] = speed
            if r == 0:
                for k in range(5):
                    q_s[k, 0:ROWS, :] = jnp.broadcast_to(q[k][0:1], (ROWS, LANES))
                    f_s[k, 0:ROWS, :] = jnp.broadcast_to(flux[k][0:1], (ROWS, LANES))
                speed_s[0:ROWS, :] = jnp.broadcast_to(speed[0:1], (ROWS, LANES))
            if r == tiles - 1:
                speed_s[end : end + ROWS, :] = jnp.broadcast_to(
                    speed[ROWS - 1 : ROWS], (ROWS, LANES)
                )
        for k in range(5):
            changes = [
                (
                    q_s[k, still(r), :] - q_s[k, at(r, -1), :],
                    f_s[k, still(r), :] - f_s[k, at(r, -1), :],
                )
                for r in range(tiles)
            ]
            for r in range(tiles):
                dq_s[k, still(r), :] = changes[r][0]
                df_s[k, still(r), :] = changes[r][1]
        alphas, switches = [], []
        for r in range(tiles):
            alpha = speed_s[still(r), :]
            for shift in (-3, -2, -1, 1, 2):
                alpha = jnp.maximum(alpha, speed_s[at(r, shift), :])
            alphas.append(alpha)
            switches.append(mask_ref[low + plane, r * ROWS : r * ROWS + ROWS, lane] > 0)
        for k in range(5):
            hats = []
            for r in range(tiles):
                dq = [dq_s[k, at(r, s), :] for s in (-2, -1)]
                df = [df_s[k, at(r, s), :] for s in (-2, -1)]
                dq += [dq_s[k, still(r), :]]
                df += [df_s[k, still(r), :]]
                dq += [dq_s[k, at(r, s), :] for s in (1, 2)]
                df += [df_s[k, at(r, s), :] for s in (1, 2)]
                here = f_s[k, still(r), :]
                both = here + here - df[2]
                hats.append(face_value(dq, df, both, alphas[r], switches[r]))
            top = (
                60.0 * f_s[k, end - 1 : end, :]
                + 7.0 * df_s[k, end - 1 : end, :]
                - df_s[k, end - 2 : end - 1, :]
            )
            turned = [pltpu.roll(hat, ROWS - 1, 0) for hat in hats]
            turned.append(jnp.broadcast_to(top, (ROWS, LANES)))
            for r in range(tiles):
                after = jnp.where(row == ROWS - 1, turned[r + 1], turned[r])
                mine = slice(r * ROWS, r * ROWS + ROWS)
                out_ref[k, plane, mine, lane] = q_s[k, still(r), :] + FACE_SCALE * (after - hats[r])
        return carry

    lax.fori_loop(0, out_ref.shape[1] * (width // LANES), column, 0)


def wall_part(state, mask_y, low, count, after):
    fields, depth, rows_y, width = state.shape
    tall = rows_y + 2 * ROWS
    padded = pltpu.VMEM((fields, tall, LANES), jnp.float32)

    def kernel(state_ref, mask_ref, after_ref, out_ref, *scratch):
        wall_kernel(low, state_ref, mask_ref, out_ref, *scratch)

    return call(
        kernel,
        "wall_faces",
        5.0 * count / depth,
        [PLACE, PLACE, ANYWHERE],
        PLACE,
        shape_of(fields, count, rows_y, width),
        [padded, padded, pltpu.VMEM((tall, LANES), jnp.float32), padded, padded],
    )(state, mask_y, after)


def pack_kernel(parts, state_ref, mask_ref, *refs):
    outs = refs[: len(parts)]
    mask_s, sems = refs[len(parts) :]
    planes = state_ref.shape[0]
    mask_copy = pltpu.make_async_copy(mask_ref.at[0], mask_s, sems.at[len(parts)])
    mask_copy.start()
    copies = [
        pltpu.make_async_copy(
            state_ref.at[:, pl.ds(row, rows), pl.ds(lane, width)],
            out.at[pl.ds(0, planes)],
            sems.at[c],
        )
        for c, ((row, rows, lane, width), out) in enumerate(zip(parts, outs))
    ]
    for copy in copies:
        copy.start()
    mask_copy.wait()
    for (row, rows, lane, width), out in zip(parts, outs):
        out[planes] = mask_s[row : row + rows, lane : lane + width].astype(jnp.float32)
    for copy in copies:
        copy.wait()


def pack_part(state, mask_x, parts):
    fields, depth, rows_all, width = state.shape
    planes = fields * depth
    return call(
        functools.partial(pack_kernel, parts),
        "pack_bricks",
        1.0,
        [HBM, HBM],
        [PLACE] * len(parts),
        [shape_of(planes + 1, rows, lane_count) for _, rows, _, lane_count in parts],
        [
            pltpu.VMEM((rows_all, width), jnp.int32),
            pltpu.SemaphoreType.DMA((len(parts) + 1,)),
        ],
        vmem=PACK_BYTES,
    )(state.reshape(planes, rows_all, width), mask_x)


def bring_kernel(part, state_ref, mask_ref, after_ref, out):
    row, rows, lane, width = part
    fields, depth, _, _ = state_ref.shape
    for k in range(fields):
        for i in range(depth):
            out[depth * k + i] = state_ref[k, i, row : row + rows, lane : lane + width]
    switches = mask_ref[0, row : row + rows, lane : lane + width]
    out[depth * fields] = switches.astype(jnp.float32)


def bring_part(state, mask_x, part, after):
    fields, depth, _, _ = state.shape
    _, rows, _, width = part
    return call(
        functools.partial(bring_kernel, part),
        "bring_planes",
        0.5,
        [PLACE, PLACE, ANYWHERE],
        PLACE,
        shape_of(depth * fields + 1, rows, width),
    )(state, mask_x, after)


def pass_kernel(depth, pair_ref, after_ref, out_ref):
    planes = pair_ref.shape[0] - 1
    skip = 1 - lax.rem(lax.axis_index("gx"), 2)
    for k in range(planes // depth):
        for i in range(3):
            out_ref[3 * k + i] = pair_ref[depth * k + i + skip * (depth - 3)]
    out_ref[3 * (planes // depth)] = pair_ref[planes]


def pass_part(pair, depth, after):
    planes, rows_y, width = pair.shape
    return call(
        functools.partial(pass_kernel, depth),
        "pass_planes",
        0.5,
        [PLACE, ANYWHERE],
        PLACE,
        shape_of(3 * (planes - 1) // depth + 1, rows_y, width),
    )(pair, after)


def stream_kernel(part, others, *refs):
    (state_ref, pair_ref, far_ref, mask_ref, base_ref), refs = refs[:5], refs[5:]
    if others is None:
        _, out_ref, dq_s, df_s, both_s, alpha_s = refs
        result = out_ref
    else:
        sum_ref, other_refs, refs = refs[0], refs[1 : 1 + len(others)], refs[1 + len(others) :]
        _, out_ref, dq_s, df_s, both_s, alpha_s, result, sem, other_sem = refs[:9]
        staged = refs[9:]
    fields, depth, _, _ = state_ref.shape
    start, rows_y, start_lane, width = part
    stride = depth
    rank = lax.axis_index("gx")
    even = lax.rem(rank, 2) == 0
    first = rank == 0
    last = rank == lax.axis_size("gx") - 1
    lane_tiles = width // LANES
    faces = depth + 1
    tiles = (rows_y // ROWS) * lane_tiles

    def rows(row, shift):
        return pl.ds(pl.multiple_of(row + shift, ROWS), ROWS)

    def place(number):
        lane = (number % lane_tiles) * LANES
        return (
            (number // lane_tiles) * ROWS,
            pl.ds(pl.multiple_of(lane, LANES), LANES),
            pl.ds(pl.multiple_of(lane + start_lane, LANES), LANES),
        )

    def point(number, carry):
        at, lane, there = place(number)
        row, mine = rows(at, 0), rows(at, start)
        own = [[state_ref[k, i, mine, there] for k in range(5)] for i in range(depth)]
        cells = []
        for i in range(3):
            cells.append(
                [
                    jnp.where(
                        first,
                        own[0][k],
                        jnp.where(
                            even,
                            far_ref[3 * k + i, row, lane],
                            pair_ref[stride * k + stride - 3 + i, row, lane],
                        ),
                    )
                    for k in range(5)
                ]
            )
        cells += own
        for i in range(3):
            cells.append(
                [
                    jnp.where(
                        last,
                        own[depth - 1][k],
                        jnp.where(
                            even,
                            pair_ref[stride * k + i, row, lane],
                            far_ref[3 * k + i, row, lane],
                        ),
                    )
                    for k in range(5)
                ]
            )
        speeds, before = [], None
        for j, q in enumerate(cells):
            flux, pressure, thin, along = flux_of(q, 0)
            speeds.append(speed_of(pressure, thin, along))
            if j > 0:
                for k in range(5):
                    dq_s[number, k, j - 1] = q[k] - cells[j - 1][k]
                    df_s[number, k, j - 1] = flux[k] - before[k]
                    if 3 <= j < 3 + faces:
                        both_s[number, k, j - 3] = flux[k] + before[k]
            before = flux
        pairs = [jnp.maximum(speeds[i], speeds[i + 1]) for i in range(depth + 5)]
        for f in range(faces):
            alpha_s[number, f] = jnp.maximum(jnp.maximum(pairs[f], pairs[f + 2]), pairs[f + 4])
        return carry

    lax.fori_loop(0, tiles, point, 0)

    def faces_of(number, carry):
        at, lane, there = place(number)
        row, mine = rows(at, 0), rows(at, start)
        border = jnp.where(
            even, pair_ref[stride * fields, row, lane], far_ref[3 * fields, row, lane]
        )
        border = jnp.where(last, 0.0, border)
        switches = [mask_ref[i, mine, there] > 0 for i in range(depth)] + [border > 0.0]
        results = []
        for k in range(5):
            dq = [dq_s[number, k, j] for j in range(depth + 5)]
            df = [df_s[number, k, j] for j in range(depth + 5)]
            hats = [
                face_value(
                    dq[f : f + 5], df[f : f + 5], both_s[number, k, f], alpha_s[number, f], switches[f]
                )
                for f in range(faces)
            ]
            for i in range(depth):
                value = base_ref[k, i, mine, there] + FACE_SCALE * (hats[i + 1] - hats[i])
                if others is not None:
                    value = value - TIME_STEP * sum_ref[k, i, mine, there]
                results.append(value)
        for k in range(5):
            for i in range(depth):
                result[k, i, row, lane] = results[k * depth + i]
        if others is not None:
            hand_out(number).start()
        return carry

    def hand_out(number):
        at, lane, there = place(number)
        return pltpu.make_async_copy(
            result.at[:, :, rows(at, 0), lane],
            out_ref.at[:, :, rows(at, start), there],
            sem.at[number],
        )

    def settle(number, carry):
        hand_out(number).wait()
        return carry

    copies = []
    for number, other in enumerate(others or []):
        top, tall, left, wide = other

        def line(index, carry, number=number, top=top, tall=tall, left=left, wide=wide):
            k, i = index // depth, index % depth
            staged[number][k, i] = other_refs[number][k, i] - TIME_STEP * (
                sum_ref[k, i, top : top + tall, left : left + wide]
            )
            return carry

        lax.fori_loop(0, fields * depth, line, 0)
        copy = pltpu.make_async_copy(
            staged[number],
            out_ref.at[:, :, pl.ds(top, tall), pl.ds(left, wide)],
            other_sem.at[number],
        )
        copy.start()
        copies.append(copy)
    lax.fori_loop(0, tiles, faces_of, 0)
    if others is not None:
        lax.fori_loop(0, tiles, settle, 0)
    for copy in copies:
        copy.wait()


def stream_part(state, pair, far, mask_x, part, base, after, arrived=None, others=None, chained=False):
    fields, depth, _, _ = state.shape
    _, rows_y, _, width = part
    tiles = rows_y * width // (ROWS * LANES)

    def vregs(*dims):
        return pltpu.VMEM(dims + (ROWS, LANES), jnp.float32)

    def cells(part):
        return (fields, depth, part[1], part[3])

    scratch = [
        vregs(tiles, fields, depth + 5),
        vregs(tiles, fields, depth + 5),
        vregs(tiles, fields, depth + 1),
        vregs(tiles, depth + 1),
    ]
    inputs = [state, pair, far, mask_x, base]
    if others is None:
        places = None
        target, target_shape = PLACE, shape_of(*cells(part))
    else:
        places = [place for place, _ in others]
        inputs += [arrived] + [array for _, array in others]
        target, target_shape = HBM, shape_of(*state.shape)
        scratch += [
            pltpu.VMEM(cells(part), jnp.float32),
            pltpu.SemaphoreType.DMA((tiles,)),
            pltpu.SemaphoreType.DMA((max(1, len(others)),)),
        ] + [pltpu.VMEM(cells(place), jnp.float32) for place in places]
    return call(
        functools.partial(stream_kernel, part, places),
        "stream_faces",
        0.3 * tiles,
        [PLACE] * len(inputs) + [HBM if chained else ANYWHERE],
        target,
        target_shape,
        scratch,
        {len(inputs): 0} if chained else None,
    )(*inputs, after)


def circulant_tables(span):
    half = span // 2
    step = 1
    while step * step < half:
        step *= 2
    count = half // step
    places = np.arange(span)
    period = max(2 * count, LANES)
    high = 2.0 * np.pi / span * ((np.arange(count)[:, None] * step * places[None, :period]) % span)
    low = 2.0 * np.pi / span * ((np.arange(step)[:, None] * places[None]) % span)
    tables = [np.concatenate([np.cos(a), np.sin(a)]) for a in (high, low)]
    return step, count, [jnp.asarray(t.astype(np.float32)) for t in tables]


def circulant_kernel(
    count, step, filter_ref, inner_ref, outer_ref, after_ref, high_ref, low_ref, band
):
    period = inner_ref.shape[1]
    span = outer_ref.shape[1]
    tall, wide = high_ref.shape
    order = step * lax.broadcasted_iota(
        jnp.int32, (count, step), 0
    ) + lax.broadcasted_iota(jnp.int32, (count, step), 1)
    scale = 2.0 / span * (2.0 * np.pi / span) * order.astype(jnp.float32) * filter_ref[...]

    def dot(table):
        return lax.dot_general(
            scale,
            table,
            (((0,), (0,)), ((), ())),
            precision=lax.Precision.HIGHEST,
            preferred_element_type=jnp.float32,
        )

    repeat = span // period
    inner_cos = jnp.concatenate([dot(inner_ref[:count])] * repeat, 1)
    inner_sin = jnp.concatenate([dot(inner_ref[count:])] * repeat, 1)
    line = jnp.sum(
        outer_ref[step:] * inner_cos + outer_ref[:step] * inner_sin, axis=0, keepdims=True
    )
    base = jnp.broadcast_to(-line, (ROWS, span))
    place = lax.broadcasted_iota(jnp.int32, (ROWS, span), 0)
    skew = base
    for i in range(1, ROWS):
        skew = jnp.where(place == i, pltpu.roll(base, i, 1), skew)
    for b in range(LANES // ROWS):
        rows = skew if b == 0 else pltpu.roll(skew, b * ROWS, 1)
        for q in range(tall // LANES):
            at = q * LANES + b * ROWS
            first = q * LANES
            if first:
                band[at : at + ROWS, :first] = rows[:, span - first :]
            band[at : at + ROWS, first:span] = rows[:, : span - first]
    full = band[...]
    high = full.astype(jnp.bfloat16)
    low = (full - high.astype(jnp.float32)).astype(jnp.bfloat16)
    high_ref[:, :span] = high
    low_ref[:, :span] = low
    high_ref[:, span:] = high[:, : wide - span]
    low_ref[:, span:] = low[:, : wide - span]


def circulant(span_filter, span, width, after):
    tall = min(256, width)
    step, count, tables = circulant_tables(span)
    band = shape_of(tall, span + width, dtype=jnp.bfloat16)
    return call(
        functools.partial(circulant_kernel, count, step),
        "circulant_band",
        1.0,
        [PLACE, PLACE, PLACE, ANYWHERE],
        [PLACE, PLACE],
        [band, band],
        [pltpu.VMEM((tall, span), jnp.float32)],
    )(span_filter.reshape(count, step), *tables, after)


def fill_lines(shards, x_refs):
    _, depth, rows_y, width = shards[0].shape
    xh, xl = x_refs
    for number, shard in enumerate(shards):

        def plane(index, carry):
            i = index // (width // LANES)
            t = index % (width // LANES)
            flux, _, _, _ = flux_of([shard[k, i, :, lanes(t)] for k in range(5)], 2)
            to = lanes(t + number * (width // LANES))
            for k in range(5):
                high = flux[k].astype(jnp.bfloat16)
                line = pl.ds(pl.multiple_of((k * depth + i) * rows_y, rows_y), rows_y)
                xh[line, to] = high
                xl[line, to] = (flux[k] - high.astype(jnp.float32)).astype(jnp.bfloat16)
            return carry

        lax.fori_loop(0, depth * (width // LANES), plane, 0)


def product(target, sources, high_ref, low_ref, xh, xl, w_s):
    tall, wide = high_ref.shape
    width = xh.shape[1] // len(sources)
    span = wide - width
    deep = xh.shape[1]
    for number, source in enumerate(sources):
        for q in range(width // tall):
            start = lax.rem((target - source) * width - q * tall + 2 * span, span)
            start = pl.multiple_of(start, LANES)
            at = number * width + q * tall
            w_s[at : at + tall, :] = high_ref[:, pl.ds(start, width)]
            w_s[deep + at : deep + at + tall, :] = low_ref[:, pl.ds(start, width)]
    dot = functools.partial(jnp.dot, preferred_element_type=jnp.float32)
    high = w_s[:deep, :]
    return dot(xh[...], high) + dot(xl[...], high) + dot(xh[...], w_s[deep:, :])


def away_kernel(masks, high_ref, low_ref, own_ref, core_ref, *refs):
    sums = refs[: len(masks)]
    xh, xl, w_s = refs[len(masks) :]
    me = lax.axis_index("gz")
    fill_lines([own_ref, core_ref], [xh, xl])
    for mask, sum_ref in zip(masks, sums):
        total = product(me ^ mask, [me, me ^ 1], high_ref, low_ref, xh, xl, w_s)
        sum_ref[...] = total.reshape(own_ref.shape)


def away_part(band, state, core, masks):
    fields, depth, rows_all, width = state.shape
    line = shape_of(fields * depth * rows_all, 2 * width, dtype=jnp.bfloat16)
    outs = call(
        functools.partial(away_kernel, masks),
        "span_away",
        3.0,
        [PLACE] * 4,
        [PLACE] * (len(masks) + 2),
        [shape_of(*state.shape)] * len(masks) + [line, line],
        [pltpu.VMEM((4 * width, width), jnp.bfloat16)],
    )(*band, state, core)
    return outs[: len(masks)], outs[len(masks) :]


def home_kernel(high_ref, low_ref, xh, xl, first_ref, second_ref, after_ref, out_ref, w_s):
    me = lax.axis_index("gz")
    half = first_ref.shape[1]
    total = product(me, [me, me ^ 1], high_ref, low_ref, xh, xl, w_s).reshape(out_ref.shape)
    out_ref[:, :half] = first_ref[...] - TIME_STEP * total[:, :half]
    out_ref[:, half:] = second_ref[...] - TIME_STEP * total[:, half:]


def home_part(band, lines, first, second, after):
    fields, half, rows_all, width = first.shape
    return call(
        home_kernel,
        "span_home",
        2.0,
        [PLACE] * 6 + [ANYWHERE],
        PLACE,
        shape_of(fields, half + second.shape[1], rows_all, width),
        [pltpu.VMEM((4 * width, width), jnp.bfloat16)],
    )(*band, *lines, first, second, after)


def per_device(state, mask_x, mask_y, span_filter):
    fields, depth, rows_all, width = state.shape
    groups = lax.axis_size("gz")
    slabs = lax.axis_size("gx")
    span = width * groups

    def flip(array, bit):
        return lax.ppermute(array, "gz", [(g, g ^ bit) for g in range(groups)])

    swap = [(i, i ^ 1) for i in range(slabs)]
    carry = [(i, i + 2) for i in range(0, slabs - 2, 2)] + [
        (i, i - 2) for i in range(3, slabs, 2)
    ]
    core = flip(state, 1)
    low = rows_all // 2
    if width % (4 * LANES) == 0:
        lane = width // 4
        parts = [
            (0, low, 0, 3 * lane),
            (low, low, 0, 2 * lane),
            (0, rows_all, 3 * lane, lane),
            (low, low, 2 * lane, lane),
        ]
    else:
        parts = [(row, rows_all // 4, 0, width) for row in range(0, rows_all, rows_all // 4)]
    (brick,) = pack_part(state, mask_x, parts[:1])
    pairs = [lax.ppermute(brick, "gx", swap)]
    band = circulant(span_filter, span, width, core)

    masks = list(range(2, groups, 2))
    sums, lines = away_part(band, state, core, masks)
    arrived = sum(flip(part_sum, mask) for part_sum, mask in zip(sums, masks))
    half = depth // 2
    fars = []

    def exchange(c, after):
        brick = bring_part(state, mask_x, parts[c], after)
        pairs.append(lax.ppermute(brick, "gx", swap))
        return brick

    def hand_on(c, after):
        planes = pass_part(pairs[c], depth, after)
        fars.append(lax.ppermute(planes, "gx", carry))
        return planes

    def stream(c, after, *rest):
        return stream_part(state, pairs[c], fars[c], mask_x, parts[c], base, after, *rest)

    acc_low = wall_part(state, mask_y, 0, half, lines[0])
    after = exchange(1, acc_low)
    acc_high = wall_part(state, mask_y, half, depth - half, after)
    after = exchange(2, hand_on(0, acc_high))
    base = home_part(band, lines, acc_low, acc_high, after)
    after = exchange(3, hand_on(1, base))
    early = stream(0, after)
    after = hand_on(3, hand_on(2, early))
    out = stream(1, after, arrived, [])
    out = stream(2, out, arrived, [], True)
    return stream(3, out, arrived, [(parts[0], early)], True)


def solution(mesh):
    return jax.shard_map(
        per_device,
        mesh=mesh,
        in_specs=(P(None, "gx", None, "gz"), P("gx", None, "gz"), P("gx", None, "gz"), P()),
        out_specs=P(None, "gx", None, "gz"),
        check_vma=False,
    )
```

```python
import functools

import jax
import jax.numpy as jnp
import numpy as np
from jax import lax
from jax.experimental import pallas as pl
from jax.experimental.pallas import tpu as pltpu
from jax.sharding import PartitionSpec as P

GAMMA_GAS = 1.4
SMALL_EPS = 1e-06
TIME_STEP = 0.1
ROWS = 8
LANES = 128
VMEM_BYTES = 24 * 1024 * 1024
PACK_BYTES = 60 * 1024 * 1024
FACE_SCALE = -TIME_STEP / 60.0
PLACE = pl.BlockSpec(memory_space=pltpu.VMEM)
ANYWHERE = pl.BlockSpec(memory_space=pl.ANY)
HBM = pl.BlockSpec(memory_space=pltpu.HBM)


def call(kernel, name, weight, ins, outs, out_shape, scratch=(), aliases=None, vmem=VMEM_BYTES):
    return pl.pallas_call(
        kernel,
        out_shape=out_shape,
        in_specs=ins,
        out_specs=outs,
        scratch_shapes=list(scratch),
        input_output_aliases=aliases or {},
        compiler_params=pltpu.CompilerParams(vmem_limit_bytes=vmem),
        cost_estimate=pl.CostEstimate(
            flops=int(weight * 1e9), bytes_accessed=int(weight * 3e6), transcendentals=0
        ),
        name=name,
    )


def shape_of(*dims, dtype=jnp.float32):
    return jax.ShapeDtypeStruct(dims, dtype)


def flux_of(q, normal):
    thin = pl.reciprocal(q[0], approx=True)
    velocity = [q[1] * thin, q[2] * thin, q[3] * thin]
    pressure = (GAMMA_GAS - 1.0) * (
        q[4] - 0.5 * (q[1] * velocity[0] + q[2] * velocity[1] + q[3] * velocity[2])
    )
    along = velocity[normal]
    flux = [q[normal + 1], q[1] * along, q[2] * along, q[3] * along, (q[4] + pressure) * along]
    flux[normal + 1] = flux[normal + 1] + pressure
    return flux, pressure, thin, along


def speed_of(pressure, thin, along):
    return jnp.abs(along) + jnp.sqrt(GAMMA_GAS * pressure * thin)


def weno_rest(d1, d2, d3, d4):
    low = d2 * d2 * 0.609375 + 3.0 * SMALL_EPS
    high = d3 * d3 * 0.609375 + 3.0 * SMALL_EPS
    x0 = d1 - 1.375 * d2
    x1 = d2 - 0.625 * d3
    x2 = d4 - 1.375 * d3
    t0 = low + x0 * x0
    t1 = high + x1 * x1
    t2 = high + x2 * x2
    w0 = t1 * t2
    w1 = t0 * t2
    w2 = t0 * t1
    w0 = w0 * w0
    w1 = w1 * w1
    w2 = w2 * w2 * 1.5
    top = w0 * (x0 + (d3 - 0.625 * d2)) + w2 * (x1 + x2)
    bottom = 0.5 * w0 + 3.0 * w1 + w2
    return top * pl.reciprocal(bottom, approx=True)


def face_value(dq, df, both, alpha, upwind):
    aq = [alpha * value for value in dq]
    plus = [df[k] + aq[k] for k in range(4)]
    minus = [df[k] - aq[k] for k in range(1, 5)]
    bend = df[1] - df[3]
    central = 7.0 * bend + (df[4] - df[0])
    rest = weno_rest(minus[3], minus[2], minus[1], minus[0]) - weno_rest(*plus)
    biased = 5.0 * (bend + (aq[1] + aq[3]) - (aq[2] + aq[2]) + rest)
    return 30.0 * both + jnp.where(upwind, biased, central)


def lanes(number):
    return pl.ds(pl.multiple_of(number * LANES, LANES), LANES)


def wall_kernel(low, state_ref, mask_ref, out_ref, q_s, f_s, speed_s, dq_s, df_s):
    rows_y = state_ref.shape[2]
    width = state_ref.shape[3]
    tiles = rows_y // ROWS
    end = ROWS + rows_y
    zero = jnp.zeros((5, ROWS, LANES), jnp.float32)
    for side in (dq_s, df_s):
        side[:, 0:ROWS, :] = zero
        side[:, end : end + ROWS, :] = zero
    row = lax.broadcasted_iota(jnp.int32, (ROWS, LANES), 0)

    def column(number, carry):
        plane = number // (width // LANES)
        lane = lanes(number % (width // LANES))
        zero_row = jnp.minimum(number, 0)

        def at(r, shift):
            return pl.ds(zero_row + (r * ROWS + ROWS + shift), ROWS)

        def still(r):
            return slice(r * ROWS + ROWS, r * ROWS + 2 * ROWS)

        qs = []
        for r in range(tiles):
            mine = slice(r * ROWS, r * ROWS + ROWS)
            q = [state_ref[k, low + plane, mine, lane] for k in range(5)]
            flux, pressure, thin, along = flux_of(q, 1)
            speed = speed_of(pressure, thin, along)
            for k in range(5):
                q_s[k, still(r), :] = q[k]
                f_s[k, still(r), :] = flux[k]
            speed_s[still(r), :] = speed
            if r == 0:
                for k in range(5):
                    q_s[k, 0:ROWS, :] = jnp.broadcast_to(q[k][0:1], (ROWS, LANES))
                    f_s[k, 0:ROWS, :] = jnp.broadcast_to(flux[k][0:1], (ROWS, LANES))
                speed_s[0:ROWS, :] = jnp.broadcast_to(speed[0:1], (ROWS, LANES))
            if r == tiles - 1:
                speed_s[end : end + ROWS, :] = jnp.broadcast_to(
                    speed[ROWS - 1 : ROWS], (ROWS, LANES)
                )
        for k in range(5):
            changes = [
                (
                    q_s[k, still(r), :] - q_s[k, at(r, -1), :],
                    f_s[k, still(r), :] - f_s[k, at(r, -1), :],
                )
                for r in range(tiles)
            ]
            for r in range(tiles):
                dq_s[k, still(r), :] = changes[r][0]
                df_s[k, still(r), :] = changes[r][1]
        alphas, switches = [], []
        for r in range(tiles):
            alpha = speed_s[still(r), :]
            for shift in (-3, -2, -1, 1, 2):
                alpha = jnp.maximum(alpha, speed_s[at(r, shift), :])
            alphas.append(alpha)
            switches.append(mask_ref[low + plane, r * ROWS : r * ROWS + ROWS, lane] > 0)
        for k in range(5):
            hats = []
            for r in range(tiles):
                dq = [dq_s[k, at(r, s), :] for s in (-2, -1)]
                df = [df_s[k, at(r, s), :] for s in (-2, -1)]
                dq += [dq_s[k, still(r), :]]
                df += [df_s[k, still(r), :]]
                dq += [dq_s[k, at(r, s), :] for s in (1, 2)]
                df += [df_s[k, at(r, s), :] for s in (1, 2)]
                here = f_s[k, still(r), :]
                both = here + here - df[2]
                hats.append(face_value(dq, df, both, alphas[r], switches[r]))
            top = (
                60.0 * f_s[k, end - 1 : end, :]
                + 7.0 * df_s[k, end - 1 : end, :]
                - df_s[k, end - 2 : end - 1, :]
            )
            turned = [pltpu.roll(hat, ROWS - 1, 0) for hat in hats]
            turned.append(jnp.broadcast_to(top, (ROWS, LANES)))
            for r in range(tiles):
                after = jnp.where(row == ROWS - 1, turned[r + 1], turned[r])
                mine = slice(r * ROWS, r * ROWS + ROWS)
                out_ref[k, plane, mine, lane] = q_s[k, still(r), :] + FACE_SCALE * (after - hats[r])
        return carry

    lax.fori_loop(0, out_ref.shape[1] * (width // LANES), column, 0)


def wall_part(state, mask_y, low, count, after):
    fields, depth, rows_y, width = state.shape
    tall = rows_y + 2 * ROWS
    padded = pltpu.VMEM((fields, tall, LANES), jnp.float32)

    def kernel(state_ref, mask_ref, after_ref, out_ref, *scratch):
        wall_kernel(low, state_ref, mask_ref, out_ref, *scratch)

    return call(
        kernel,
        "wall_faces",
        5.0 * count / depth,
        [PLACE, PLACE, ANYWHERE],
        PLACE,
        shape_of(fields, count, rows_y, width),
        [padded, padded, pltpu.VMEM((tall, LANES), jnp.float32), padded, padded],
    )(state, mask_y, after)


def pack_kernel(parts, state_ref, mask_ref, *refs):
    outs = refs[: len(parts)]
    mask_s, sems = refs[len(parts) :]
    planes = state_ref.shape[0]
    mask_copy = pltpu.make_async_copy(mask_ref.at[0], mask_s, sems.at[len(parts)])
    mask_copy.start()
    copies = [
        pltpu.make_async_copy(
            state_ref.at[:, pl.ds(row, rows), pl.ds(lane, width)],
            out.at[pl.ds(0, planes)],
            sems.at[c],
        )
        for c, ((row, rows, lane, width), out) in enumerate(zip(parts, outs))
    ]
    for copy in copies:
        copy.start()
    mask_copy.wait()
    for (row, rows, lane, width), out in zip(parts, outs):
        out[planes] = mask_s[row : row + rows, lane : lane + width].astype(jnp.float32)
    for copy in copies:
        copy.wait()


def pack_part(state, mask_x, parts):
    fields, depth, rows_all, width = state.shape
    planes = fields * depth
    return call(
        functools.partial(pack_kernel, parts),
        "pack_bricks",
        1.0,
        [HBM, HBM],
        [PLACE] * len(parts),
        [shape_of(planes + 1, rows, lane_count) for _, rows, _, lane_count in parts],
        [
            pltpu.VMEM((rows_all, width), jnp.int32),
            pltpu.SemaphoreType.DMA((len(parts) + 1,)),
        ],
        vmem=PACK_BYTES,
    )(state.reshape(planes, rows_all, width), mask_x)


def bring_kernel(part, state_ref, mask_ref, after_ref, out):
    row, rows, lane, width = part
    fields, depth, _, _ = state_ref.shape
    for k in range(fields):
        for i in range(depth):
            out[depth * k + i] = state_ref[k, i, row : row + rows, lane : lane + width]
    switches = mask_ref[0, row : row + rows, lane : lane + width]
    out[depth * fields] = switches.astype(jnp.float32)


def bring_part(state, mask_x, part, after):
    fields, depth, _, _ = state.shape
    _, rows, _, width = part
    return call(
        functools.partial(bring_kernel, part),
        "bring_planes",
        0.5,
        [PLACE, PLACE, ANYWHERE],
        PLACE,
        shape_of(depth * fields + 1, rows, width),
    )(state, mask_x, after)


def pass_kernel(depth, pair_ref, after_ref, out_ref):
    planes = pair_ref.shape[0] - 1
    skip = 1 - lax.rem(lax.axis_index("gx"), 2)
    for k in range(planes // depth):
        for i in range(3):
            out_ref[3 * k + i] = pair_ref[depth * k + i + skip * (depth - 3)]
    out_ref[3 * (planes // depth)] = pair_ref[planes]


def pass_part(pair, depth, after):
    planes, rows_y, width = pair.shape
    return call(
        functools.partial(pass_kernel, depth),
        "pass_planes",
        0.5,
        [PLACE, ANYWHERE],
        PLACE,
        shape_of(3 * (planes - 1) // depth + 1, rows_y, width),
    )(pair, after)


def stream_kernel(part, others, *refs):
    (state_ref, pair_ref, far_ref, mask_ref, base_ref), refs = refs[:5], refs[5:]
    if others is None:
        _, out_ref, dq_s, df_s, both_s, alpha_s = refs
        result = out_ref
    else:
        sum_ref, other_refs, refs = refs[0], refs[1 : 1 + len(others)], refs[1 + len(others) :]
        out_ref, dq_s, df_s, both_s, alpha_s, result, sem, other_sem = refs[:8]
        staged = refs[8:]
    fields, depth, _, _ = state_ref.shape
    start, rows_y, start_lane, width = part
    stride = depth
    rank = lax.axis_index("gx")
    even = lax.rem(rank, 2) == 0
    first = rank == 0
    last = rank == lax.axis_size("gx") - 1
    lane_tiles = width // LANES
    faces = depth + 1
    tiles = (rows_y // ROWS) * lane_tiles

    def rows(row, shift):
        return pl.ds(pl.multiple_of(row + shift, ROWS), ROWS)

    def place(number):
        lane = (number % lane_tiles) * LANES
        return (
            (number // lane_tiles) * ROWS,
            pl.ds(pl.multiple_of(lane, LANES), LANES),
            pl.ds(pl.multiple_of(lane + start_lane, LANES), LANES),
        )

    def point(number, carry):
        at, lane, there = place(number)
        row, mine = rows(at, 0), rows(at, start)
        own = [[state_ref[k, i, mine, there] for k in range(5)] for i in range(depth)]
        cells = []
        for i in range(3):
            cells.append(
                [
                    jnp.where(
                        first,
                        own[0][k],
                        jnp.where(
                            even,
                            far_ref[3 * k + i, row, lane],
                            pair_ref[stride * k + stride - 3 + i, row, lane],
                        ),
                    )
                    for k in range(5)
                ]
            )
        cells += own
        for i in range(3):
            cells.append(
                [
                    jnp.where(
                        last,
                        own[depth - 1][k],
                        jnp.where(
                            even,
                            pair_ref[stride * k + i, row, lane],
                            far_ref[3 * k + i, row, lane],
                        ),
                    )
                    for k in range(5)
                ]
            )
        speeds, before = [], None
        for j, q in enumerate(cells):
            flux, pressure, thin, along = flux_of(q, 0)
            speeds.append(speed_of(pressure, thin, along))
            if j > 0:
                for k in range(5):
                    dq_s[number, k, j - 1] = q[k] - cells[j - 1][k]
                    df_s[number, k, j - 1] = flux[k] - before[k]
                    if 3 <= j < 3 + faces:
                        both_s[number, k, j - 3] = flux[k] + before[k]
            before = flux
        pairs = [jnp.maximum(speeds[i], speeds[i + 1]) for i in range(depth + 5)]
        for f in range(faces):
            alpha_s[number, f] = jnp.maximum(jnp.maximum(pairs[f], pairs[f + 2]), pairs[f + 4])
        return carry

    lax.fori_loop(0, tiles, point, 0)

    def faces_of(number, carry):
        at, lane, there = place(number)
        row, mine = rows(at, 0), rows(at, start)
        border = jnp.where(
            even, pair_ref[stride * fields, row, lane], far_ref[3 * fields, row, lane]
        )
        border = jnp.where(last, 0.0, border)
        switches = [mask_ref[i, mine, there] > 0 for i in range(depth)] + [border > 0.0]
        results = []
        for k in range(5):
            dq = [dq_s[number, k, j] for j in range(depth + 5)]
            df = [df_s[number, k, j] for j in range(depth + 5)]
            hats = [
                face_value(
                    dq[f : f + 5], df[f : f + 5], both_s[number, k, f], alpha_s[number, f], switches[f]
                )
                for f in range(faces)
            ]
            for i in range(depth):
                value = base_ref[k, i, mine, there] + FACE_SCALE * (hats[i + 1] - hats[i])
                if others is not None:
                    value = value - TIME_STEP * sum_ref[k, i, mine, there]
                results.append(value)
        for k in range(5):
            for i in range(depth):
                result[k, i, row, lane] = results[k * depth + i]
        if others is not None:
            hand_out(number).start()
        return carry

    def hand_out(number):
        at, lane, there = place(number)
        return pltpu.make_async_copy(
            result.at[:, :, rows(at, 0), lane],
            out_ref.at[:, :, rows(at, start), there],
            sem.at[number],
        )

    def settle(number, carry):
        hand_out(number).wait()
        return carry

    copies = []
    for number, other in enumerate(others or []):
        top, tall, left, wide = other

        def line(index, carry, number=number, top=top, tall=tall, left=left, wide=wide):
            k, i = index // depth, index % depth
            staged[number][k, i] = other_refs[number][k, i] - TIME_STEP * (
                sum_ref[k, i, top : top + tall, left : left + wide]
            )
            return carry

        lax.fori_loop(0, fields * depth, line, 0)
        copy = pltpu.make_async_copy(
            staged[number],
            out_ref.at[:, :, pl.ds(top, tall), pl.ds(left, wide)],
            other_sem.at[number],
        )
        copy.start()
        copies.append(copy)
    lax.fori_loop(0, tiles, faces_of, 0)
    if others is not None:
        lax.fori_loop(0, tiles, settle, 0)
    for copy in copies:
        copy.wait()


def stream_part(state, pair, far, mask_x, part, base, after=None, arrived=None, others=None):
    fields, depth, _, _ = state.shape
    _, rows_y, _, width = part
    tiles = rows_y * width // (ROWS * LANES)

    def vregs(*dims):
        return pltpu.VMEM(dims + (ROWS, LANES), jnp.float32)

    def cells(part):
        return (fields, depth, part[1], part[3])

    scratch = [
        vregs(tiles, fields, depth + 5),
        vregs(tiles, fields, depth + 5),
        vregs(tiles, fields, depth + 1),
        vregs(tiles, depth + 1),
    ]
    inputs = [state, pair, far, mask_x, base]
    places_in = [PLACE] * len(inputs)
    if others is None:
        inputs.append(after)
        places_in.append(ANYWHERE)
        places = None
        target, target_shape = PLACE, shape_of(*cells(part))
    else:
        places = [place for place, _ in others]
        inputs += [arrived] + [array for _, array in others]
        places_in = [PLACE] * len(inputs)
        target, target_shape = HBM, shape_of(*state.shape)
        scratch += [
            pltpu.VMEM(cells(part), jnp.float32),
            pltpu.SemaphoreType.DMA((tiles,)),
            pltpu.SemaphoreType.DMA((len(others),)),
        ] + [pltpu.VMEM(cells(place), jnp.float32) for place in places]
    return call(
        functools.partial(stream_kernel, part, places),
        "stream_faces",
        0.3 * tiles,
        places_in,
        target,
        target_shape,
        scratch,
    )(*inputs)


def circulant_tables(span):
    half = span // 2
    step = 1
    while step * step < half:
        step *= 2
    count = half // step
    places = np.arange(span)
    period = max(2 * count, LANES)
    high = 2.0 * np.pi / span * ((np.arange(count)[:, None] * step * places[None, :period]) % span)
    low = 2.0 * np.pi / span * ((np.arange(step)[:, None] * places[None]) % span)
    tables = [np.concatenate([np.cos(a), np.sin(a)]) for a in (high, low)]
    return step, count, [jnp.asarray(t.astype(np.float32)) for t in tables]


def circulant_kernel(
    count, step, filter_ref, inner_ref, outer_ref, after_ref, high_ref, low_ref, band
):
    period = inner_ref.shape[1]
    span = outer_ref.shape[1]
    tall, wide = high_ref.shape
    order = step * lax.broadcasted_iota(
        jnp.int32, (count, step), 0
    ) + lax.broadcasted_iota(jnp.int32, (count, step), 1)
    scale = 2.0 / span * (2.0 * np.pi / span) * order.astype(jnp.float32) * filter_ref[...]

    def dot(table):
        return lax.dot_general(
            scale,
            table,
            (((0,), (0,)), ((), ())),
            precision=lax.Precision.HIGHEST,
            preferred_element_type=jnp.float32,
        )

    repeat = span // period
    inner_cos = jnp.concatenate([dot(inner_ref[:count])] * repeat, 1)
    inner_sin = jnp.concatenate([dot(inner_ref[count:])] * repeat, 1)
    line = jnp.sum(
        outer_ref[step:] * inner_cos + outer_ref[:step] * inner_sin, axis=0, keepdims=True
    )
    base = jnp.broadcast_to(-line, (ROWS, span))
    place = lax.broadcasted_iota(jnp.int32, (ROWS, span), 0)
    skew = base
    for i in range(1, ROWS):
        skew = jnp.where(place == i, pltpu.roll(base, i, 1), skew)
    for b in range(LANES // ROWS):
        rows = skew if b == 0 else pltpu.roll(skew, b * ROWS, 1)
        for q in range(tall // LANES):
            at = q * LANES + b * ROWS
            first = q * LANES
            if first:
                band[at : at + ROWS, :first] = rows[:, span - first :]
            band[at : at + ROWS, first:span] = rows[:, : span - first]
    full = band[...]
    high = full.astype(jnp.bfloat16)
    low = (full - high.astype(jnp.float32)).astype(jnp.bfloat16)
    high_ref[:, :span] = high
    low_ref[:, :span] = low
    high_ref[:, span:] = high[:, : wide - span]
    low_ref[:, span:] = low[:, : wide - span]


def circulant(span_filter, span, width, after):
    tall = min(256, width)
    step, count, tables = circulant_tables(span)
    band = shape_of(tall, span + width, dtype=jnp.bfloat16)
    return call(
        functools.partial(circulant_kernel, count, step),
        "circulant_band",
        1.0,
        [PLACE, PLACE, PLACE, ANYWHERE],
        [PLACE, PLACE],
        [band, band],
        [pltpu.VMEM((tall, span), jnp.float32)],
    )(span_filter.reshape(count, step), *tables, after)


def fill_lines(shards, x_refs):
    _, depth, rows_y, width = shards[0].shape
    xh, xl = x_refs
    for number, shard in enumerate(shards):

        def plane(index, carry):
            i = index // (width // LANES)
            t = index % (width // LANES)
            flux, _, _, _ = flux_of([shard[k, i, :, lanes(t)] for k in range(5)], 2)
            to = lanes(t + number * (width // LANES))
            for k in range(5):
                high = flux[k].astype(jnp.bfloat16)
                line = pl.ds(pl.multiple_of((k * depth + i) * rows_y, rows_y), rows_y)
                xh[line, to] = high
                xl[line, to] = (flux[k] - high.astype(jnp.float32)).astype(jnp.bfloat16)
            return carry

        lax.fori_loop(0, depth * (width // LANES), plane, 0)


def product(target, sources, high_ref, low_ref, xh, xl, w_s):
    tall, wide = high_ref.shape
    width = xh.shape[1] // len(sources)
    span = wide - width
    deep = xh.shape[1]
    for number, source in enumerate(sources):
        for q in range(width // tall):
            start = lax.rem((target - source) * width - q * tall + 2 * span, span)
            start = pl.multiple_of(start, LANES)
            at = number * width + q * tall
            w_s[at : at + tall, :] = high_ref[:, pl.ds(start, width)]
            w_s[deep + at : deep + at + tall, :] = low_ref[:, pl.ds(start, width)]
    dot = functools.partial(jnp.dot, preferred_element_type=jnp.float32)
    high = w_s[:deep, :]
    return dot(xh[...], high) + dot(xl[...], high) + dot(xh[...], w_s[deep:, :])


def away_kernel(masks, high_ref, low_ref, own_ref, core_ref, *refs):
    sums = refs[: len(masks)]
    xh, xl, w_s = refs[len(masks) :]
    me = lax.axis_index("gz")
    fill_lines([own_ref, core_ref], [xh, xl])
    for mask, sum_ref in zip(masks, sums):
        total = product(me ^ mask, [me, me ^ 1], high_ref, low_ref, xh, xl, w_s)
        sum_ref[...] = total.reshape(own_ref.shape)


def away_part(band, state, core, masks):
    fields, depth, rows_all, width = state.shape
    line = shape_of(fields * depth * rows_all, 2 * width, dtype=jnp.bfloat16)
    outs = call(
        functools.partial(away_kernel, masks),
        "span_away",
        3.0,
        [PLACE] * 4,
        [PLACE] * (len(masks) + 2),
        [shape_of(*state.shape)] * len(masks) + [line, line],
        [pltpu.VMEM((4 * width, width), jnp.bfloat16)],
    )(*band, state, core)
    return outs[: len(masks)], outs[len(masks) :]


def home_kernel(high_ref, low_ref, xh, xl, first_ref, second_ref, after_ref, out_ref, w_s):
    me = lax.axis_index("gz")
    half = first_ref.shape[1]
    total = product(me, [me, me ^ 1], high_ref, low_ref, xh, xl, w_s).reshape(out_ref.shape)
    out_ref[:, :half] = first_ref[...] - TIME_STEP * total[:, :half]
    out_ref[:, half:] = second_ref[...] - TIME_STEP * total[:, half:]


def home_part(band, lines, first, second, after):
    fields, half, rows_all, width = first.shape
    return call(
        home_kernel,
        "span_home",
        2.0,
        [PLACE] * 6 + [ANYWHERE],
        PLACE,
        shape_of(fields, half + second.shape[1], rows_all, width),
        [pltpu.VMEM((4 * width, width), jnp.bfloat16)],
    )(*band, *lines, first, second, after)


def per_device(state, mask_x, mask_y, span_filter):
    fields, depth, rows_all, width = state.shape
    groups = lax.axis_size("gz")
    slabs = lax.axis_size("gx")
    span = width * groups

    def flip(array, bit):
        return lax.ppermute(array, "gz", [(g, g ^ bit) for g in range(groups)])

    swap = [(i, i ^ 1) for i in range(slabs)]
    carry = [(i, i + 2) for i in range(0, slabs - 2, 2)] + [
        (i, i - 2) for i in range(3, slabs, 2)
    ]
    core = flip(state, 1)
    low = rows_all // 2
    if width % (4 * LANES) == 0:
        lane = width // 4
        parts = [
            (0, rows_all, 3 * lane, lane),
            (0, low, 0, 3 * lane),
            (low, low, 0, 2 * lane),
            (low, low, 2 * lane, lane),
        ]
    else:
        parts = [(row, rows_all // 4, 0, width) for row in range(0, rows_all, rows_all // 4)]
    (brick,) = pack_part(state, mask_x, parts[:1])
    pairs = [lax.ppermute(brick, "gx", swap)]
    band = circulant(span_filter, span, width, core)

    masks = list(range(2, groups, 2))
    sums, lines = away_part(band, state, core, masks)
    arrived = sum(flip(part_sum, mask) for part_sum, mask in zip(sums, masks))
    half = depth // 2
    fars, others = [], []

    def exchange(c, after):
        brick = bring_part(state, mask_x, parts[c], after)
        pairs.append(lax.ppermute(brick, "gx", swap))
        return brick

    def hand_on(c, after):
        planes = pass_part(pairs[c], depth, after)
        fars.append(lax.ppermute(planes, "gx", carry))
        return planes

    def stream(c, after):
        done = stream_part(state, pairs[c], fars[c], mask_x, parts[c], base, after)
        others.append((parts[c], done))
        return done

    acc_low = wall_part(state, mask_y, 0, half, lines[0])
    after = exchange(1, acc_low)
    acc_high = wall_part(state, mask_y, half, depth - half, after)
    after = exchange(2, hand_on(0, acc_high))
    base = home_part(band, lines, acc_low, acc_high, after)
    after = exchange(3, hand_on(1, base))
    after = hand_on(2, stream(0, after))
    after = hand_on(3, after)
    stream(2, stream(1, after))
    return stream_part(
        state, pairs[3], fars[3], mask_x, parts[3], base, arrived=arrived, others=others
    )


def solution(mesh):
    return jax.shard_map(
        per_device,
        mesh=mesh,
        in_specs=(P(None, "gx", None, "gz"), P("gx", None, "gz"), P("gx", None, "gz"), P()),
        out_specs=P(None, "gx", None, "gz"),
        check_vma=False,
    )
```
